32 devices in a mesh: row: 8 (over y, x, core), col: 4 (over z).
Axes of the slice: x: 2, y: 2, z: 4, core: 2. Of those that a mesh axis runs over, the one named last changes fastest.
Arguments:
- phi: bfloat16 [80, 80, 80, 256], P('col', 'row'), may hold values from -1 to 1
- psi: bfloat16 [80, 80, 80, 256], P('col', 'row'), may hold values from -1 to 1
- points: int32 [16384], P(('row', 'col')), may hold values from 0 to 511999, as said below
Outputs:
- schur: float32 [16384, 16384], P('row', 'col')
- panel: float32 [16384, 256], P('row')
- potential: float32 [80, 80, 80, 256], P('col', 'row')
The draws below stay inside these ranges and needn't reach their ends.
Inputs may be any that keep to these rules, and one draw needn't show every extreme that they name: `points`: block k of 512 consecutive entries holds distinct indices (x 80 + y) * 80 + z of cells with x // 20 = k mod (4) and y // 10 = k div (4).
All inputs are finite; a program needn't handle non-finite values.
Results may differ from the reference program's by a relative error of at most 0.0003.
Values may be sent and summed in bfloat16 or wider, within the bound.
No kernel may reach another device: no remote copies, remote signals or barrier semaphores. Data moves between devices by JAX's collectives and lax.ppermute only.
A program may use at most 256 MiB of HBM per device.

```python
import math
import jax
import jax.numpy as jnp
from jax import lax

NORB = 256
NMU = 16384
PB = 256
GX = 80
GY = 80
GZ = 80
CX = 20
CY = 10
MU_DEV = 512
N_ROW = 8


def draw_points(key, part):
    cells = CX * CY * GZ
    col_blocks = GX // CX

    def one_block(block_id):
        order = jax.random.permutation(jax.random.fold_in(key, block_id), cells)[:MU_DEV]
        row_blk = block_id // col_blocks
        col_blk = block_id % col_blocks
        local_x = order // (CY * GZ)
        local_y = order // GZ % CY
        local_z = order % GZ
        return ((col_blk * CX + local_x) * GY + row_blk * CY + local_y) * GZ + local_z
    blocks = jax.vmap(one_block)(jnp.arange(NMU // MU_DEV, dtype=jnp.int32))
    return blocks.reshape(NMU).astype(jnp.int32)


def wave_basis(length, weights):
    phases = jnp.arange(length, dtype=jnp.float32) * (2.0 * math.pi / length)
    waves = jnp.stack([jnp.ones_like(phases), jnp.cos(phases), jnp.sin(phases), jnp.cos(2.0 * phases), jnp.sin(2.0 * phases)])
    factors = jnp.array([1.0, 2.0, 2.0, 2.0, 2.0], jnp.float32) * weights
    return waves * jnp.sqrt(factors)[:, None]


def orbital_field(key):
    coeff_key, common_key, white_key = jax.random.split(key, 3)
    weights = jnp.array([0.3, 0.25, 0.25, 0.1, 0.1], jnp.float32)
    common_share = 0.3
    smooth_share = 0.5
    white_share = 1.0 - common_share - smooth_share
    basis_x = wave_basis(GX, weights)
    basis_y = wave_basis(GY, weights)
    basis_z = wave_basis(GZ, weights)
    coeffs = jax.random.normal(coeff_key, (5, 5, 5, NORB), jnp.float32)
    smooth = jnp.einsum('abco,cz->abzo', coeffs, basis_z)
    smooth = jnp.einsum('abzo,by->ayzo', smooth, basis_y)
    smooth = jnp.einsum('ayzo,ax->xyzo', smooth, basis_x)
    common = jax.random.normal(common_key, (NORB,), jnp.float32)
    white_part = jax.random.normal(white_key, (GX, GY, GZ, NORB), jnp.float32)
    orbital = math.sqrt(common_share) * common[None, None, None, :] + math.sqrt(smooth_share) * smooth + math.sqrt(white_share) * white_part
    return jnp.clip(0.25 * orbital, -1.0, 1.0).astype(jnp.bfloat16)


def draw_phi(key, part):
    return orbital_field(jax.random.fold_in(key, 101))


def draw_psi(key, part):
    return orbital_field(jax.random.fold_in(key, 202))


def setup_inputs(seed: int = 0) -> dict:
    splits = jax.random.split(jax.random.key(seed), 4)
    return {
        "phi": draw_phi(jax.random.fold_in(splits[3], 71), 0),
        "psi": draw_psi(jax.random.fold_in(splits[3], 71), 0),
        "points": draw_points(jax.random.fold_in(splits[3], 71), 0),
    }


shift_value = 4.0
box_length = 2.0

def signed_frequency(length):
    index = jnp.arange(length, dtype=jnp.int32)
    return jnp.where(2 * index < length, index, index - length).astype(jnp.float32)

def coulomb_table(x_freq, y_freq, z_freq):
    squared = x_freq[:, None, None] ** 2 + y_freq[None, :, None] ** 2 + z_freq[None, None, :] ** 2
    safe = jnp.maximum(squared, 1.0)
    return jnp.where(squared > 0.5, box_length * box_length / math.pi / safe, 0.0).astype(jnp.float32)

def reference(phi, psi, points):
    flat_phi = phi.reshape(GX * GY * GZ, NORB)
    flat_psi = psi.reshape(GX * GY * GZ, NORB)
    samples_a = jnp.take(flat_phi, points, axis=0)
    samples_b = jnp.take(flat_psi, points, axis=0)
    pivot_a = samples_a[:PB]
    pivot_b = samples_b[:PB]
    global_rows = jnp.arange(NMU, dtype=jnp.int32)
    pivots = jnp.arange(PB, dtype=jnp.int32)
    column_part = jnp.dot(samples_a.astype(jnp.float32), pivot_a.T.astype(jnp.float32), preferred_element_type=jnp.float32) * jnp.dot(samples_b.astype(jnp.float32), pivot_b.T.astype(jnp.float32), preferred_element_type=jnp.float32)
    column_part = column_part + shift_value * (global_rows[:, None] == pivots[None, :]).astype(jnp.float32)
    corner = column_part[:PB]
    lower_factor = jnp.linalg.cholesky(corner)
    inverse = lax.linalg.triangular_solve(lower_factor, jnp.eye(PB, dtype=jnp.float32), left_side=True, lower=True)
    panel = jnp.dot(column_part, inverse.T, precision=lax.Precision.HIGHEST)
    row_count = NMU // N_ROW

    def schur_rows(block_id):
        start = block_id * row_count
        rows_a = lax.dynamic_slice_in_dim(samples_a, start, row_count, 0)
        rows_b = lax.dynamic_slice_in_dim(samples_b, start, row_count, 0)
        rows_panel = lax.dynamic_slice_in_dim(panel, start, row_count, 0)
        index = start + jnp.arange(row_count, dtype=jnp.int32)
        gram = jnp.dot(rows_a.astype(jnp.float32), samples_a.T.astype(jnp.float32), preferred_element_type=jnp.float32) * jnp.dot(rows_b.astype(jnp.float32), samples_b.T.astype(jnp.float32), preferred_element_type=jnp.float32)
        gram = gram + shift_value * (index[:, None] == global_rows[None, :]).astype(jnp.float32)
        return gram - jnp.dot(rows_panel, panel.T, precision=lax.Precision.HIGHEST)
    schur = lax.map(schur_rows, jnp.arange(N_ROW, dtype=jnp.int32)).reshape(NMU, NMU)
    pair_rows = jnp.dot(flat_phi.astype(jnp.float32), pivot_a.T.astype(jnp.float32), preferred_element_type=jnp.float32) * jnp.dot(flat_psi.astype(jnp.float32), pivot_b.T.astype(jnp.float32), preferred_element_type=jnp.float32)
    fitting = jnp.dot(pair_rows, inverse.T, precision=lax.Precision.HIGHEST).reshape(GX, GY, GZ, PB)
    kernel = coulomb_table(signed_frequency(GX), signed_frequency(GY), signed_frequency(GZ))
    spectrum = jnp.fft.fftn(fitting, axes=(0, 1, 2))
    potential = jnp.real(jnp.fft.ifftn(spectrum * kernel[:, :, :, None], axes=(0, 1, 2)))
    return (schur, panel, potential.astype(jnp.float32))
```

```python
import math

import jax
import jax.numpy as jnp
import ml_dtypes
import numpy as np
from jax import lax
from jax.experimental import pallas as pl
from jax.experimental.pallas import tpu as pltpu
from jax.sharding import PartitionSpec as P


PB = 256
LANES = 128
SHIFT = 4.0
BOX = 2.0
LEVELS = 32767.0
STEPS_PER_OCTAVE = 256.0
MIB = 1 << 20
NT = (((1,), (1,)), ((), ()))
highest = lax.Precision.HIGHEST


def cas_table(length):
    index = np.arange(length)
    angle = (index[:, None] * index[None, :] % length) * (2.0 * math.pi / length)
    table = ((np.cos(angle) + np.sin(angle)) / math.sqrt(length)).astype(np.float32)
    high = table.astype(ml_dtypes.bfloat16)
    low = (table - high.astype(np.float32)).astype(ml_dtypes.bfloat16)
    return np.concatenate([high, high, low], axis=1)


def split(value):
    high = value.astype(jnp.bfloat16)
    return high, (value - high.astype(jnp.float32)).astype(jnp.bfloat16)


def stacked(value):
    high, low = split(value)
    return jnp.concatenate([high, low, high], axis=0)


def transform(table, columns):
    data = jnp.concatenate([stacked(c) for c in columns], axis=1)
    out = jnp.dot(table, data, preferred_element_type=jnp.float32)
    return [out[:, i * LANES : (i + 1) * LANES] for i in range(len(columns))]


def encode(rows, padded):
    count = rows.shape[0]
    peak = jnp.maximum(jnp.max(jnp.abs(rows), axis=0, keepdims=True), 1e-30)
    octave = jnp.ceil(jnp.log2(peak) * STEPS_PER_OCTAVE)
    scale = jnp.exp2(octave * (-1.0 / STEPS_PER_OCTAVE)) * LEVELS
    code = jnp.clip(jnp.round(rows * scale), -LEVELS, LEVELS)
    tail = jnp.broadcast_to(octave, (padded - count, LANES))
    return jnp.concatenate([code, tail], axis=0).astype(jnp.int32).astype(jnp.int16)


def decode(block, count):
    value = block.astype(jnp.int32).astype(jnp.float32)
    scale = jnp.exp2(value[count : count + 1] * (1.0 / STEPS_PER_OCTAVE)) * (1.0 / LEVELS)
    return value[:count] * scale


def source_kernel(group, cells, depth, padded, pieces, *refs):
    phi, psi, pivot_a, pivot_b, inverse, table = refs[:6]
    outs, grid_rows = refs[6:-1], refs[-1]
    step = pl.program_id(0)
    first = lax.dot_general(phi[...], pivot_a[...], NT, preferred_element_type=jnp.float32)
    second = lax.dot_general(psi[...], pivot_b[...], NT, preferred_element_type=jnp.float32)
    pair_high, pair_low = split(first * second)
    inv_high, inv_low = split(inverse[...])
    fitting = (
        lax.dot_general(pair_high, inv_high, NT, preferred_element_type=jnp.float32)
        + lax.dot_general(pair_low, inv_high, NT, preferred_element_type=jnp.float32)
        + lax.dot_general(pair_high, inv_low, NT, preferred_element_type=jnp.float32)
    )
    columns = [fitting[g * depth : (g + 1) * depth] for g in range(group)]
    for g, out in enumerate(transform(table[...], columns)):
        grid_rows[pl.ds(step * group + g, depth, stride=cells), :] = out

    @pl.when(step == pl.num_programs(0) - 1)
    def _():
        base = 0
        for out_ref, count in zip(outs, pieces):

            def one(i, carry, base=base, out_ref=out_ref):
                start = pl.multiple_of((base + i) * cells, math.gcd(cells, 8))
                out_ref[i] = encode(grid_rows[pl.ds(start, cells), :], padded)
                return carry

            lax.fori_loop(0, count, one, 0)
            base += count


def source(phi, psi, pivot_a, pivot_b, inverse, table, cells, depth, padded, pieces):
    group = max(g for g in range(1, 11) if cells % g == 0)
    orbitals = phi.shape[1]
    pivots = pivot_a.shape[0]
    whole = lambda shape: pl.BlockSpec(shape, lambda i: (0,) * len(shape))
    return pl.pallas_call(
        lambda *refs: source_kernel(group, cells, depth, padded, pieces, *refs),
        grid=(cells // group,),
        in_specs=[
            pl.BlockSpec((group * depth, orbitals), lambda i: (i, 0)),
            pl.BlockSpec((group * depth, orbitals), lambda i: (i, 0)),
            whole(pivot_a.shape),
            whole(pivot_b.shape),
            whole(inverse.shape),
            whole(table.shape),
        ],
        out_specs=[whole((n, padded, LANES)) for n in pieces],
        out_shape=[jax.ShapeDtypeStruct((n, padded, LANES), jnp.int16) for n in pieces],
        scratch_shapes=[pltpu.VMEM((depth * cells, LANES), jnp.float32)],
        compiler_params=pltpu.CompilerParams(vmem_limit_bytes=50 * MIB),
        cost_estimate=pl.CostEstimate(
            flops=4 * cells * depth * orbitals * pivots + 10 * cells * depth * pivots * LANES,
            bytes_accessed=4 * cells * depth * orbitals + 2 * depth * padded * LANES,
            transcendentals=0,
        ),
        name="source",
    )(phi, psi, pivot_a, pivot_b, inverse, table)


def middle_kernel(sizes, padded, z_freq, piece, x_table, y_table, out_ref, arrived, spectrum):
    grid_x, grid_y, lines, blocks = sizes
    cells = grid_x * grid_y // blocks
    batch = 4

    def load(i, carry):
        start = pl.multiple_of(i * cells, math.gcd(cells, 8))
        arrived[pl.ds(start, cells), :] = decode(piece[i], cells)
        return carry

    lax.fori_loop(0, blocks, load, 0)

    def line_start(y):
        return y // lines * (grid_x * lines) + y % lines

    def x_forward(i, carry):
        ys = [i * batch + b for b in range(batch)]
        columns = [arrived[pl.ds(line_start(y), grid_x, stride=lines), :] for y in ys]
        for y, out in zip(ys, transform(x_table[...], columns)):
            spectrum[pl.ds(y, grid_x, stride=grid_y), :] = out
        return carry

    lax.fori_loop(0, grid_y // batch, x_forward, 0)

    y_index = lax.broadcasted_iota(jnp.int32, (grid_y, LANES), 0)
    y_freq = jnp.minimum(y_index, grid_y - y_index).astype(jnp.float32)
    z_squared = (z_freq[0] * z_freq[0]).astype(jnp.float32)
    yz_squared = y_freq * y_freq + z_squared

    def y_both(i, carry):
        xs = [i * batch + b for b in range(batch)]
        columns = [spectrum[pl.ds(pl.multiple_of(x * grid_y, 8), grid_y), :] for x in xs]
        scaled = []
        for x, out in zip(xs, transform(y_table[...], columns)):
            x_freq = jnp.minimum(x, grid_x - x)
            squared = yz_squared + (x_freq * x_freq).astype(jnp.float32)
            kernel = BOX * BOX / math.pi / jnp.maximum(squared, 1.0)
            scaled.append(jnp.where(squared > 0.5, kernel, 0.0) * out)
        for x, out in zip(xs, transform(y_table[...], scaled)):
            spectrum[pl.ds(pl.multiple_of(x * grid_y, 8), grid_y), :] = out
        return carry

    lax.fori_loop(0, grid_x // batch, y_both, 0)

    def x_back(i, carry):
        ys = [i * batch + b for b in range(batch)]
        columns = [spectrum[pl.ds(y, grid_x, stride=grid_y), :] for y in ys]
        for y, out in zip(ys, transform(x_table[...], columns)):
            arrived[pl.ds(line_start(y), grid_x, stride=lines), :] = out
        return carry

    lax.fori_loop(0, grid_y // batch, x_back, 0)

    def store(i, carry):
        start = pl.multiple_of(i * cells, math.gcd(cells, 8))
        out_ref[i] = encode(arrived[pl.ds(start, cells), :], padded)
        return carry

    lax.fori_loop(0, blocks, store, 0)


def middle(z_freq, piece, x_table, y_table, grid_x, grid_y, lines):
    blocks, padded, _ = piece.shape
    sizes = (grid_x, grid_y, lines, blocks)
    vmem = pl.BlockSpec(memory_space=pltpu.VMEM)
    points = grid_x * grid_y
    return pl.pallas_call(
        lambda *refs: middle_kernel(sizes, padded, *refs),
        in_specs=[pl.BlockSpec(memory_space=pltpu.SMEM), vmem, vmem, vmem],
        out_specs=vmem,
        out_shape=jax.ShapeDtypeStruct(piece.shape, jnp.int16),
        scratch_shapes=[
            pltpu.VMEM((points, LANES), jnp.float32),
            pltpu.VMEM((points, LANES), jnp.float32),
        ],
        compiler_params=pltpu.CompilerParams(vmem_limit_bytes=32 * MIB),
        cost_estimate=pl.CostEstimate(
            flops=12 * points * LANES * (grid_x + grid_y),
            bytes_accessed=4 * blocks * padded * LANES,
            transcendentals=0,
        ),
        name="middle",
    )(z_freq, piece, x_table, y_table)


def target_kernel(group, cells, depth, spans, aliased, *refs):
    count = len(spans)
    arrived, table = refs[:count], refs[count]
    out_ref, grid_rows = refs[-2:]
    step = pl.program_id(0)

    @pl.when(step == 0)
    def _():
        base = 0
        for piece, (start, number) in zip(arrived, spans):

            def one(i, carry, base=base, start=start, piece=piece):
                row = pl.multiple_of((base + i) * cells, math.gcd(cells, 8))
                grid_rows[pl.ds(row, cells), :] = decode(piece[start + i], cells)
                return carry

            lax.fori_loop(0, number, one, 0)
            base += number

    columns = [
        grid_rows[pl.ds(step * group + g, depth, stride=cells), :] for g in range(group)
    ]
    for g, out in enumerate(transform(table[...], columns)):
        out_ref[pl.ds(g * depth, depth), :] = out


def target(pieces, spans, table, before, half, cells, depth, functions):
    group = max(g for g in range(1, 11) if cells % g == 0)
    whole = lambda shape: pl.BlockSpec(shape, lambda i: (0,) * len(shape))
    in_specs = [whole(p.shape) for p in pieces] + [whole(table.shape)]
    operands = [*pieces, table]
    aliases = {}
    if before is not None:
        in_specs.append(pl.BlockSpec(memory_space=pl.ANY))
        aliases = {len(operands): 0}
        operands.append(before)
    return pl.pallas_call(
        lambda *refs: target_kernel(group, cells, depth, spans, before is not None, *refs),
        grid=(cells // group,),
        in_specs=in_specs,
        out_specs=pl.BlockSpec((group * depth, LANES), lambda i: (i, half)),
        out_shape=jax.ShapeDtypeStruct((cells * depth, functions), jnp.float32),
        scratch_shapes=[pltpu.VMEM((depth * cells, LANES), jnp.float32)],
        input_output_aliases=aliases,
        compiler_params=pltpu.CompilerParams(vmem_limit_bytes=50 * MIB),
        cost_estimate=pl.CostEstimate(
            flops=6 * cells * depth * LANES * depth,
            bytes_accessed=6 * cells * depth * LANES,
            transcendentals=0,
        ),
        name="target",
    )(*operands)


def panel_kernel(first_row, left_a, left_b, pivot_a, pivot_b, inverse, panel, high_ref, low_ref):
    step = pl.program_id(0)
    rows, pivots = panel.shape
    gram = lax.dot_general(left_a[...], pivot_a[...], NT, preferred_element_type=jnp.float32)
    gram *= lax.dot_general(left_b[...], pivot_b[...], NT, preferred_element_type=jnp.float32)
    row = lax.broadcasted_iota(jnp.int32, (rows, pivots), 0) + first_row[0] + step * rows
    gram += jnp.where(row == lax.broadcasted_iota(jnp.int32, (rows, pivots), 1), SHIFT, 0.0)
    value = lax.dot_general(
        gram, inverse[...], NT, precision=highest, preferred_element_type=jnp.float32
    )
    panel[...] = value
    high_ref[...], low_ref[...] = split(value)


def panel_rows(first_row, left, pivot, inverse):
    _, rows, orbitals = left.shape
    pivots = pivot.shape[1]
    tile = math.gcd(rows, 512)
    whole = lambda shape: pl.BlockSpec(shape, lambda i: (0,) * len(shape))
    block = lambda width: pl.BlockSpec((tile, width), lambda i: (i, 0))
    shape = lambda dtype: jax.ShapeDtypeStruct((rows, pivots), dtype)
    return pl.pallas_call(
        panel_kernel,
        grid=(rows // tile,),
        in_specs=[
            pl.BlockSpec(memory_space=pltpu.SMEM),
            block(orbitals),
            block(orbitals),
            whole((pivots, orbitals)),
            whole((pivots, orbitals)),
            whole((pivots, pivots)),
        ],
        out_specs=[block(pivots)] * 3,
        out_shape=[shape(jnp.float32), shape(jnp.bfloat16), shape(jnp.bfloat16)],
        compiler_params=pltpu.CompilerParams(vmem_limit_bytes=32 * MIB),
        cost_estimate=pl.CostEstimate(
            flops=16 * rows * pivots * orbitals,
            bytes_accessed=4 * rows * orbitals + 8 * rows * pivots,
            transcendentals=0,
        ),
        name="panel",
    )(first_row, left[0], left[1], pivot[0], pivot[1], inverse)


def schur_kernel(
    offsets, row_a, row_b, row_high, row_low, col_a, col_b, col_high, col_low, out_ref
):
    rows, cols = out_ref.shape
    product = lambda left, right: lax.dot_general(
        left[...], right[...], NT, preferred_element_type=jnp.float32
    )
    gram = product(row_a, col_a) * product(row_b, col_b)
    update = product(row_high, col_high) + (
        product(row_high, col_low) + product(row_low, col_high)
    )
    row_start = offsets[0] + pl.program_id(0) * rows
    col_start = offsets[1] + pl.program_id(1) * cols
    out_ref[...] = gram - update
    overlap = jnp.logical_and(row_start < col_start + cols, col_start < row_start + rows)

    @pl.when(overlap)
    def _():
        row = lax.broadcasted_iota(jnp.int32, (rows, cols), 0) + row_start
        col = lax.broadcasted_iota(jnp.int32, (rows, cols), 1) + col_start
        out_ref[...] += jnp.where(row == col, SHIFT, 0.0)


def schur_block(offsets, row_side, col_side):
    rows, orbitals = row_side[0].shape
    cols = col_side[0].shape[0]
    row_tile, col_tile = math.gcd(rows, 512), math.gcd(cols, 1024)
    row_block = lambda a: pl.BlockSpec((row_tile, a.shape[1]), lambda i, j: (i, 0))
    col_block = lambda a: pl.BlockSpec((col_tile, a.shape[1]), lambda i, j: (j, 0))
    return pl.pallas_call(
        schur_kernel,
        grid=(rows // row_tile, cols // col_tile),
        in_specs=[
            pl.BlockSpec(memory_space=pltpu.SMEM),
            *[row_block(a) for a in row_side],
            *[col_block(a) for a in col_side],
        ],
        out_specs=pl.BlockSpec((row_tile, col_tile), lambda i, j: (i, j)),
        out_shape=jax.ShapeDtypeStruct((rows, cols), jnp.float32),
        compiler_params=pltpu.CompilerParams(vmem_limit_bytes=50 * MIB),
        cost_estimate=pl.CostEstimate(
            flops=10 * rows * cols * orbitals,
            bytes_accessed=4 * rows * cols + 8 * (rows + cols) * orbitals,
            transcendentals=0,
        ),
        name="schur",
    )(offsets, *row_side, *col_side)


def lower_inverse(corner):
    factor = lax.linalg.cholesky(corner, symmetrize_input=False)
    return factor, lax.linalg.triangular_solve(
        factor, jnp.eye(corner.shape[0], dtype=jnp.float32), left_side=True, lower=True
    )


def on_device(phi, psi, points):
    col_count = lax.axis_size("col")
    row_count = lax.axis_size("row")
    col_index = lax.axis_index("col")
    row_index = lax.axis_index("row")
    axes = ("row", "col")
    devices = row_count * col_count
    me = row_index * col_count + col_index
    plane_count, line_count, depth, orbitals = phi.shape
    grid_x, grid_y = plane_count * col_count, line_count * row_count
    cells = plane_count * line_count
    flat_phi = phi.reshape(cells * depth, orbitals)
    flat_psi = psi.reshape(cells * depth, orbitals)
    owned = points.shape[0]
    half = PB // 2

    global_x = points // (grid_y * depth)
    global_y = points // depth % grid_y
    local_cell = (
        (global_x - col_index * plane_count) * line_count + global_y - row_index * line_count
    ) * depth + points % depth

    slot = jnp.arange(PB, dtype=jnp.int32) - me * owned
    is_owned = jnp.logical_and(slot >= 0, slot < owned)
    pivot_cell = jnp.take(local_cell, jnp.clip(slot, 0, owned - 1), axis=0, mode="clip")
    pivot = jnp.stack(
        [
            jnp.take(flat_phi, pivot_cell, axis=0, mode="clip"),
            jnp.take(flat_psi, pivot_cell, axis=0, mode="clip"),
        ]
    )
    pivot = jnp.where(is_owned[None, :, None], pivot, jnp.zeros_like(pivot))
    pivot = lax.psum(pivot, axes)

    own = jnp.stack(
        [
            jnp.take(flat_phi, local_cell, axis=0, mode="clip"),
            jnp.take(flat_psi, local_cell, axis=0, mode="clip"),
        ]
    )
    swap = [
        (c * row_count + r, r * col_count + c)
        for r in range(row_count)
        for c in range(col_count)
    ]
    crossed = lax.ppermute(own, axes, swap)
    row_samples = lax.all_gather(own, "col", axis=1, tiled=True)
    col_samples = lax.all_gather(crossed, "row", axis=1, tiled=True)

    gram = lambda left, right: lax.dot_general(
        pivot[0, left], pivot[0, right], NT, preferred_element_type=jnp.float32
    ) * lax.dot_general(pivot[1, left], pivot[1, right], NT, preferred_element_type=jnp.float32)
    shift = SHIFT * jnp.eye(half, dtype=jnp.float32)
    lead, rest = slice(0, half), slice(half, PB)
    _, lead_inverse = lower_inverse(gram(lead, lead) + shift)
    matmul = lambda a, b: jnp.dot(a, b, precision=highest)
    coupling = matmul(gram(rest, lead), lead_inverse.T)
    _, rest_inverse = lower_inverse(gram(rest, rest) + shift - matmul(coupling, coupling.T))
    lower_left = -matmul(rest_inverse, matmul(coupling, lead_inverse))
    rest_rows = jnp.concatenate([lower_left, rest_inverse], axis=1)
    lead_rows = jnp.concatenate([lead_inverse, jnp.zeros_like(lead_inverse)], axis=1)
    inverse = jnp.concatenate([lead_rows, rest_rows], axis=0)

    x_table, y_table, z_table = (jnp.asarray(cas_table(n)) for n in (grid_x, grid_y, depth))
    padded = (cells // 16 + 1) * 16
    halves = PB // LANES
    rounds = -(-depth * halves // devices)
    parts = []
    for h in range(halves):
        edges = [h * depth, (h + 1) * depth]
        cuts = [k * devices for k in range(rounds) if edges[0] < k * devices < edges[1]]
        marks = [edges[0], *cuts, edges[1]]
        parts.append([(a // devices, a % devices, b - a) for a, b in zip(marks, marks[1:])])

    outgoing = [[] for _ in range(rounds)]
    for h, rows in enumerate((lead_inverse, rest_rows)):
        used = rows.shape[1]
        made = source(
            flat_phi,
            flat_psi,
            pivot[0, :used],
            pivot[1, :used],
            rows,
            z_table,
            cells,
            depth,
            padded,
            [n for _, _, n in parts[h]],
        )
        for (k, _, _), piece in zip(parts[h], made):
            outgoing[k].append(piece)
    spare = rounds * devices - depth * halves
    if spare:
        outgoing[-1].append(jnp.zeros((spare, padded, LANES), jnp.int16))

    exchange = lambda a: lax.all_to_all(a, axes, split_axis=0, concat_axis=0, tiled=True)
    returned = []
    for k, pieces in enumerate(outgoing):
        sent = pieces[0] if len(pieces) == 1 else jnp.concatenate(pieces, axis=0)
        unit = k * devices + me
        z_index = unit % depth
        z_freq = jnp.minimum(z_index, depth - z_index).astype(jnp.int32).reshape(1)
        back = middle(z_freq, exchange(sent), x_table, y_table, grid_x, grid_y, line_count)
        returned.append(exchange(back))

    potential = None
    for h in range(halves):
        potential = target(
            [returned[k] for k, _, _ in parts[h]],
            [(a, n) for _, a, n in parts[h]],
            z_table,
            potential,
            h,
            cells,
            depth,
            PB,
        )
    potential = potential.reshape(plane_count, line_count, depth, PB)

    row_start = row_index * row_samples.shape[1]
    col_start = col_index * col_samples.shape[1]
    scalar = lambda *v: jnp.stack([jnp.asarray(a, jnp.int32) for a in v])
    panel, row_high, row_low = panel_rows(scalar(row_start), row_samples, pivot, inverse)
    _, col_high, col_low = panel_rows(scalar(col_start), col_samples, pivot, inverse)
    schur = schur_block(
        scalar(row_start, col_start),
        (row_samples[0], row_samples[1], row_high, row_low),
        (col_samples[0], col_samples[1], col_high, col_low),
    )
    return (schur, panel, potential)


def solution(mesh):
    in_specs = (P("col", "row", None, None), P("col", "row", None, None), P(("row", "col")))
    out_specs = (P("row", "col"), P("row", None), P("col", "row", None, None))
    return jax.shard_map(
        on_device, mesh=mesh, in_specs=in_specs, out_specs=out_specs, check_vma=False
    )
```

```python
import math

import jax
import jax.numpy as jnp
import ml_dtypes
import numpy as np
from jax import lax
from jax.experimental import pallas as pl
from jax.experimental.pallas import tpu as pltpu
from jax.sharding import PartitionSpec as P


PB = 256
LANES = 128
SHIFT = 4.0
BOX = 2.0
LEVELS = 32767.0
STEPS_PER_OCTAVE = 256.0
MIB = 1 << 20
NT = (((1,), (1,)), ((), ()))
highest = lax.Precision.HIGHEST


def cost(micros, moved):
    return pl.CostEstimate(
        flops=int(micros * 1.15e9), bytes_accessed=int(moved), transcendentals=0
    )


def cas_table(length):
    index = np.arange(length)
    angle = (index[:, None] * index[None, :] % length) * (2.0 * math.pi / length)
    table = ((np.cos(angle) + np.sin(angle)) / math.sqrt(length)).astype(np.float32)
    high = table.astype(ml_dtypes.bfloat16)
    low = (table - high.astype(np.float32)).astype(ml_dtypes.bfloat16)
    return np.concatenate([high, high, low], axis=1)


def split(value):
    high = value.astype(jnp.bfloat16)
    return high, (value - high.astype(jnp.float32)).astype(jnp.bfloat16)


def stacked(value):
    high, low = split(value)
    return jnp.concatenate([high, low, high], axis=0)


def transform(table, columns):
    data = jnp.concatenate([stacked(c) for c in columns], axis=1)
    out = jnp.dot(table, data, preferred_element_type=jnp.float32)
    return [out[:, i * LANES : (i + 1) * LANES] for i in range(len(columns))]


def encode(rows, padded):
    count = rows.shape[0]
    peak = jnp.maximum(jnp.max(jnp.abs(rows), axis=0, keepdims=True), 1e-30)
    octave = jnp.ceil(jnp.log2(peak) * STEPS_PER_OCTAVE)
    scale = jnp.exp2(octave * (-1.0 / STEPS_PER_OCTAVE)) * LEVELS
    code = jnp.clip(jnp.round(rows * scale), -LEVELS, LEVELS)
    tail = jnp.broadcast_to(octave, (padded - count, LANES))
    return jnp.concatenate([code, tail], axis=0).astype(jnp.int32).astype(jnp.int16)


def decode(block, count):
    value = block.astype(jnp.int32).astype(jnp.float32)
    scale = jnp.exp2(value[count : count + 1] * (1.0 / STEPS_PER_OCTAVE)) * (1.0 / LEVELS)
    return value[:count] * scale


def source_kernel(group, cells, depth, padded, pieces, *refs):
    phi, psi, pivot_a, pivot_b, inverse, table = refs[:6]
    outs, grid_rows = refs[6:-1], refs[-1]
    step = pl.program_id(0)
    first = lax.dot_general(phi[...], pivot_a[...], NT, preferred_element_type=jnp.float32)
    second = lax.dot_general(psi[...], pivot_b[...], NT, preferred_element_type=jnp.float32)
    pair_high, pair_low = split(first * second)
    inv_high, inv_low = split(inverse[...])
    fitting = product_nt(
        jnp.concatenate([pair_high, pair_low, pair_high], axis=1),
        jnp.concatenate([inv_high, inv_high, inv_low], axis=1),
    )
    columns = [fitting[g * depth : (g + 1) * depth] for g in range(group)]
    for g, out in enumerate(transform(table[...], columns)):
        grid_rows[pl.ds(step * group + g, depth, stride=cells), :] = out

    @pl.when(step == pl.num_programs(0) - 1)
    def _():
        base = 0
        for out_ref, count in zip(outs, pieces):

            def one(i, carry, base=base, out_ref=out_ref):
                start = pl.multiple_of((base + i) * cells, math.gcd(cells, 8))
                out_ref[i] = encode(grid_rows[pl.ds(start, cells), :], padded)
                return carry

            lax.fori_loop(0, count, one, 0)
            base += count


def source(phi, psi, pivot_a, pivot_b, inverse, half, table, cells, depth, padded, pieces):
    group = max(g for g in range(1, 11) if cells % g == 0)
    orbitals = phi.shape[1]
    pivots = pivot_a.shape[0]
    whole = lambda shape: pl.BlockSpec(shape, lambda i: (0,) * len(shape))
    return pl.pallas_call(
        lambda *refs: source_kernel(group, cells, depth, padded, pieces, *refs),
        grid=(cells // group,),
        in_specs=[
            pl.BlockSpec((group * depth, orbitals), lambda i: (i, 0)),
            pl.BlockSpec((group * depth, orbitals), lambda i: (i, 0)),
            whole(pivot_a.shape),
            whole(pivot_b.shape),
            pl.BlockSpec((LANES, pivots), lambda i: (half, 0)),
            whole(table.shape),
        ],
        out_specs=[whole((n, padded, LANES)) for n in pieces],
        out_shape=[jax.ShapeDtypeStruct((n, padded, LANES), jnp.int16) for n in pieces],
        scratch_shapes=[pltpu.VMEM((depth * cells, LANES), jnp.float32)],
        compiler_params=pltpu.CompilerParams(vmem_limit_bytes=50 * MIB),
        cost_estimate=cost(
            cells * depth / 600, 4 * cells * depth * orbitals
        ),
        name="source",
    )(phi, psi, pivot_a, pivot_b, inverse, table)


def middle_kernel(sizes, padded, z_freq, piece, x_table, y_table, out_ref, arrived, spectrum):
    grid_x, grid_y, lines, blocks = sizes
    cells = grid_x * grid_y // blocks
    batch = 4

    def load(i, carry):
        start = pl.multiple_of(i * cells, math.gcd(cells, 8))
        arrived[pl.ds(start, cells), :] = decode(piece[i], cells)
        return carry

    lax.fori_loop(0, blocks, load, 0)

    def line_start(y):
        return y // lines * (grid_x * lines) + y % lines

    def x_forward(i, carry):
        ys = [i * batch + b for b in range(batch)]
        columns = [arrived[pl.ds(line_start(y), grid_x, stride=lines), :] for y in ys]
        for y, out in zip(ys, transform(x_table[...], columns)):
            spectrum[pl.ds(y, grid_x, stride=grid_y), :] = out
        return carry

    lax.fori_loop(0, grid_y // batch, x_forward, 0)

    y_index = lax.broadcasted_iota(jnp.int32, (grid_y, LANES), 0)
    y_freq = jnp.minimum(y_index, grid_y - y_index).astype(jnp.float32)
    z_squared = (z_freq[0] * z_freq[0]).astype(jnp.float32)
    yz_squared = y_freq * y_freq + z_squared

    def y_both(i, carry):
        xs = [i * batch + b for b in range(batch)]
        columns = [spectrum[pl.ds(pl.multiple_of(x * grid_y, 8), grid_y), :] for x in xs]
        scaled = []
        for x, out in zip(xs, transform(y_table[...], columns)):
            x_freq = jnp.minimum(x, grid_x - x)
            squared = yz_squared + (x_freq * x_freq).astype(jnp.float32)
            kernel = BOX * BOX / math.pi / jnp.maximum(squared, 1.0)
            scaled.append(jnp.where(squared > 0.5, kernel, 0.0) * out)
        for x, out in zip(xs, transform(y_table[...], scaled)):
            spectrum[pl.ds(pl.multiple_of(x * grid_y, 8), grid_y), :] = out
        return carry

    lax.fori_loop(0, grid_x // batch, y_both, 0)

    def x_back(i, carry):
        ys = [i * batch + b for b in range(batch)]
        columns = [spectrum[pl.ds(y, grid_x, stride=grid_y), :] for y in ys]
        for y, out in zip(ys, transform(x_table[...], columns)):
            arrived[pl.ds(line_start(y), grid_x, stride=lines), :] = out
        return carry

    lax.fori_loop(0, grid_y // batch, x_back, 0)

    def store(i, carry):
        start = pl.multiple_of(i * cells, math.gcd(cells, 8))
        out_ref[i] = encode(arrived[pl.ds(start, cells), :], padded)
        return carry

    lax.fori_loop(0, blocks, store, 0)


def middle(z_freq, piece, x_table, y_table, grid_x, grid_y, lines, after):
    blocks, padded, _ = piece.shape
    sizes = (grid_x, grid_y, lines, blocks)
    vmem = pl.BlockSpec(memory_space=pltpu.VMEM)
    points = grid_x * grid_y
    return pl.pallas_call(
        lambda *refs: middle_kernel(sizes, padded, *refs[:4], *refs[4 + len(after) :]),
        in_specs=[
            pl.BlockSpec(memory_space=pltpu.SMEM),
            vmem,
            vmem,
            vmem,
            *[pl.BlockSpec(memory_space=pl.ANY) for _ in after],
        ],
        out_specs=vmem,
        out_shape=jax.ShapeDtypeStruct(piece.shape, jnp.int16),
        scratch_shapes=[
            pltpu.VMEM((points, LANES), jnp.float32),
            pltpu.VMEM((points, LANES), jnp.float32),
        ],
        compiler_params=pltpu.CompilerParams(vmem_limit_bytes=32 * MIB),
        cost_estimate=cost(points / 400, 4 * blocks * padded * LANES),
        name="middle",
    )(z_freq, piece, x_table, y_table, *after)


def target_kernel(group, cells, depth, spans, *refs):
    count = len(spans)
    arrived, table = refs[:count], refs[count]
    out_ref, grid_rows = refs[-2:]
    step = pl.program_id(0)

    @pl.when(step == 0)
    def _():
        base = 0
        for piece, (start, number) in zip(arrived, spans):

            def one(i, carry, base=base, start=start, piece=piece):
                row = pl.multiple_of((base + i) * cells, math.gcd(cells, 8))
                grid_rows[pl.ds(row, cells), :] = decode(piece[start + i], cells)
                return carry

            lax.fori_loop(0, number, one, 0)
            base += number

    columns = [
        grid_rows[pl.ds(step * group + g, depth, stride=cells), :] for g in range(group)
    ]
    for g, out in enumerate(transform(table[...], columns)):
        out_ref[pl.ds(g * depth, depth), :] = out


def target(pieces, spans, table, before, half, cells, depth, functions):
    group = max(g for g in range(1, 11) if cells % g == 0)
    whole = lambda shape: pl.BlockSpec(shape, lambda i: (0,) * len(shape))
    in_specs = [whole(p.shape) for p in pieces] + [whole(table.shape)]
    operands = [*pieces, table]
    aliases = {}
    if before is not None:
        in_specs.append(pl.BlockSpec(memory_space=pl.ANY))
        aliases = {len(operands): 0}
        operands.append(before)
    return pl.pallas_call(
        lambda *refs: target_kernel(group, cells, depth, spans, *refs),
        grid=(cells // group,),
        in_specs=in_specs,
        out_specs=pl.BlockSpec((group * depth, LANES), lambda i: (i, half)),
        out_shape=jax.ShapeDtypeStruct((cells * depth, functions), jnp.float32),
        scratch_shapes=[pltpu.VMEM((depth * cells, LANES), jnp.float32)],
        input_output_aliases=aliases,
        compiler_params=pltpu.CompilerParams(vmem_limit_bytes=50 * MIB),
        cost_estimate=cost(cells * depth / 1200, 6 * cells * depth * LANES),
        name="target",
    )(*operands)


def panel_kernel(first_row, left_a, left_b, pivot_a, pivot_b, inverse, panel, high_ref, low_ref):
    step = pl.program_id(0)
    rows, pivots = panel.shape
    gram = lax.dot_general(left_a[...], pivot_a[...], NT, preferred_element_type=jnp.float32)
    gram *= lax.dot_general(left_b[...], pivot_b[...], NT, preferred_element_type=jnp.float32)
    row = lax.broadcasted_iota(jnp.int32, (rows, pivots), 0) + first_row[0] + step * rows
    gram += jnp.where(row == lax.broadcasted_iota(jnp.int32, (rows, pivots), 1), SHIFT, 0.0)
    value = lax.dot_general(
        gram, inverse[...], NT, precision=highest, preferred_element_type=jnp.float32
    )
    panel[...] = value
    high_ref[...], low_ref[...] = split(value)


def panel_rows(first_row, left, pivot, inverse):
    _, rows, orbitals = left.shape
    pivots = pivot.shape[1]
    tile = math.gcd(rows, 512)
    whole = lambda shape: pl.BlockSpec(shape, lambda i: (0,) * len(shape))
    block = lambda width: pl.BlockSpec((tile, width), lambda i: (i, 0))
    shape = lambda dtype: jax.ShapeDtypeStruct((rows, pivots), dtype)
    return pl.pallas_call(
        panel_kernel,
        grid=(rows // tile,),
        in_specs=[
            pl.BlockSpec(memory_space=pltpu.SMEM),
            block(orbitals),
            block(orbitals),
            whole((pivots, orbitals)),
            whole((pivots, orbitals)),
            whole((pivots, pivots)),
        ],
        out_specs=[block(pivots)] * 3,
        out_shape=[shape(jnp.float32), shape(jnp.bfloat16), shape(jnp.bfloat16)],
        compiler_params=pltpu.CompilerParams(vmem_limit_bytes=32 * MIB),
        cost_estimate=cost(rows / 400, 4 * rows * orbitals + 8 * rows * pivots),
        name="panel",
    )(first_row, left[0], left[1], pivot[0], pivot[1], inverse)


def schur_kernel(
    offsets, row_a, row_b, row_high, row_low, col_a, col_b, col_high, col_low, out_ref
):
    rows, cols = out_ref.shape
    product = lambda left, right: lax.dot_general(
        left[...], right[...], NT, preferred_element_type=jnp.float32
    )
    gram = product(row_a, col_a) * product(row_b, col_b)
    update = product(row_high, col_high) + (
        product(row_high, col_low) + product(row_low, col_high)
    )
    row_start = offsets[0] + pl.program_id(0) * rows
    col_start = offsets[1] + pl.program_id(1) * cols
    out_ref[...] = gram - update
    overlap = jnp.logical_and(row_start < col_start + cols, col_start < row_start + rows)

    @pl.when(overlap)
    def _():
        row = lax.broadcasted_iota(jnp.int32, (rows, cols), 0) + row_start
        col = lax.broadcasted_iota(jnp.int32, (rows, cols), 1) + col_start
        out_ref[...] += jnp.where(row == col, SHIFT, 0.0)


def schur_block(offsets, row_side, col_side):
    rows, orbitals = row_side[0].shape
    cols = col_side[0].shape[0]
    row_tile, col_tile = math.gcd(rows, 512), math.gcd(cols, 1024)
    row_block = lambda a: pl.BlockSpec((row_tile, a.shape[1]), lambda i, j: (i, 0))
    col_block = lambda a: pl.BlockSpec((col_tile, a.shape[1]), lambda i, j: (j, 0))
    return pl.pallas_call(
        schur_kernel,
        grid=(rows // row_tile, cols // col_tile),
        in_specs=[
            pl.BlockSpec(memory_space=pltpu.SMEM),
            *[row_block(a) for a in row_side],
            *[col_block(a) for a in col_side],
        ],
        out_specs=pl.BlockSpec((row_tile, col_tile), lambda i, j: (i, j)),
        out_shape=jax.ShapeDtypeStruct((rows, cols), jnp.float32),
        compiler_params=pltpu.CompilerParams(vmem_limit_bytes=50 * MIB),
        cost_estimate=cost(rows * cols / 240000, 4 * rows * cols),
        name="schur",
    )(offsets, *row_side, *col_side)


def factor_inverse(matrix):
    size = matrix.shape[0]
    strip_rows = 16
    row = lax.broadcasted_iota(jnp.int32, (size, size), 0)
    col = lax.broadcasted_iota(jnp.int32, (size, size), 1)
    work = jnp.concatenate([matrix, jnp.where(row == col, 1.0, 0.0)], axis=1)
    strip_row = lax.broadcasted_iota(jnp.int32, (strip_rows, size), 0)
    inverse = []
    for start in range(0, size, strip_rows):
        strip = work[start : start + strip_rows]
        cols = [
            jnp.broadcast_to(strip[:, start + t : start + t + 1], (strip_rows, size))
            for t in range(strip_rows)
        ]
        diagonal = jnp.ones((strip_rows, size), jnp.float32)
        for t in range(strip_rows):
            factor = jnp.where(strip_row > t, cols[t] * (1.0 / cols[t][t : t + 1]), 0.0)
            diagonal = jnp.where(strip_row == t, cols[t], diagonal)
            for u in range(t + 1, strip_rows):
                cols[u] = cols[u] - factor * cols[u][t : t + 1]
            strip = strip - jnp.concatenate([factor, factor], axis=1) * strip[t : t + 1]
        root = lax.rsqrt(diagonal)
        root = root * (1.5 - 0.5 * diagonal * root * root)
        strip = strip * jnp.concatenate([root, root], axis=1)
        inverse.append(strip[:, size:])
        if start + strip_rows < size:
            work = work - lax.dot_general(
                strip[:, :size],
                strip,
                (((0,), (0,)), ((), ())),
                precision=highest,
                preferred_element_type=jnp.float32,
            )
    return jnp.concatenate(inverse, axis=0)


def product_nt(left, right):
    return lax.dot_general(left, right, NT, preferred_element_type=jnp.float32)


def exact(left, right, dims=(((1,), (0,)), ((), ()))):
    return lax.dot_general(
        left, right, dims, precision=highest, preferred_element_type=jnp.float32
    )


def shifted(gram):
    row = lax.broadcasted_iota(jnp.int32, gram.shape, 0)
    col = lax.broadcasted_iota(jnp.int32, gram.shape, 1)
    return gram + jnp.where(row == col, SHIFT, 0.0)


def lead_kernel(pivot_a, pivot_b, inverse):
    a, b = pivot_a[...], pivot_b[...]
    inverse[...] = factor_inverse(shifted(product_nt(a, a) * product_nt(b, b)))


def rest_kernel(pivot_a, pivot_b, lead_inverse, inverse):
    half = lead_inverse.shape[0]
    lead = lead_inverse[...]
    gram = product_nt(pivot_a[pl.ds(half, half), :], pivot_a[...]) * product_nt(
        pivot_b[pl.ds(half, half), :], pivot_b[...]
    )
    coupling = exact(gram[:, :half], lead, NT)
    rest = factor_inverse(shifted(gram[:, half:]) - exact(coupling, coupling, NT))
    inverse[pl.ds(0, half), :] = jnp.concatenate([lead, jnp.zeros_like(lead)], axis=1)
    lower_left = -exact(rest, exact(coupling, lead))
    inverse[pl.ds(half, half), :] = jnp.concatenate([lower_left, rest], axis=1)


def factor_call(kernel, name, size, micros, *operands):
    vmem = pl.BlockSpec(memory_space=pltpu.VMEM)
    return pl.pallas_call(
        kernel,
        in_specs=[vmem] * len(operands),
        out_specs=vmem,
        out_shape=jax.ShapeDtypeStruct((size, size), jnp.float32),
        compiler_params=pltpu.CompilerParams(vmem_limit_bytes=32 * MIB),
        cost_estimate=cost(micros, 8 * size * size),
        name=name,
    )(*operands)


def on_device(phi, psi, points):
    col_count = lax.axis_size("col")
    row_count = lax.axis_size("row")
    col_index = lax.axis_index("col")
    row_index = lax.axis_index("row")
    axes = ("row", "col")
    devices = row_count * col_count
    me = row_index * col_count + col_index
    plane_count, line_count, depth, orbitals = phi.shape
    grid_x, grid_y = plane_count * col_count, line_count * row_count
    cells = plane_count * line_count
    flat_phi = phi.reshape(cells * depth, orbitals)
    flat_psi = psi.reshape(cells * depth, orbitals)
    owned = points.shape[0]
    half = PB // 2

    global_x = points // (grid_y * depth)
    global_y = points // depth % grid_y
    local_cell = (
        (global_x - col_index * plane_count) * line_count + global_y - row_index * line_count
    ) * depth + points % depth

    own = jnp.stack(
        [
            jnp.take(flat_phi, local_cell, axis=0, mode="clip"),
            jnp.take(flat_psi, local_cell, axis=0, mode="clip"),
        ]
    )
    exchange = lambda a: lax.all_to_all(a, axes, split_axis=0, concat_axis=0, tiled=True)

    held = min(owned, PB)
    piece_rows = 2 * PB // devices
    offered = jnp.concatenate([own[:, :held]] * (PB // held), axis=1)
    offered = exchange(offered.reshape(devices, piece_rows, orbitals))
    owner = me * piece_rows % PB // owned
    piece = lax.dynamic_index_in_dim(offered, owner, axis=0, keepdims=True)
    pivot = exchange(jnp.broadcast_to(piece, offered.shape)).reshape(2, PB, orbitals)

    own, pivot = lax.optimization_barrier((own, pivot))
    swap = [
        (c * row_count + r, r * col_count + c)
        for r in range(row_count)
        for c in range(col_count)
    ]
    crossed = lax.ppermute(own, axes, swap)
    row_samples = lax.all_gather(own, "col", axis=1, tiled=True)
    col_samples = lax.all_gather(crossed, "row", axis=1, tiled=True)

    lead_inverse = factor_call(lead_kernel, "lead", half, 10, pivot[0, :half], pivot[1, :half])
    inverse = factor_call(rest_kernel, "rest", PB, 14, pivot[0], pivot[1], lead_inverse)

    x_table, y_table, z_table = (jnp.asarray(cas_table(n)) for n in (grid_x, grid_y, depth))
    padded = (cells // 16 + 1) * 16
    halves = PB // LANES
    rounds = -(-depth * halves // devices)
    parts = []
    for h in range(halves):
        edges = [h * depth, (h + 1) * depth]
        cuts = [k * devices for k in range(rounds) if edges[0] < k * devices < edges[1]]
        marks = [edges[0], *cuts, edges[1]]
        parts.append([(a // devices, a % devices, b - a) for a, b in zip(marks, marks[1:])])

    outgoing = [[] for _ in range(rounds)]
    for h, rows in enumerate((lead_inverse, inverse)):
        used = rows.shape[1]
        made = source(
            flat_phi,
            flat_psi,
            pivot[0, :used],
            pivot[1, :used],
            rows,
            h,
            z_table,
            cells,
            depth,
            padded,
            [n for _, _, n in parts[h]],
        )
        for (k, _, _), piece in zip(parts[h], made):
            outgoing[k].append(piece)
    spare = rounds * devices - depth * halves
    if spare:
        outgoing[-1].append(jnp.zeros((spare, padded, LANES), jnp.int16))

    row_start = row_index * row_samples.shape[1]
    col_start = col_index * col_samples.shape[1]
    scalar = lambda *v: jnp.stack([jnp.asarray(a, jnp.int32) for a in v])
    panel, row_high, row_low = panel_rows(scalar(row_start), row_samples, pivot, inverse)
    _, col_high, col_low = panel_rows(scalar(col_start), col_samples, pivot, inverse)
    schur = schur_block(
        scalar(row_start, col_start),
        (row_samples[0], row_samples[1], row_high, row_low),
        (col_samples[0], col_samples[1], col_high, col_low),
    )

    waits = [[] for _ in range(rounds)]
    waits[0] += [made[-1], row_samples, col_samples]
    waits[min(2, rounds - 1)] += [row_high, col_high]
    waits[min(3, rounds - 1)] += [schur]
    latest = None

    def in_turn(block):
        nonlocal latest
        if latest is not None:
            block, latest = lax.optimization_barrier((block, latest))
        latest = exchange(block)
        return latest

    arrived, returned = [], []
    for k in range(rounds + 1):
        if k < rounds:
            pieces = outgoing[k]
            sent = pieces[0] if len(pieces) == 1 else jnp.concatenate(pieces, axis=0)
            arrived.append(in_turn(sent))
        if k > 0:
            z_index = ((k - 1) * devices + me) % depth
            z_freq = jnp.minimum(z_index, depth - z_index).astype(jnp.int32).reshape(1)
            back = middle(
                z_freq,
                arrived[k - 1],
                x_table,
                y_table,
                grid_x,
                grid_y,
                line_count,
                waits[k - 1],
            )
            returned.append(in_turn(back))

    potential = None
    for h in range(halves):
        potential = target(
            [returned[k] for k, _, _ in parts[h]],
            [(a, n) for _, a, n in parts[h]],
            z_table,
            potential,
            h,
            cells,
            depth,
            PB,
        )
    potential = potential.reshape(plane_count, line_count, depth, PB)
    return (schur, panel, potential)


def solution(mesh):
    in_specs = (P("col", "row", None, None), P("col", "row", None, None), P(("row", "col")))
    out_specs = (P("row", "col"), P("row", None), P("col", "row", None, None))
    return jax.shard_map(
        on_device, mesh=mesh, in_specs=in_specs, out_specs=out_specs, check_vma=False
    )
```

```python
import math

import jax
import jax.numpy as jnp
import ml_dtypes
import numpy as np
from jax import lax
from jax.experimental import pallas as pl
from jax.experimental.pallas import tpu as pltpu
from jax.sharding import PartitionSpec as P


PB = 256
GROUP = 20
LANES = 128
SHIFT = 4.0
BOX = 2.0
LEVELS = 32767.0
STEPS_PER_OCTAVE = 256.0
MIB = 1 << 20
NT = (((1,), (1,)), ((), ()))
highest = lax.Precision.HIGHEST


def cost(micros, moved):
    return pl.CostEstimate(
        flops=int(micros * 1.15e9), bytes_accessed=int(moved), transcendentals=0
    )


def cas_table(length):
    index = np.arange(length)
    angle = (index[:, None] * index[None, :] % length) * (2.0 * math.pi / length)
    table = ((np.cos(angle) + np.sin(angle)) / math.sqrt(length)).astype(np.float32)
    high = table.astype(ml_dtypes.bfloat16)
    low = (table - high.astype(np.float32)).astype(ml_dtypes.bfloat16)
    return np.concatenate([high, high, low], axis=1)


def split(value):
    high = value.astype(jnp.bfloat16)
    return high, (value - high.astype(jnp.float32)).astype(jnp.bfloat16)


def stacked(value):
    high, low = split(value)
    return jnp.concatenate([high, low, high], axis=0)


def transform(table, columns):
    data = jnp.concatenate([stacked(c) for c in columns], axis=1)
    out = jnp.dot(table, data, preferred_element_type=jnp.float32)
    return [out[:, i * LANES : (i + 1) * LANES] for i in range(len(columns))]


def encode(rows, padded):
    count = rows.shape[0]
    peak = jnp.maximum(jnp.max(jnp.abs(rows), axis=0, keepdims=True), 1e-30)
    octave = jnp.ceil(jnp.log2(peak) * STEPS_PER_OCTAVE)
    scale = jnp.exp2(octave * (-1.0 / STEPS_PER_OCTAVE)) * LEVELS
    code = jnp.clip(jnp.round(rows * scale), -LEVELS, LEVELS)
    tail = jnp.broadcast_to(octave, (padded - count, LANES))
    return jnp.concatenate([code, tail], axis=0).astype(jnp.int32).astype(jnp.int16)


def decode(block, count):
    value = block.astype(jnp.int32).astype(jnp.float32)
    scale = jnp.exp2(value[count : count + 1] * (1.0 / STEPS_PER_OCTAVE)) * (1.0 / LEVELS)
    return value[:count] * scale


def source_kernel(group, cells, depth, padded, pieces, *refs):
    phi, psi, pivot_a, pivot_b, inverse, table = refs[:6]
    outs, grid_rows = refs[6:-1], refs[-1]
    step = pl.program_id(0)
    first = lax.dot_general(phi[...], pivot_a[...], NT, preferred_element_type=jnp.float32)
    second = lax.dot_general(psi[...], pivot_b[...], NT, preferred_element_type=jnp.float32)
    pair_high, pair_low = split(first * second)
    inv_high, inv_low = split(inverse[...])
    fitting = product_nt(
        jnp.concatenate([pair_high, pair_low, pair_high], axis=1),
        jnp.concatenate([inv_high, inv_high, inv_low], axis=1),
    )
    columns = [fitting[g * depth : (g + 1) * depth] for g in range(group)]
    for g, out in enumerate(transform(table[...], columns)):
        grid_rows[pl.ds(step * group + g, out.shape[0], stride=cells), :] = out

    @pl.when(step == pl.num_programs(0) - 1)
    def _():
        base = 0
        for out_ref, count in zip(outs, pieces):

            def one(i, carry, base=base, out_ref=out_ref):
                start = pl.multiple_of((base + i) * cells, math.gcd(cells, 8))
                out_ref[i] = encode(grid_rows[pl.ds(start, cells), :], padded)
                return carry

            lax.fori_loop(0, count, one, 0)
            base += count


def source(phi, psi, pivot_a, pivot_b, inverse, half, table, cells, depth, padded, pieces):
    group = max(g for g in range(1, GROUP + 1) if cells % g == 0)
    orbitals = phi.shape[1]
    pivots = pivot_a.shape[0]
    whole = lambda shape: pl.BlockSpec(shape, lambda i: (0,) * len(shape))
    return pl.pallas_call(
        lambda *refs: source_kernel(group, cells, depth, padded, pieces, *refs),
        grid=(cells // group,),
        in_specs=[
            pl.BlockSpec((group * depth, orbitals), lambda i: (i, 0)),
            pl.BlockSpec((group * depth, orbitals), lambda i: (i, 0)),
            whole(pivot_a.shape),
            whole(pivot_b.shape),
            pl.BlockSpec((LANES, pivots), lambda i: (half, 0)),
            whole(table.shape),
        ],
        out_specs=[whole((n, padded, LANES)) for n in pieces],
        out_shape=[jax.ShapeDtypeStruct((n, padded, LANES), jnp.int16) for n in pieces],
        scratch_shapes=[pltpu.VMEM((table.shape[0] * cells, LANES), jnp.float32)],
        compiler_params=pltpu.CompilerParams(vmem_limit_bytes=50 * MIB),
        cost_estimate=cost(
            cells * depth / 600, 4 * cells * depth * orbitals
        ),
        name="source",
    )(phi, psi, pivot_a, pivot_b, inverse, table)


def middle_kernel(sizes, padded, z_freq, piece, x_table, y_table, out_ref, arrived, spectrum):
    grid_x, grid_y, lines, blocks = sizes
    cells = grid_x * grid_y // blocks
    batch = 4

    def load(i, carry):
        start = pl.multiple_of(i * cells, math.gcd(cells, 8))
        arrived[pl.ds(start, cells), :] = decode(piece[i], cells)
        return carry

    lax.fori_loop(0, blocks, load, 0)

    def line_start(y):
        return y // lines * (grid_x * lines) + y % lines

    def x_forward(i, carry):
        ys = [i * batch + b for b in range(batch)]
        columns = [arrived[pl.ds(line_start(y), grid_x, stride=lines), :] for y in ys]
        for y, out in zip(ys, transform(x_table[...], columns)):
            spectrum[pl.ds(y, grid_x, stride=grid_y), :] = out
        return carry

    lax.fori_loop(0, grid_y // batch, x_forward, 0)

    y_index = lax.broadcasted_iota(jnp.int32, (grid_y, LANES), 0)
    y_freq = jnp.minimum(y_index, grid_y - y_index).astype(jnp.float32)
    z_squared = (z_freq[0] * z_freq[0]).astype(jnp.float32)
    yz_squared = y_freq * y_freq + z_squared

    def y_both(i, carry):
        xs = [i * batch + b for b in range(batch)]
        columns = [spectrum[pl.ds(pl.multiple_of(x * grid_y, 8), grid_y), :] for x in xs]
        scaled = []
        for x, out in zip(xs, transform(y_table[...], columns)):
            x_freq = jnp.minimum(x, grid_x - x)
            squared = yz_squared + (x_freq * x_freq).astype(jnp.float32)
            kernel = BOX * BOX / math.pi / jnp.maximum(squared, 1.0)
            scaled.append(jnp.where(squared > 0.5, kernel, 0.0) * out)
        for x, out in zip(xs, transform(y_table[...], scaled)):
            spectrum[pl.ds(pl.multiple_of(x * grid_y, 8), grid_y), :] = out
        return carry

    lax.fori_loop(0, grid_x // batch, y_both, 0)

    def x_back(i, carry):
        ys = [i * batch + b for b in range(batch)]
        columns = [spectrum[pl.ds(y, grid_x, stride=grid_y), :] for y in ys]
        for y, out in zip(ys, transform(x_table[...], columns)):
            arrived[pl.ds(line_start(y), grid_x, stride=lines), :] = out
        return carry

    lax.fori_loop(0, grid_y // batch, x_back, 0)

    def store(i, carry):
        start = pl.multiple_of(i * cells, math.gcd(cells, 8))
        out_ref[i] = encode(arrived[pl.ds(start, cells), :], padded)
        return carry

    lax.fori_loop(0, blocks, store, 0)


def middle(z_freq, piece, x_table, y_table, grid_x, grid_y, lines):
    blocks, padded, _ = piece.shape
    sizes = (grid_x, grid_y, lines, blocks)
    vmem = pl.BlockSpec(memory_space=pltpu.VMEM)
    points = grid_x * grid_y
    return pl.pallas_call(
        lambda *refs: middle_kernel(sizes, padded, *refs),
        in_specs=[pl.BlockSpec(memory_space=pltpu.SMEM), vmem, vmem, vmem],
        out_specs=vmem,
        out_shape=jax.ShapeDtypeStruct(piece.shape, jnp.int16),
        scratch_shapes=[
            pltpu.VMEM((points, LANES), jnp.float32),
            pltpu.VMEM((points, LANES), jnp.float32),
        ],
        compiler_params=pltpu.CompilerParams(vmem_limit_bytes=32 * MIB),
        cost_estimate=cost(points / 400, 4 * blocks * padded * LANES),
        name="middle",
    )(z_freq, piece, x_table, y_table)


def target_kernel(group, cells, depth, spans, *refs):
    count = len(spans)
    arrived, table = refs[:count], refs[count]
    out_ref, grid_rows = refs[-2:]
    step = pl.program_id(0)

    @pl.when(step == 0)
    def _():
        base = 0
        for piece, (start, number) in zip(arrived, spans):

            def one(i, carry, base=base, start=start, piece=piece):
                row = pl.multiple_of((base + i) * cells, math.gcd(cells, 8))
                grid_rows[pl.ds(row, cells), :] = decode(piece[start + i], cells)
                return carry

            lax.fori_loop(0, number, one, 0)
            base += number

    columns = [
        grid_rows[pl.ds(step * group + g, depth, stride=cells), :] for g in range(group)
    ]
    for g, out in enumerate(transform(table[...], columns)):
        out_ref[pl.ds(g * depth, depth), :] = out


def target(pieces, spans, table, before, half, cells, depth, functions):
    group = max(g for g in range(1, GROUP + 1) if cells % g == 0)
    whole = lambda shape: pl.BlockSpec(shape, lambda i: (0,) * len(shape))
    in_specs = [whole(p.shape) for p in pieces] + [whole(table.shape)]
    operands = [*pieces, table]
    aliases = {}
    if before is not None:
        in_specs.append(pl.BlockSpec(memory_space=pl.ANY))
        aliases = {len(operands): 0}
        operands.append(before)
    return pl.pallas_call(
        lambda *refs: target_kernel(group, cells, depth, spans, *refs),
        grid=(cells // group,),
        in_specs=in_specs,
        out_specs=pl.BlockSpec((group * depth, LANES), lambda i: (i, half)),
        out_shape=jax.ShapeDtypeStruct((cells * depth, functions), jnp.float32),
        scratch_shapes=[pltpu.VMEM((depth * cells, LANES), jnp.float32)],
        input_output_aliases=aliases,
        compiler_params=pltpu.CompilerParams(vmem_limit_bytes=50 * MIB),
        cost_estimate=cost(cells * depth / 1200, 6 * cells * depth * LANES),
        name="target",
    )(*operands)


def panel_kernel(first_row, left_a, left_b, pivot_a, pivot_b, inverse, panel, high_ref, low_ref):
    step = pl.program_id(0)
    rows, pivots = panel.shape
    gram = lax.dot_general(left_a[...], pivot_a[...], NT, preferred_element_type=jnp.float32)
    gram *= lax.dot_general(left_b[...], pivot_b[...], NT, preferred_element_type=jnp.float32)
    row = lax.broadcasted_iota(jnp.int32, (rows, pivots), 0) + first_row[0] + step * rows
    gram += jnp.where(row == lax.broadcasted_iota(jnp.int32, (rows, pivots), 1), SHIFT, 0.0)
    value = lax.dot_general(
        gram, inverse[...], NT, precision=highest, preferred_element_type=jnp.float32
    )
    panel[...] = value
    high_ref[...], low_ref[...] = split(value)


def panel_rows(first_row, left, pivot, inverse):
    _, rows, orbitals = left.shape
    pivots = pivot.shape[1]
    tile = math.gcd(rows, 512)
    whole = lambda shape: pl.BlockSpec(shape, lambda i: (0,) * len(shape))
    block = lambda width: pl.BlockSpec((tile, width), lambda i: (i, 0))
    shape = lambda dtype: jax.ShapeDtypeStruct((rows, pivots), dtype)
    return pl.pallas_call(
        panel_kernel,
        grid=(rows // tile,),
        in_specs=[
            pl.BlockSpec(memory_space=pltpu.SMEM),
            block(orbitals),
            block(orbitals),
            whole((pivots, orbitals)),
            whole((pivots, orbitals)),
            whole((pivots, pivots)),
        ],
        out_specs=[block(pivots)] * 3,
        out_shape=[shape(jnp.float32), shape(jnp.bfloat16), shape(jnp.bfloat16)],
        compiler_params=pltpu.CompilerParams(vmem_limit_bytes=32 * MIB),
        cost_estimate=cost(rows / 400, 4 * rows * orbitals + 8 * rows * pivots),
        name="panel",
    )(first_row, left[0], left[1], pivot[0], pivot[1], inverse)


def schur_kernel(
    offsets, row_a, row_b, row_high, row_low, col_a, col_b, col_high, col_low, out_ref
):
    rows, cols = out_ref.shape
    product = lambda left, right: lax.dot_general(
        left[...], right[...], NT, preferred_element_type=jnp.float32
    )
    gram = product(row_a, col_a) * product(row_b, col_b)
    update = product(row_high, col_high) + (
        product(row_high, col_low) + product(row_low, col_high)
    )
    row_start = offsets[0] + pl.program_id(0) * rows
    col_start = offsets[1] + pl.program_id(1) * cols
    out_ref[...] = gram - update
    overlap = jnp.logical_and(row_start < col_start + cols, col_start < row_start + rows)

    @pl.when(overlap)
    def _():
        row = lax.broadcasted_iota(jnp.int32, (rows, cols), 0) + row_start
        col = lax.broadcasted_iota(jnp.int32, (rows, cols), 1) + col_start
        out_ref[...] += jnp.where(row == col, SHIFT, 0.0)


def schur_block(offsets, row_side, col_side):
    rows, orbitals = row_side[0].shape
    cols = col_side[0].shape[0]
    row_tile, col_tile = math.gcd(rows, 512), math.gcd(cols, 1024)
    row_block = lambda a: pl.BlockSpec((row_tile, a.shape[1]), lambda i, j: (i, 0))
    col_block = lambda a: pl.BlockSpec((col_tile, a.shape[1]), lambda i, j: (j, 0))
    return pl.pallas_call(
        schur_kernel,
        grid=(rows // row_tile, cols // col_tile),
        in_specs=[
            pl.BlockSpec(memory_space=pltpu.SMEM),
            *[row_block(a) for a in row_side],
            *[col_block(a) for a in col_side],
        ],
        out_specs=pl.BlockSpec((row_tile, col_tile), lambda i, j: (i, j)),
        out_shape=jax.ShapeDtypeStruct((rows, cols), jnp.float32),
        compiler_params=pltpu.CompilerParams(vmem_limit_bytes=50 * MIB),
        cost_estimate=cost(rows * cols / 240000, 4 * rows * cols),
        name="schur",
    )(offsets, *row_side, *col_side)


def factor_inverse(matrix):
    size = matrix.shape[0]
    strip_rows = 16
    row = lax.broadcasted_iota(jnp.int32, (size, size), 0)
    col = lax.broadcasted_iota(jnp.int32, (size, size), 1)
    work = jnp.concatenate([matrix, jnp.where(row == col, 1.0, 0.0)], axis=1)
    strip_row = lax.broadcasted_iota(jnp.int32, (strip_rows, size), 0)
    inverse = []
    for start in range(0, size, strip_rows):
        strip = work[start : start + strip_rows]
        cols = [
            jnp.broadcast_to(strip[:, start + t : start + t + 1], (strip_rows, size))
            for t in range(strip_rows)
        ]
        diagonal = jnp.ones((strip_rows, size), jnp.float32)
        for t in range(strip_rows):
            factor = jnp.where(strip_row > t, cols[t] * (1.0 / cols[t][t : t + 1]), 0.0)
            diagonal = jnp.where(strip_row == t, cols[t], diagonal)
            for u in range(t + 1, strip_rows):
                cols[u] = cols[u] - factor * cols[u][t : t + 1]
            strip = strip - jnp.concatenate([factor, factor], axis=1) * strip[t : t + 1]
        root = lax.rsqrt(diagonal)
        root = root * (1.5 - 0.5 * diagonal * root * root)
        strip = strip * jnp.concatenate([root, root], axis=1)
        inverse.append(strip[:, size:])
        if start + strip_rows < size:
            work = work - lax.dot_general(
                strip[:, :size],
                strip,
                (((0,), (0,)), ((), ())),
                precision=highest,
                preferred_element_type=jnp.float32,
            )
    return jnp.concatenate(inverse, axis=0)


def product_nt(left, right):
    return lax.dot_general(left, right, NT, preferred_element_type=jnp.float32)


def exact(left, right, dims=(((1,), (0,)), ((), ()))):
    return lax.dot_general(
        left, right, dims, precision=highest, preferred_element_type=jnp.float32
    )


def shifted(gram):
    row = lax.broadcasted_iota(jnp.int32, gram.shape, 0)
    col = lax.broadcasted_iota(jnp.int32, gram.shape, 1)
    return gram + jnp.where(row == col, SHIFT, 0.0)


def lead_kernel(pivot_a, pivot_b, inverse):
    a, b = pivot_a[...], pivot_b[...]
    inverse[...] = factor_inverse(shifted(product_nt(a, a) * product_nt(b, b)))


def rest_kernel(pivot_a, pivot_b, lead_inverse, inverse):
    half = lead_inverse.shape[0]
    lead = lead_inverse[...]
    gram = product_nt(pivot_a[pl.ds(half, half), :], pivot_a[...]) * product_nt(
        pivot_b[pl.ds(half, half), :], pivot_b[...]
    )
    coupling = exact(gram[:, :half], lead, NT)
    rest = factor_inverse(shifted(gram[:, half:]) - exact(coupling, coupling, NT))
    inverse[pl.ds(0, half), :] = jnp.concatenate([lead, jnp.zeros_like(lead)], axis=1)
    lower_left = -exact(rest, exact(coupling, lead))
    inverse[pl.ds(half, half), :] = jnp.concatenate([lower_left, rest], axis=1)


def factor_call(kernel, name, size, micros, *operands):
    vmem = pl.BlockSpec(memory_space=pltpu.VMEM)
    return pl.pallas_call(
        kernel,
        in_specs=[vmem] * len(operands),
        out_specs=vmem,
        out_shape=jax.ShapeDtypeStruct((size, size), jnp.float32),
        compiler_params=pltpu.CompilerParams(vmem_limit_bytes=32 * MIB),
        cost_estimate=cost(micros, 8 * size * size),
        name=name,
    )(*operands)


def on_device(phi, psi, points):
    col_count = lax.axis_size("col")
    row_count = lax.axis_size("row")
    col_index = lax.axis_index("col")
    row_index = lax.axis_index("row")
    axes = ("row", "col")
    devices = row_count * col_count
    me = row_index * col_count + col_index
    plane_count, line_count, depth, orbitals = phi.shape
    grid_x, grid_y = plane_count * col_count, line_count * row_count
    cells = plane_count * line_count
    flat_phi = phi.reshape(cells * depth, orbitals)
    flat_psi = psi.reshape(cells * depth, orbitals)
    owned = points.shape[0]
    half = PB // 2

    global_x = points // (grid_y * depth)
    global_y = points // depth % grid_y
    local_cell = (
        (global_x - col_index * plane_count) * line_count + global_y - row_index * line_count
    ) * depth + points % depth

    own = jnp.stack(
        [
            jnp.take(flat_phi, local_cell, axis=0, mode="clip"),
            jnp.take(flat_psi, local_cell, axis=0, mode="clip"),
        ]
    )
    exchange = lambda a: lax.all_to_all(a, axes, split_axis=0, concat_axis=0, tiled=True)

    held = min(owned, PB)
    piece_rows = 2 * PB // devices
    offered = jnp.concatenate([own[:, :held]] * (PB // held), axis=1)
    swap = [
        (c * row_count + r, r * col_count + c)
        for r in range(row_count)
        for c in range(col_count)
    ]
    crossed = lax.ppermute(own, axes, swap)
    offered = exchange(offered.reshape(devices, piece_rows, orbitals))
    own, crossed, offered = lax.optimization_barrier((own, crossed, offered))
    owner = me * piece_rows % PB // owned
    piece = lax.dynamic_index_in_dim(offered, owner, axis=0, keepdims=True)
    pivot = exchange(jnp.broadcast_to(piece, offered.shape)).reshape(2, PB, orbitals)

    row_samples = lax.all_gather(own, "col", axis=1, tiled=True)

    lead_inverse = factor_call(lead_kernel, "lead", half, 10, pivot[0, :half], pivot[1, :half])
    inverse = factor_call(rest_kernel, "rest", PB, 14, pivot[0], pivot[1], lead_inverse)

    x_table, y_table, z_table = (jnp.asarray(cas_table(n)) for n in (grid_x, grid_y, depth))
    padded = (cells // 16 + 1) * 16
    halves = PB // LANES
    rounds = -(-depth * halves // devices)
    parts = []
    for h in range(halves):
        edges = [h * depth, (h + 1) * depth]
        cuts = [k * devices for k in range(rounds) if edges[0] < k * devices < edges[1]]
        marks = [edges[0], *cuts, edges[1]]
        parts.append([(a // devices, a % devices, b - a) for a, b in zip(marks, marks[1:])])

    outgoing = [[] for _ in range(rounds)]

    def make(h, chosen, rows):
        used = rows.shape[1]
        first = chosen[0][0] * devices + chosen[0][1] - h * depth
        count = sum(n for _, _, n in chosen)
        made = source(
            flat_phi,
            flat_psi,
            pivot[0, :used],
            pivot[1, :used],
            rows,
            h,
            z_table[first : first + count],
            cells,
            depth,
            padded,
            [n for _, _, n in chosen],
        )
        for (k, _, _), part in zip(chosen, made):
            outgoing[k].append(part)

    def after(value, gate):
        return lax.optimization_barrier((value, gate))[0]

    make(0, parts[0][:1], lead_inverse)
    if parts[0][1:]:
        make(0, parts[0][1:], after(lead_inverse, row_samples))
    row_start = row_index * row_samples.shape[1]
    col_start = col_index * row_count * owned
    scalar = lambda *v: jnp.stack([jnp.asarray(a, jnp.int32) for a in v])

    latest = outgoing[0][0]
    columns = crossed.reshape(2, 1, owned, orbitals)
    distances = [1 << b for b in reversed(range(row_count.bit_length() - 1))]

    def double(block):
        distance = distances.pop(0)
        pairs = [(r, r ^ distance) for r in range(row_count)]
        other = lax.ppermute(block, "row", pairs)
        upper = row_index // distance % 2 == 1
        halves = [jnp.where(upper, other, block), jnp.where(upper, block, other)]
        return jnp.stack(halves, axis=2).reshape(2, -1, owned, orbitals)

    def in_turn(block, *ready):
        nonlocal latest, columns
        before, latest = latest, lax.optimization_barrier((block, latest, columns, *ready))[0]
        if distances:
            columns = double(after(columns, before))
        latest = exchange(latest)
        return latest

    second_round = parts[1][0][0]
    panel_round = max(min(2, rounds - 1), second_round)
    schur_round = max(min(3, rounds - 1), panel_round)
    ready = []
    arrived, returned = [], []
    for k in range(rounds + 1):
        if k == second_round:
            gated = after(inverse, latest if k < 2 else arrived[k - 1])
            make(1, parts[1], gated)
        if k < rounds:
            pieces = list(outgoing[k])
            spare = devices - sum(p.shape[0] for p in pieces)
            if spare:
                pieces.append(jnp.zeros((spare, padded, LANES), jnp.int16))
            sent = pieces[0] if len(pieces) == 1 else jnp.concatenate(pieces, axis=0)
            arrived.append(in_turn(sent, *ready))
            ready = []
        if k == panel_round:
            while distances:
                columns = double(columns)
            col_samples = columns.reshape(2, row_count * owned, orbitals)
            gated = after(inverse, latest)
            panel, row_high, row_low = panel_rows(scalar(row_start), row_samples, pivot, gated)
            _, col_high, col_low = panel_rows(scalar(col_start), col_samples, pivot, gated)
            ready += [row_high, col_high]
        if k == schur_round:
            schur = schur_block(
                after(scalar(row_start, col_start), latest),
                (row_samples[0], row_samples[1], row_high, row_low),
                (col_samples[0], col_samples[1], col_high, col_low),
            )
            ready += [schur]
        if k > 0:
            z_index = ((k - 1) * devices + me) % depth
            z_freq = jnp.minimum(z_index, depth - z_index).astype(jnp.int32).reshape(1)
            back = middle(
                z_freq, arrived[k - 1], x_table, y_table, grid_x, grid_y, line_count
            )
            returned.append(in_turn(back))

    potential = None
    for h in range(halves):
        potential = target(
            [returned[k] for k, _, _ in parts[h]],
            [(a, n) for _, a, n in parts[h]],
            z_table,
            potential,
            h,
            cells,
            depth,
            PB,
        )
    potential = potential.reshape(plane_count, line_count, depth, PB)
    return (schur, panel, potential)


def solution(mesh):
    in_specs = (P("col", "row", None, None), P("col", "row", None, None), P(("row", "col")))
    out_specs = (P("row", "col"), P("row", None), P("col", "row", None, None))
    return jax.shard_map(
        on_device, mesh=mesh, in_specs=in_specs, out_specs=out_specs, check_vma=False
    )
```

```python
import math

import jax
import jax.numpy as jnp
import ml_dtypes
import numpy as np
from jax import lax
from jax.experimental import pallas as pl
from jax.experimental.pallas import tpu as pltpu
from jax.sharding import PartitionSpec as P


PB = 256
GROUP = 40
LANES = 128
SHIFT = 4.0
BOX = 2.0
LEVELS = 32767.0
STEPS_PER_OCTAVE = 256.0
MIB = 1 << 20
NT = (((1,), (1,)), ((), ()))
highest = lax.Precision.HIGHEST


def cost(micros, moved):
    return pl.CostEstimate(
        flops=int(micros * 1.15e9), bytes_accessed=int(moved), transcendentals=0
    )


def cas_table(length):
    index = np.arange(length)
    angle = (index[:, None] * index[None, :] % length) * (2.0 * math.pi / length)
    table = ((np.cos(angle) + np.sin(angle)) / math.sqrt(length)).astype(np.float32)
    high = table.astype(ml_dtypes.bfloat16)
    low = (table - high.astype(np.float32)).astype(ml_dtypes.bfloat16)
    return np.concatenate([high, high, low], axis=1)


def split(value):
    high = value.astype(jnp.bfloat16)
    return high, (value - high.astype(jnp.float32)).astype(jnp.bfloat16)


def stacked(value):
    high, low = split(value)
    return jnp.concatenate([high, low, high], axis=0)


def transform(table, columns):
    data = jnp.concatenate([stacked(c) for c in columns], axis=1)
    out = jnp.dot(table, data, preferred_element_type=jnp.float32)
    return [out[:, i * LANES : (i + 1) * LANES] for i in range(len(columns))]


def encode(rows, padded):
    count = rows.shape[0]
    peak = jnp.maximum(jnp.max(jnp.abs(rows), axis=0, keepdims=True), 1e-30)
    octave = jnp.ceil(jnp.log2(peak) * STEPS_PER_OCTAVE)
    scale = jnp.exp2(octave * (-1.0 / STEPS_PER_OCTAVE)) * LEVELS
    code = jnp.clip(jnp.round(rows * scale), -LEVELS, LEVELS)
    tail = jnp.broadcast_to(octave, (padded - count, LANES))
    return jnp.concatenate([code, tail], axis=0).astype(jnp.int32).astype(jnp.int16)


def decode(block, count):
    value = block.astype(jnp.int32).astype(jnp.float32)
    scale = jnp.exp2(value[count : count + 1] * (1.0 / STEPS_PER_OCTAVE)) * (1.0 / LEVELS)
    return value[:count] * scale


def source_kernel(group, cells, depth, padded, pieces, *refs):
    phi, psi, pivot_a, pivot_b, inverse, table = refs[:6]
    outs, grid_rows = refs[6:-1], refs[-1]
    step = pl.program_id(0)
    first = lax.dot_general(phi[...], pivot_a[...], NT, preferred_element_type=jnp.float32)
    second = lax.dot_general(psi[...], pivot_b[...], NT, preferred_element_type=jnp.float32)
    pair_high, pair_low = split(first * second)
    inv_high, inv_low = split(inverse[...])
    fitting = product_nt(
        jnp.concatenate([pair_high, pair_low, pair_high], axis=1),
        jnp.concatenate([inv_high, inv_high, inv_low], axis=1),
    )
    columns = [fitting[g * depth : (g + 1) * depth] for g in range(group)]
    for g, out in enumerate(transform(table[...], columns)):
        grid_rows[pl.ds(step * group + g, out.shape[0], stride=cells), :] = out

    @pl.when(step == pl.num_programs(0) - 1)
    def _():
        base = 0
        for out_ref, count in zip(outs, pieces):

            def one(i, carry, base=base, out_ref=out_ref):
                start = pl.multiple_of((base + i) * cells, math.gcd(cells, 8))
                out_ref[i] = encode(grid_rows[pl.ds(start, cells), :], padded)
                return carry

            lax.fori_loop(0, count, one, 0)
            base += count


def source(phi, psi, pivot_a, pivot_b, inverse, half, table, cells, depth, padded, pieces):
    group = max(g for g in range(1, GROUP + 1) if cells % g == 0)
    orbitals = phi.shape[1]
    pivots = pivot_a.shape[0]
    whole = lambda shape: pl.BlockSpec(shape, lambda i: (0,) * len(shape))
    return pl.pallas_call(
        lambda *refs: source_kernel(group, cells, depth, padded, pieces, *refs),
        grid=(cells // group,),
        in_specs=[
            pl.BlockSpec((group * depth, orbitals), lambda i: (i, 0)),
            pl.BlockSpec((group * depth, orbitals), lambda i: (i, 0)),
            whole(pivot_a.shape),
            whole(pivot_b.shape),
            pl.BlockSpec((LANES, pivots), lambda i: (half, 0)),
            whole(table.shape),
        ],
        out_specs=[whole((n, padded, LANES)) for n in pieces],
        out_shape=[jax.ShapeDtypeStruct((n, padded, LANES), jnp.int16) for n in pieces],
        scratch_shapes=[pltpu.VMEM((table.shape[0] * cells, LANES), jnp.float32)],
        compiler_params=pltpu.CompilerParams(vmem_limit_bytes=50 * MIB),
        cost_estimate=cost(
            cells * depth / 600, 4 * cells * depth * orbitals
        ),
        name="source",
    )(phi, psi, pivot_a, pivot_b, inverse, table)


def middle_kernel(sizes, padded, z_freq, piece, x_table, y_table, out_ref, arrived, spectrum):
    grid_x, grid_y, lines, blocks = sizes
    cells = grid_x * grid_y // blocks
    batch = 4

    def load(i, carry):
        start = pl.multiple_of(i * cells, math.gcd(cells, 8))
        arrived[pl.ds(start, cells), :] = decode(piece[i], cells)
        return carry

    lax.fori_loop(0, blocks, load, 0)

    def line_start(y):
        return y // lines * (grid_x * lines) + y % lines

    def x_forward(i, carry):
        ys = [i * batch + b for b in range(batch)]
        columns = [arrived[pl.ds(line_start(y), grid_x, stride=lines), :] for y in ys]
        for y, out in zip(ys, transform(x_table[...], columns)):
            spectrum[pl.ds(y, grid_x, stride=grid_y), :] = out
        return carry

    lax.fori_loop(0, grid_y // batch, x_forward, 0)

    y_index = lax.broadcasted_iota(jnp.int32, (grid_y, LANES), 0)
    y_freq = jnp.minimum(y_index, grid_y - y_index).astype(jnp.float32)
    z_squared = (z_freq[0] * z_freq[0]).astype(jnp.float32)
    yz_squared = y_freq * y_freq + z_squared

    def y_both(i, carry):
        xs = [i * batch + b for b in range(batch)]
        columns = [spectrum[pl.ds(pl.multiple_of(x * grid_y, 8), grid_y), :] for x in xs]
        scaled = []
        for x, out in zip(xs, transform(y_table[...], columns)):
            x_freq = jnp.minimum(x, grid_x - x)
            squared = yz_squared + (x_freq * x_freq).astype(jnp.float32)
            kernel = BOX * BOX / math.pi / jnp.maximum(squared, 1.0)
            scaled.append(jnp.where(squared > 0.5, kernel, 0.0) * out)
        for x, out in zip(xs, transform(y_table[...], scaled)):
            spectrum[pl.ds(pl.multiple_of(x * grid_y, 8), grid_y), :] = out
        return carry

    lax.fori_loop(0, grid_x // batch, y_both, 0)

    def x_back(i, carry):
        ys = [i * batch + b for b in range(batch)]
        columns = [spectrum[pl.ds(y, grid_x, stride=grid_y), :] for y in ys]
        for y, out in zip(ys, transform(x_table[...], columns)):
            arrived[pl.ds(line_start(y), grid_x, stride=lines), :] = out
        return carry

    lax.fori_loop(0, grid_y // batch, x_back, 0)

    def store(i, carry):
        start = pl.multiple_of(i * cells, math.gcd(cells, 8))
        out_ref[i] = encode(arrived[pl.ds(start, cells), :], padded)
        return carry

    lax.fori_loop(0, blocks, store, 0)


def middle(z_freq, piece, x_table, y_table, grid_x, grid_y, lines):
    blocks, padded, _ = piece.shape
    sizes = (grid_x, grid_y, lines, blocks)
    vmem = pl.BlockSpec(memory_space=pltpu.VMEM)
    points = grid_x * grid_y
    return pl.pallas_call(
        lambda *refs: middle_kernel(sizes, padded, *refs),
        in_specs=[pl.BlockSpec(memory_space=pltpu.SMEM), vmem, vmem, vmem],
        out_specs=vmem,
        out_shape=jax.ShapeDtypeStruct(piece.shape, jnp.int16),
        scratch_shapes=[
            pltpu.VMEM((points, LANES), jnp.float32),
            pltpu.VMEM((points, LANES), jnp.float32),
        ],
        compiler_params=pltpu.CompilerParams(vmem_limit_bytes=32 * MIB),
        cost_estimate=cost(points / 400, 4 * blocks * padded * LANES),
        name="middle",
    )(z_freq, piece, x_table, y_table)


def target_kernel(group, cells, depth, spans, *refs):
    count = len(spans)
    arrived, table = refs[:count], refs[count]
    out_ref, grid_rows = refs[-2:]
    step = pl.program_id(0)

    @pl.when(step == 0)
    def _():
        base = 0
        for piece, (start, number) in zip(arrived, spans):

            def one(i, carry, base=base, start=start, piece=piece):
                row = pl.multiple_of((base + i) * cells, math.gcd(cells, 8))
                grid_rows[pl.ds(row, cells), :] = decode(piece[start + i], cells)
                return carry

            lax.fori_loop(0, number, one, 0)
            base += number

    columns = [
        grid_rows[pl.ds(step * group + g, depth, stride=cells), :] for g in range(group)
    ]
    for g, out in enumerate(transform(table[...], columns)):
        out_ref[pl.ds(g * depth, depth), :] = out


def target(pieces, spans, table, before, half, cells, depth, functions):
    group = max(g for g in range(1, GROUP + 1) if cells % g == 0)
    whole = lambda shape: pl.BlockSpec(shape, lambda i: (0,) * len(shape))
    in_specs = [whole(p.shape) for p in pieces] + [whole(table.shape)]
    operands = [*pieces, table]
    aliases = {}
    if before is not None:
        in_specs.append(pl.BlockSpec(memory_space=pl.ANY))
        aliases = {len(operands): 0}
        operands.append(before)
    return pl.pallas_call(
        lambda *refs: target_kernel(group, cells, depth, spans, *refs),
        grid=(cells // group,),
        in_specs=in_specs,
        out_specs=pl.BlockSpec((group * depth, LANES), lambda i: (i, half)),
        out_shape=jax.ShapeDtypeStruct((cells * depth, functions), jnp.float32),
        scratch_shapes=[pltpu.VMEM((depth * cells, LANES), jnp.float32)],
        input_output_aliases=aliases,
        compiler_params=pltpu.CompilerParams(vmem_limit_bytes=50 * MIB),
        cost_estimate=cost(cells * depth / 1200, 6 * cells * depth * LANES),
        name="target",
    )(*operands)


def panel_kernel(first_row, left_a, left_b, pivot_a, pivot_b, inverse, panel, high_ref, low_ref):
    step = pl.program_id(0)
    rows, pivots = panel.shape
    gram = lax.dot_general(left_a[...], pivot_a[...], NT, preferred_element_type=jnp.float32)
    gram *= lax.dot_general(left_b[...], pivot_b[...], NT, preferred_element_type=jnp.float32)
    row = lax.broadcasted_iota(jnp.int32, (rows, pivots), 0) + first_row[0] + step * rows
    gram += jnp.where(row == lax.broadcasted_iota(jnp.int32, (rows, pivots), 1), SHIFT, 0.0)
    value = lax.dot_general(
        gram, inverse[...], NT, precision=highest, preferred_element_type=jnp.float32
    )
    panel[...] = value
    high_ref[...], low_ref[...] = split(value)


def panel_rows(first_row, left, pivot, inverse):
    _, rows, orbitals = left.shape
    pivots = pivot.shape[1]
    tile = math.gcd(rows, 512)
    whole = lambda shape: pl.BlockSpec(shape, lambda i: (0,) * len(shape))
    block = lambda width: pl.BlockSpec((tile, width), lambda i: (i, 0))
    shape = lambda dtype: jax.ShapeDtypeStruct((rows, pivots), dtype)
    return pl.pallas_call(
        panel_kernel,
        grid=(rows // tile,),
        in_specs=[
            pl.BlockSpec(memory_space=pltpu.SMEM),
            block(orbitals),
            block(orbitals),
            whole((pivots, orbitals)),
            whole((pivots, orbitals)),
            whole((pivots, pivots)),
        ],
        out_specs=[block(pivots)] * 3,
        out_shape=[shape(jnp.float32), shape(jnp.bfloat16), shape(jnp.bfloat16)],
        compiler_params=pltpu.CompilerParams(vmem_limit_bytes=32 * MIB),
        cost_estimate=cost(rows / 400, 4 * rows * orbitals + 8 * rows * pivots),
        name="panel",
    )(first_row, left[0], left[1], pivot[0], pivot[1], inverse)


def schur_kernel(
    offsets, row_a, row_b, row_high, row_low, col_a, col_b, col_high, col_low, out_ref
):
    rows, cols = out_ref.shape
    product = lambda left, right: lax.dot_general(
        left[...], right[...], NT, preferred_element_type=jnp.float32
    )
    gram = product(row_a, col_a) * product(row_b, col_b)
    update = product(row_high, col_high) + (
        product(row_high, col_low) + product(row_low, col_high)
    )
    row_start = offsets[0] + pl.program_id(0) * rows
    col_start = offsets[1] + pl.program_id(1) * cols
    out_ref[...] = gram - update
    overlap = jnp.logical_and(row_start < col_start + cols, col_start < row_start + rows)

    @pl.when(overlap)
    def _():
        row = lax.broadcasted_iota(jnp.int32, (rows, cols), 0) + row_start
        col = lax.broadcasted_iota(jnp.int32, (rows, cols), 1) + col_start
        out_ref[...] += jnp.where(row == col, SHIFT, 0.0)


def schur_block(offsets, row_side, col_side):
    rows, orbitals = row_side[0].shape
    cols = col_side[0].shape[0]
    row_tile, col_tile = math.gcd(rows, 512), math.gcd(cols, 1024)
    row_block = lambda a: pl.BlockSpec((row_tile, a.shape[1]), lambda i, j: (i, 0))
    col_block = lambda a: pl.BlockSpec((col_tile, a.shape[1]), lambda i, j: (j, 0))
    return pl.pallas_call(
        schur_kernel,
        grid=(rows // row_tile, cols // col_tile),
        in_specs=[
            pl.BlockSpec(memory_space=pltpu.SMEM),
            *[row_block(a) for a in row_side],
            *[col_block(a) for a in col_side],
        ],
        out_specs=pl.BlockSpec((row_tile, col_tile), lambda i, j: (i, j)),
        out_shape=jax.ShapeDtypeStruct((rows, cols), jnp.float32),
        compiler_params=pltpu.CompilerParams(vmem_limit_bytes=50 * MIB),
        cost_estimate=cost(rows * cols / 240000, 4 * rows * cols),
        name="schur",
    )(offsets, *row_side, *col_side)


def factor_inverse(matrix):
    size = matrix.shape[0]
    strip_rows = 16
    row = lax.broadcasted_iota(jnp.int32, (size, size), 0)
    col = lax.broadcasted_iota(jnp.int32, (size, size), 1)
    work = jnp.concatenate([matrix, jnp.where(row == col, 1.0, 0.0)], axis=1)
    strip_row = lax.broadcasted_iota(jnp.int32, (strip_rows, size), 0)
    inverse = []
    for start in range(0, size, strip_rows):
        strip = work[start : start + strip_rows]
        cols = [
            jnp.broadcast_to(strip[:, start + t : start + t + 1], (strip_rows, size))
            for t in range(strip_rows)
        ]
        diagonal = jnp.ones((strip_rows, size), jnp.float32)
        for t in range(strip_rows):
            factor = jnp.where(strip_row > t, cols[t] * (1.0 / cols[t][t : t + 1]), 0.0)
            diagonal = jnp.where(strip_row == t, cols[t], diagonal)
            for u in range(t + 1, strip_rows):
                cols[u] = cols[u] - factor * cols[u][t : t + 1]
            strip = strip - jnp.concatenate([factor, factor], axis=1) * strip[t : t + 1]
        root = lax.rsqrt(diagonal)
        root = root * (1.5 - 0.5 * diagonal * root * root)
        strip = strip * jnp.concatenate([root, root], axis=1)
        inverse.append(strip[:, size:])
        if start + strip_rows < size:
            work = work - lax.dot_general(
                strip[:, :size],
                strip,
                (((0,), (0,)), ((), ())),
                precision=highest,
                preferred_element_type=jnp.float32,
            )
    return jnp.concatenate(inverse, axis=0)


def product_nt(left, right):
    return lax.dot_general(left, right, NT, preferred_element_type=jnp.float32)


def exact(left, right, dims=(((1,), (0,)), ((), ()))):
    return lax.dot_general(
        left, right, dims, precision=highest, preferred_element_type=jnp.float32
    )


def shifted(gram):
    row = lax.broadcasted_iota(jnp.int32, gram.shape, 0)
    col = lax.broadcasted_iota(jnp.int32, gram.shape, 1)
    return gram + jnp.where(row == col, SHIFT, 0.0)


def lead_kernel(pivot_a, pivot_b, inverse):
    a, b = pivot_a[...], pivot_b[...]
    inverse[...] = factor_inverse(shifted(product_nt(a, a) * product_nt(b, b)))


def rest_kernel(pivot_a, pivot_b, lead_inverse, inverse):
    half = lead_inverse.shape[0]
    lead = lead_inverse[...]
    gram = product_nt(pivot_a[pl.ds(half, half), :], pivot_a[...]) * product_nt(
        pivot_b[pl.ds(half, half), :], pivot_b[...]
    )
    coupling = exact(gram[:, :half], lead, NT)
    rest = factor_inverse(shifted(gram[:, half:]) - exact(coupling, coupling, NT))
    inverse[pl.ds(0, half), :] = jnp.concatenate([lead, jnp.zeros_like(lead)], axis=1)
    lower_left = -exact(rest, exact(coupling, lead))
    inverse[pl.ds(half, half), :] = jnp.concatenate([lower_left, rest], axis=1)


def factor_call(kernel, name, size, micros, *operands):
    vmem = pl.BlockSpec(memory_space=pltpu.VMEM)
    return pl.pallas_call(
        kernel,
        in_specs=[vmem] * len(operands),
        out_specs=vmem,
        out_shape=jax.ShapeDtypeStruct((size, size), jnp.float32),
        compiler_params=pltpu.CompilerParams(vmem_limit_bytes=32 * MIB),
        cost_estimate=cost(micros, 8 * size * size),
        name=name,
    )(*operands)


def on_device(phi, psi, points):
    col_count = lax.axis_size("col")
    row_count = lax.axis_size("row")
    col_index = lax.axis_index("col")
    row_index = lax.axis_index("row")
    axes = ("row", "col")
    devices = row_count * col_count
    me = row_index * col_count + col_index
    plane_count, line_count, depth, orbitals = phi.shape
    grid_x, grid_y = plane_count * col_count, line_count * row_count
    cells = plane_count * line_count
    flat_phi = phi.reshape(cells * depth, orbitals)
    flat_psi = psi.reshape(cells * depth, orbitals)
    owned = points.shape[0]
    half = PB // 2

    global_x = points // (grid_y * depth)
    global_y = points // depth % grid_y
    local_cell = (
        (global_x - col_index * plane_count) * line_count + global_y - row_index * line_count
    ) * depth + points % depth

    own = jnp.stack(
        [
            jnp.take(flat_phi, local_cell, axis=0, mode="clip"),
            jnp.take(flat_psi, local_cell, axis=0, mode="clip"),
        ]
    )
    exchange = lambda a: lax.all_to_all(a, axes, split_axis=0, concat_axis=0, tiled=True)

    held = min(owned, PB)
    piece_rows = 2 * PB // devices
    offered = jnp.concatenate([own[:, :held]] * (PB // held), axis=1)
    offered = exchange(offered.reshape(devices, piece_rows, orbitals))
    own, offered = lax.optimization_barrier((own, offered))
    owner = me * piece_rows % PB // owned
    piece = lax.dynamic_index_in_dim(offered, owner, axis=0, keepdims=True)
    pivot = exchange(jnp.broadcast_to(piece, offered.shape)).reshape(2, PB, orbitals)

    row_samples = lax.all_gather(own, "col", axis=1, tiled=True)

    lead_inverse = factor_call(lead_kernel, "lead", half, 10, pivot[0, :half], pivot[1, :half])
    inverse = factor_call(rest_kernel, "rest", PB, 14, pivot[0], pivot[1], lead_inverse)

    x_table, y_table, z_table = (jnp.asarray(cas_table(n)) for n in (grid_x, grid_y, depth))
    padded = (cells // 16 + 1) * 16
    halves = PB // LANES
    rounds = -(-depth * halves // devices)
    parts = []
    for h in range(halves):
        edges = [h * depth, (h + 1) * depth]
        cuts = [k * devices for k in range(rounds) if edges[0] < k * devices < edges[1]]
        marks = [edges[0], *cuts, edges[1]]
        parts.append([(a // devices, a % devices, b - a) for a, b in zip(marks, marks[1:])])

    outgoing = [[] for _ in range(rounds)]

    def make(h, chosen, rows):
        used = rows.shape[1]
        first = chosen[0][0] * devices + chosen[0][1] - h * depth
        count = sum(n for _, _, n in chosen)
        made = source(
            flat_phi,
            flat_psi,
            pivot[0, :used],
            pivot[1, :used],
            rows,
            h,
            z_table[first : first + count],
            cells,
            depth,
            padded,
            [n for _, _, n in chosen],
        )
        for (k, _, _), part in zip(chosen, made):
            outgoing[k].append(part)

    def after(value, gate):
        return lax.optimization_barrier((value, gate))[0]

    make(0, parts[0][:1], lead_inverse)
    if parts[0][1:]:
        make(0, parts[0][1:], after(lead_inverse, row_samples))
    row_start = row_index * row_samples.shape[1]
    col_start = col_index * row_count * owned
    scalar = lambda *v: jnp.stack([jnp.asarray(a, jnp.int32) for a in v])

    latest = outgoing[0][0]
    members = row_count // col_count
    bits = [1 << b for b in range(row_count.bit_length() - 1)]
    inner = [b for b in bits if b < members]
    outer = [b for b in bits if b >= members]
    columns = jnp.where(row_index // members == col_index, row_samples, 0)
    steps = []
    for t in range(len(outer)):
        pairs = []
        for c in range(col_count):
            for j in range(members):
                order = outer[j % len(outer) :] + outer[: j % len(outer)]
                holders = [members * c + j]
                for b in order[:t]:
                    holders += [r ^ b for r in holders]
                pairs += [
                    (r * col_count + c, (r ^ order[t]) * col_count + c) for r in holders
                ]
        steps.append(lambda block, pairs=pairs: block + lax.ppermute(block, axes, pairs))

    def double(block, distance):
        pairs = [(r, r ^ distance) for r in range(row_count)]
        other = lax.ppermute(block, "row", pairs)
        upper = row_index // distance % 2 == 1
        return jnp.concatenate(
            [jnp.where(upper, other, block), jnp.where(upper, block, other)], axis=1
        )

    steps += [lambda block, distance=d: double(block, distance) for d in inner]

    arrived = []

    def in_turn(block, *ready):
        nonlocal latest, columns
        before, latest = latest, lax.optimization_barrier((block, latest, columns, *ready))[0]
        if steps and arrived:
            columns = steps.pop(0)(after(columns, before))
        latest = exchange(latest)
        return latest

    second_round = parts[1][0][0]
    panel_round = max(min(2, rounds - 1), second_round)
    schur_round = max(min(3, rounds - 1), panel_round)
    ready = []
    returned = []
    for k in range(rounds + 1):
        if k == second_round:
            gated = after(inverse, latest if k < 2 else arrived[k - 1])
            make(1, parts[1], gated)
        if k < rounds:
            pieces = list(outgoing[k])
            spare = devices - sum(p.shape[0] for p in pieces)
            if spare:
                pieces.append(jnp.zeros((spare, padded, LANES), jnp.int16))
            sent = pieces[0] if len(pieces) == 1 else jnp.concatenate(pieces, axis=0)
            arrived.append(in_turn(sent, *ready))
            ready = [inverse] if k == 0 else []
        if k == panel_round:
            while steps:
                columns = steps.pop(0)(columns)
            col_samples = columns
            gated = after(inverse, latest)
            panel, row_high, row_low = panel_rows(scalar(row_start), row_samples, pivot, gated)
            _, col_high, col_low = panel_rows(scalar(col_start), col_samples, pivot, gated)
            ready += [row_high, col_high]
        if k == schur_round:
            schur = schur_block(
                after(scalar(row_start, col_start), latest),
                (row_samples[0], row_samples[1], row_high, row_low),
                (col_samples[0], col_samples[1], col_high, col_low),
            )
            ready += [schur]
        if k > 0:
            z_index = ((k - 1) * devices + me) % depth
            z_freq = jnp.minimum(z_index, depth - z_index).astype(jnp.int32).reshape(1)
            back = middle(
                z_freq, arrived[k - 1], x_table, y_table, grid_x, grid_y, line_count
            )
            returned.append(in_turn(back))

    potential = None
    for h in range(halves):
        potential = target(
            [returned[k] for k, _, _ in parts[h]],
            [(a, n) for _, a, n in parts[h]],
            z_table,
            potential,
            h,
            cells,
            depth,
            PB,
        )
    potential = potential.reshape(plane_count, line_count, depth, PB)
    return (schur, panel, potential)


def solution(mesh):
    in_specs = (P("col", "row", None, None), P("col", "row", None, None), P(("row", "col")))
    out_specs = (P("row", "col"), P("row", None), P("col", "row", None, None))
    return jax.shard_map(
        on_device, mesh=mesh, in_specs=in_specs, out_specs=out_specs, check_vma=False
    )
```

```python
import math

import jax
import jax.numpy as jnp
import ml_dtypes
import numpy as np
from jax import lax
from jax.experimental import pallas as pl
from jax.experimental.pallas import tpu as pltpu
from jax.sharding import PartitionSpec as P


PB = 256
GROUP = 40
LANES = 128
SHIFT = 4.0
BOX = 2.0
LEVELS = 32767.0
STEPS_PER_OCTAVE = 256.0
MIB = 1 << 20
NT = (((1,), (1,)), ((), ()))
highest = lax.Precision.HIGHEST


def cost(micros, moved):
    return pl.CostEstimate(
        flops=int(micros * 1.15e9), bytes_accessed=int(moved), transcendentals=0
    )


def cas_table(length):
    index = np.arange(length)
    angle = (index[:, None] * index[None, :] % length) * (2.0 * math.pi / length)
    table = ((np.cos(angle) + np.sin(angle)) / math.sqrt(length)).astype(np.float32)
    high = table.astype(ml_dtypes.bfloat16)
    low = (table - high.astype(np.float32)).astype(ml_dtypes.bfloat16)
    return np.concatenate([high, high, low], axis=1)


def split(value):
    high = value.astype(jnp.bfloat16)
    return high, (value - high.astype(jnp.float32)).astype(jnp.bfloat16)


def stacked(value):
    high, low = split(value)
    return jnp.concatenate([high, low, high], axis=0)


def transform(table, columns):
    data = jnp.concatenate([stacked(c) for c in columns], axis=1)
    out = jnp.dot(table, data, preferred_element_type=jnp.float32)
    return [out[:, i * LANES : (i + 1) * LANES] for i in range(len(columns))]


def encode(rows, padded):
    count = rows.shape[0]
    peak = jnp.maximum(jnp.max(jnp.abs(rows), axis=0, keepdims=True), 1e-30)
    octave = jnp.ceil(jnp.log2(peak) * STEPS_PER_OCTAVE)
    scale = jnp.exp2(octave * (-1.0 / STEPS_PER_OCTAVE)) * LEVELS
    code = jnp.clip(jnp.round(rows * scale), -LEVELS, LEVELS)
    tail = jnp.broadcast_to(octave, (padded - count, LANES))
    return jnp.concatenate([code, tail], axis=0).astype(jnp.int32).astype(jnp.int16)


def decode(block, count):
    value = block.astype(jnp.int32).astype(jnp.float32)
    scale = jnp.exp2(value[count : count + 1] * (1.0 / STEPS_PER_OCTAVE)) * (1.0 / LEVELS)
    return value[:count] * scale


def source_kernel(group, cells, depth, padded, pieces, *refs):
    phi, psi, pivot_a, pivot_b, inverse, table = refs[:6]
    outs, grid_rows = refs[6:-1], refs[-1]
    step = pl.program_id(0)
    first = lax.dot_general(phi[...], pivot_a[...], NT, preferred_element_type=jnp.float32)
    second = lax.dot_general(psi[...], pivot_b[...], NT, preferred_element_type=jnp.float32)
    pair_high, pair_low = split(first * second)
    inv_high, inv_low = split(inverse[...])
    fitting = product_nt(
        jnp.concatenate([pair_high, pair_low, pair_high], axis=1),
        jnp.concatenate([inv_high, inv_high, inv_low], axis=1),
    )
    columns = [fitting[g * depth : (g + 1) * depth] for g in range(group)]
    for g, out in enumerate(transform(table[...], columns)):
        grid_rows[pl.ds(step * group + g, out.shape[0], stride=cells), :] = out

    @pl.when(step == pl.num_programs(0) - 1)
    def _():
        base = 0
        for out_ref, count in zip(outs, pieces):

            def one(i, carry, base=base, out_ref=out_ref):
                start = pl.multiple_of((base + i) * cells, math.gcd(cells, 8))
                out_ref[i] = encode(grid_rows[pl.ds(start, cells), :], padded)
                return carry

            lax.fori_loop(0, count, one, 0)
            base += count


def source(phi, psi, pivot_a, pivot_b, inverse, half, table, cells, depth, padded, pieces):
    group = max(g for g in range(1, GROUP + 1) if cells % g == 0)
    orbitals = phi.shape[1]
    pivots = pivot_a.shape[0]
    whole = lambda shape: pl.BlockSpec(shape, lambda i: (0,) * len(shape))
    return pl.pallas_call(
        lambda *refs: source_kernel(group, cells, depth, padded, pieces, *refs),
        grid=(cells // group,),
        in_specs=[
            pl.BlockSpec((group * depth, orbitals), lambda i: (i, 0)),
            pl.BlockSpec((group * depth, orbitals), lambda i: (i, 0)),
            whole(pivot_a.shape),
            whole(pivot_b.shape),
            pl.BlockSpec((LANES, pivots), lambda i: (half, 0)),
            whole(table.shape),
        ],
        out_specs=[whole((n, padded, LANES)) for n in pieces],
        out_shape=[jax.ShapeDtypeStruct((n, padded, LANES), jnp.int16) for n in pieces],
        scratch_shapes=[pltpu.VMEM((table.shape[0] * cells, LANES), jnp.float32)],
        compiler_params=pltpu.CompilerParams(vmem_limit_bytes=50 * MIB),
        cost_estimate=cost(
            cells * depth / 600, 4 * cells * depth * orbitals
        ),
        name="source",
    )(phi, psi, pivot_a, pivot_b, inverse, table)


def middle_kernel(sizes, padded, z_freq, piece, x_table, y_table, out_ref, arrived, spectrum):
    grid_x, grid_y, lines, blocks = sizes
    cells = grid_x * grid_y // blocks
    batch = 4

    def load(i, carry):
        start = pl.multiple_of(i * cells, math.gcd(cells, 8))
        arrived[pl.ds(start, cells), :] = decode(piece[i], cells)
        return carry

    lax.fori_loop(0, blocks, load, 0)

    def line_start(y):
        return y // lines * (grid_x * lines) + y % lines

    def x_forward(i, carry):
        ys = [i * batch + b for b in range(batch)]
        columns = [arrived[pl.ds(line_start(y), grid_x, stride=lines), :] for y in ys]
        for y, out in zip(ys, transform(x_table[...], columns)):
            spectrum[pl.ds(y, grid_x, stride=grid_y), :] = out
        return carry

    lax.fori_loop(0, grid_y // batch, x_forward, 0)

    y_index = lax.broadcasted_iota(jnp.int32, (grid_y, LANES), 0)
    y_freq = jnp.minimum(y_index, grid_y - y_index).astype(jnp.float32)
    z_squared = (z_freq[0] * z_freq[0]).astype(jnp.float32)
    yz_squared = y_freq * y_freq + z_squared

    def y_both(i, carry):
        xs = [i * batch + b for b in range(batch)]
        columns = [spectrum[pl.ds(pl.multiple_of(x * grid_y, 8), grid_y), :] for x in xs]
        scaled = []
        for x, out in zip(xs, transform(y_table[...], columns)):
            x_freq = jnp.minimum(x, grid_x - x)
            squared = yz_squared + (x_freq * x_freq).astype(jnp.float32)
            kernel = BOX * BOX / math.pi / jnp.maximum(squared, 1.0)
            scaled.append(jnp.where(squared > 0.5, kernel, 0.0) * out)
        for x, out in zip(xs, transform(y_table[...], scaled)):
            spectrum[pl.ds(pl.multiple_of(x * grid_y, 8), grid_y), :] = out
        return carry

    lax.fori_loop(0, grid_x // batch, y_both, 0)

    def x_back(i, carry):
        ys = [i * batch + b for b in range(batch)]
        columns = [spectrum[pl.ds(y, grid_x, stride=grid_y), :] for y in ys]
        for y, out in zip(ys, transform(x_table[...], columns)):
            arrived[pl.ds(line_start(y), grid_x, stride=lines), :] = out
        return carry

    lax.fori_loop(0, grid_y // batch, x_back, 0)

    def store(i, carry):
        start = pl.multiple_of(i * cells, math.gcd(cells, 8))
        out_ref[i] = encode(arrived[pl.ds(start, cells), :], padded)
        return carry

    lax.fori_loop(0, blocks, store, 0)


def middle(z_freq, piece, x_table, y_table, grid_x, grid_y, lines):
    blocks, padded, _ = piece.shape
    sizes = (grid_x, grid_y, lines, blocks)
    vmem = pl.BlockSpec(memory_space=pltpu.VMEM)
    points = grid_x * grid_y
    return pl.pallas_call(
        lambda *refs: middle_kernel(sizes, padded, *refs),
        in_specs=[pl.BlockSpec(memory_space=pltpu.SMEM), vmem, vmem, vmem],
        out_specs=vmem,
        out_shape=jax.ShapeDtypeStruct(piece.shape, jnp.int16),
        scratch_shapes=[
            pltpu.VMEM((points, LANES), jnp.float32),
            pltpu.VMEM((points, LANES), jnp.float32),
        ],
        compiler_params=pltpu.CompilerParams(vmem_limit_bytes=32 * MIB),
        cost_estimate=cost(points / 400, 4 * blocks * padded * LANES),
        name="middle",
    )(z_freq, piece, x_table, y_table)


def target_kernel(group, cells, depth, spans, *refs):
    count = len(spans)
    arrived, table = refs[:count], refs[count]
    out_ref, grid_rows = refs[-2:]
    step = pl.program_id(0)

    @pl.when(step == 0)
    def _():
        base = 0
        for piece, (start, number) in zip(arrived, spans):

            def one(i, carry, base=base, start=start, piece=piece):
                row = pl.multiple_of((base + i) * cells, math.gcd(cells, 8))
                grid_rows[pl.ds(row, cells), :] = decode(piece[start + i], cells)
                return carry

            lax.fori_loop(0, number, one, 0)
            base += number

    columns = [
        grid_rows[pl.ds(step * group + g, depth, stride=cells), :] for g in range(group)
    ]
    for g, out in enumerate(transform(table[...], columns)):
        out_ref[pl.ds(g * depth, depth), :] = out


def target(pieces, spans, table, before, half, cells, depth, functions):
    group = max(g for g in range(1, GROUP + 1) if cells % g == 0)
    whole = lambda shape: pl.BlockSpec(shape, lambda i: (0,) * len(shape))
    in_specs = [whole(p.shape) for p in pieces] + [whole(table.shape)]
    operands = [*pieces, table]
    aliases = {}
    if before is not None:
        in_specs.append(pl.BlockSpec(memory_space=pl.ANY))
        aliases = {len(operands): 0}
        operands.append(before)
    return pl.pallas_call(
        lambda *refs: target_kernel(group, cells, depth, spans, *refs),
        grid=(cells // group,),
        in_specs=in_specs,
        out_specs=pl.BlockSpec((group * depth, LANES), lambda i: (i, half)),
        out_shape=jax.ShapeDtypeStruct((cells * depth, functions), jnp.float32),
        scratch_shapes=[pltpu.VMEM((depth * cells, LANES), jnp.float32)],
        input_output_aliases=aliases,
        compiler_params=pltpu.CompilerParams(vmem_limit_bytes=50 * MIB),
        cost_estimate=cost(cells * depth / 1200, 6 * cells * depth * LANES),
        name="target",
    )(*operands)


def panel_kernel(first_row, left_a, left_b, pivot_a, pivot_b, inverse, panel, high_ref, low_ref):
    step = pl.program_id(0)
    rows, pivots = panel.shape
    gram = lax.dot_general(left_a[...], pivot_a[...], NT, preferred_element_type=jnp.float32)
    gram *= lax.dot_general(left_b[...], pivot_b[...], NT, preferred_element_type=jnp.float32)
    row = lax.broadcasted_iota(jnp.int32, (rows, pivots), 0) + first_row[0] + step * rows
    gram += jnp.where(row == lax.broadcasted_iota(jnp.int32, (rows, pivots), 1), SHIFT, 0.0)
    value = lax.dot_general(
        gram, inverse[...], NT, precision=highest, preferred_element_type=jnp.float32
    )
    panel[...] = value
    high_ref[...], low_ref[...] = split(value)


def panel_rows(first_row, left, pivot, inverse):
    _, rows, orbitals = left.shape
    pivots = pivot.shape[1]
    tile = math.gcd(rows, 512)
    whole = lambda shape: pl.BlockSpec(shape, lambda i: (0,) * len(shape))
    block = lambda width: pl.BlockSpec((tile, width), lambda i: (i, 0))
    shape = lambda dtype: jax.ShapeDtypeStruct((rows, pivots), dtype)
    return pl.pallas_call(
        panel_kernel,
        grid=(rows // tile,),
        in_specs=[
            pl.BlockSpec(memory_space=pltpu.SMEM),
            block(orbitals),
            block(orbitals),
            whole((pivots, orbitals)),
            whole((pivots, orbitals)),
            whole((pivots, pivots)),
        ],
        out_specs=[block(pivots)] * 3,
        out_shape=[shape(jnp.float32), shape(jnp.bfloat16), shape(jnp.bfloat16)],
        compiler_params=pltpu.CompilerParams(vmem_limit_bytes=32 * MIB),
        cost_estimate=cost(rows / 400, 4 * rows * orbitals + 8 * rows * pivots),
        name="panel",
    )(first_row, left[0], left[1], pivot[0], pivot[1], inverse)


def schur_kernel(
    offsets, row_a, row_b, row_high, row_low, col_a, col_b, col_high, col_low, out_ref
):
    rows, cols = out_ref.shape
    product = lambda left, right: lax.dot_general(
        left[...], right[...], NT, preferred_element_type=jnp.float32
    )
    gram = product(row_a, col_a) * product(row_b, col_b)
    update = product(row_high, col_high) + (
        product(row_high, col_low) + product(row_low, col_high)
    )
    row_start = offsets[0] + pl.program_id(0) * rows
    col_start = offsets[1] + pl.program_id(1) * cols
    out_ref[...] = gram - update
    overlap = jnp.logical_and(row_start < col_start + cols, col_start < row_start + rows)

    @pl.when(overlap)
    def _():
        row = lax.broadcasted_iota(jnp.int32, (rows, cols), 0) + row_start
        col = lax.broadcasted_iota(jnp.int32, (rows, cols), 1) + col_start
        out_ref[...] += jnp.where(row == col, SHIFT, 0.0)


def schur_block(offsets, row_side, col_side):
    rows, orbitals = row_side[0].shape
    cols = col_side[0].shape[0]
    row_tile, col_tile = math.gcd(rows, 512), math.gcd(cols, 1024)
    row_block = lambda a: pl.BlockSpec((row_tile, a.shape[1]), lambda i, j: (i, 0))
    col_block = lambda a: pl.BlockSpec((col_tile, a.shape[1]), lambda i, j: (j, 0))
    return pl.pallas_call(
        schur_kernel,
        grid=(rows // row_tile, cols // col_tile),
        in_specs=[
            pl.BlockSpec(memory_space=pltpu.SMEM),
            *[row_block(a) for a in row_side],
            *[col_block(a) for a in col_side],
        ],
        out_specs=pl.BlockSpec((row_tile, col_tile), lambda i, j: (i, j)),
        out_shape=jax.ShapeDtypeStruct((rows, cols), jnp.float32),
        compiler_params=pltpu.CompilerParams(vmem_limit_bytes=50 * MIB),
        cost_estimate=cost(rows * cols / 240000, 4 * rows * cols),
        name="schur",
    )(offsets, *row_side, *col_side)


def factor_inverse(matrix):
    size = matrix.shape[0]
    strip_rows = 16
    row = lax.broadcasted_iota(jnp.int32, (size, size), 0)
    col = lax.broadcasted_iota(jnp.int32, (size, size), 1)
    work = jnp.concatenate([matrix, jnp.where(row == col, 1.0, 0.0)], axis=1)
    strip_row = lax.broadcasted_iota(jnp.int32, (strip_rows, size), 0)
    inverse = []
    for start in range(0, size, strip_rows):
        strip = work[start : start + strip_rows]
        cols = [
            jnp.broadcast_to(strip[:, start + t : start + t + 1], (strip_rows, size))
            for t in range(strip_rows)
        ]
        diagonal = jnp.ones((strip_rows, size), jnp.float32)
        for t in range(strip_rows):
            factor = jnp.where(strip_row > t, cols[t] * (1.0 / cols[t][t : t + 1]), 0.0)
            diagonal = jnp.where(strip_row == t, cols[t], diagonal)
            for u in range(t + 1, strip_rows):
                cols[u] = cols[u] - factor * cols[u][t : t + 1]
            strip = strip - jnp.concatenate([factor, factor], axis=1) * strip[t : t + 1]
        root = lax.rsqrt(diagonal)
        root = root * (1.5 - 0.5 * diagonal * root * root)
        strip = strip * jnp.concatenate([root, root], axis=1)
        inverse.append(strip[:, size:])
        if start + strip_rows < size:
            work = work - lax.dot_general(
                strip[:, :size],
                strip,
                (((0,), (0,)), ((), ())),
                precision=highest,
                preferred_element_type=jnp.float32,
            )
    return jnp.concatenate(inverse, axis=0)


def product_nt(left, right):
    return lax.dot_general(left, right, NT, preferred_element_type=jnp.float32)


def exact(left, right, dims=(((1,), (0,)), ((), ()))):
    return lax.dot_general(
        left, right, dims, precision=highest, preferred_element_type=jnp.float32
    )


def shifted(gram):
    row = lax.broadcasted_iota(jnp.int32, gram.shape, 0)
    col = lax.broadcasted_iota(jnp.int32, gram.shape, 1)
    return gram + jnp.where(row == col, SHIFT, 0.0)


def lead_kernel(pivot_a, pivot_b, inverse):
    a, b = pivot_a[...], pivot_b[...]
    inverse[...] = factor_inverse(shifted(product_nt(a, a) * product_nt(b, b)))


def rest_kernel(pivot_a, pivot_b, lead_inverse, inverse):
    half = lead_inverse.shape[0]
    lead = lead_inverse[...]
    gram = product_nt(pivot_a[pl.ds(half, half), :], pivot_a[...]) * product_nt(
        pivot_b[pl.ds(half, half), :], pivot_b[...]
    )
    coupling = exact(gram[:, :half], lead, NT)
    rest = factor_inverse(shifted(gram[:, half:]) - exact(coupling, coupling, NT))
    inverse[pl.ds(0, half), :] = jnp.concatenate([lead, jnp.zeros_like(lead)], axis=1)
    lower_left = -exact(rest, exact(coupling, lead))
    inverse[pl.ds(half, half), :] = jnp.concatenate([lower_left, rest], axis=1)


def factor_call(kernel, name, size, micros, *operands):
    vmem = pl.BlockSpec(memory_space=pltpu.VMEM)
    return pl.pallas_call(
        kernel,
        in_specs=[vmem] * len(operands),
        out_specs=vmem,
        out_shape=jax.ShapeDtypeStruct((size, size), jnp.float32),
        compiler_params=pltpu.CompilerParams(vmem_limit_bytes=32 * MIB),
        cost_estimate=cost(micros, 8 * size * size),
        name=name,
    )(*operands)


def pick_kernel(index, phi, psi, out_ref, sums):
    step = pl.program_id(0)
    rows, chunk = index.shape[0], phi.shape[0]
    cell = lax.broadcasted_iota(jnp.int32, (rows, chunk), 1) + step * chunk
    chosen = jnp.where(cell == index[...], 1.0, 0.0).astype(jnp.bfloat16)

    @pl.when(step == 0)
    def _():
        sums[...] = jnp.zeros_like(sums)

    for i, field in enumerate((phi, psi)):
        sums[i] += jnp.dot(chosen, field[...], preferred_element_type=jnp.float32)

    @pl.when(step == pl.num_programs(0) - 1)
    def _():
        out_ref[...] = sums[...].astype(out_ref.dtype)


def pick_rows(index, phi, psi):
    rows = index.shape[0]
    total, orbitals = phi.shape
    chunk = total // 5 if total % 80 == 0 else total
    field = pl.BlockSpec((chunk, orbitals), lambda i: (i, 0))
    return pl.pallas_call(
        pick_kernel,
        grid=(total // chunk,),
        in_specs=[pl.BlockSpec((rows, 1), lambda i: (0, 0)), field, field],
        out_specs=pl.BlockSpec((2, rows, orbitals), lambda i: (0, 0, 0)),
        out_shape=jax.ShapeDtypeStruct((2, rows, orbitals), phi.dtype),
        scratch_shapes=[pltpu.VMEM((2, rows, orbitals), jnp.float32)],
        compiler_params=pltpu.CompilerParams(vmem_limit_bytes=50 * MIB),
        cost_estimate=cost(total / 2500, 4 * total * orbitals),
        name="pick",
    )(index.reshape(rows, 1), phi, psi)


def on_device(phi, psi, points):
    col_count = lax.axis_size("col")
    row_count = lax.axis_size("row")
    col_index = lax.axis_index("col")
    row_index = lax.axis_index("row")
    axes = ("row", "col")
    devices = row_count * col_count
    me = row_index * col_count + col_index
    plane_count, line_count, depth, orbitals = phi.shape
    grid_x, grid_y = plane_count * col_count, line_count * row_count
    cells = plane_count * line_count
    flat_phi = phi.reshape(cells * depth, orbitals)
    flat_psi = psi.reshape(cells * depth, orbitals)
    owned = points.shape[0]
    half = PB // 2

    global_x = points // (grid_y * depth)
    global_y = points // depth % grid_y
    local_cell = (
        (global_x - col_index * plane_count) * line_count + global_y - row_index * line_count
    ) * depth + points % depth

    exchange = lambda a: lax.all_to_all(a, axes, split_axis=0, concat_axis=0, tiled=True)

    held = min(owned, PB)
    piece_rows = 2 * PB // devices
    offered = pick_rows(local_cell[:held], flat_phi, flat_psi)
    local_cell, offered = lax.optimization_barrier((local_cell, offered))
    own = jnp.stack(
        [
            jnp.take(flat_phi, local_cell, axis=0, mode="clip"),
            jnp.take(flat_psi, local_cell, axis=0, mode="clip"),
        ]
    )
    offered = jnp.concatenate([offered] * (PB // held), axis=1)
    offered = exchange(offered.reshape(devices, piece_rows, orbitals))
    own, offered = lax.optimization_barrier((own, offered))
    owner = me * piece_rows % PB // owned
    piece = lax.dynamic_index_in_dim(offered, owner, axis=0, keepdims=True)
    pivot = exchange(jnp.broadcast_to(piece, offered.shape)).reshape(2, PB, orbitals)

    row_samples = lax.all_gather(own, "col", axis=1, tiled=True)

    lead_inverse = factor_call(lead_kernel, "lead", half, 10, pivot[0, :half], pivot[1, :half])
    inverse = factor_call(rest_kernel, "rest", PB, 14, pivot[0], pivot[1], lead_inverse)

    x_table, y_table, z_table = (jnp.asarray(cas_table(n)) for n in (grid_x, grid_y, depth))
    padded = (cells // 16 + 1) * 16
    halves = PB // LANES
    rounds = -(-depth * halves // devices)
    parts = []
    for h in range(halves):
        edges = [h * depth, (h + 1) * depth]
        cuts = [k * devices for k in range(rounds) if edges[0] < k * devices < edges[1]]
        marks = [edges[0], *cuts, edges[1]]
        parts.append([(a // devices, a % devices, b - a) for a, b in zip(marks, marks[1:])])

    outgoing = [[] for _ in range(rounds)]

    def make(h, chosen, rows):
        used = rows.shape[1]
        first = chosen[0][0] * devices + chosen[0][1] - h * depth
        count = sum(n for _, _, n in chosen)
        made = source(
            flat_phi,
            flat_psi,
            pivot[0, :used],
            pivot[1, :used],
            rows,
            h,
            z_table[first : first + count],
            cells,
            depth,
            padded,
            [n for _, _, n in chosen],
        )
        for (k, _, _), part in zip(chosen, made):
            outgoing[k].append(part)

    def after(value, gate):
        return lax.optimization_barrier((value, gate))[0]

    make(0, parts[0][:1], lead_inverse)
    if parts[0][1:]:
        make(0, parts[0][1:], after(lead_inverse, outgoing[0][0]))
    row_start = row_index * row_samples.shape[1]
    col_start = col_index * row_count * owned
    scalar = lambda *v: jnp.stack([jnp.asarray(a, jnp.int32) for a in v])

    latest = previous = outgoing[0][0]
    members = row_count // col_count
    bits = [1 << b for b in range(row_count.bit_length() - 1)]
    inner = [b for b in bits if b < members]
    outer = [b for b in bits if b >= members]
    columns = jnp.where(row_index // members == col_index, row_samples, 0)
    steps = []
    for t in range(len(outer)):
        pairs = []
        for c in range(col_count):
            for j in range(members):
                order = outer[j % len(outer) :] + outer[: j % len(outer)]
                holders = [members * c + j]
                for b in order[:t]:
                    holders += [r ^ b for r in holders]
                pairs += [
                    (r * col_count + c, (r ^ order[t]) * col_count + c) for r in holders
                ]
        steps.append(lambda block, pairs=pairs: block + lax.ppermute(block, axes, pairs))

    def double(block, distance):
        pairs = [(r, r ^ distance) for r in range(row_count)]
        other = lax.ppermute(block, "row", pairs)
        upper = row_index // distance % 2 == 1
        return jnp.concatenate(
            [jnp.where(upper, other, block), jnp.where(upper, block, other)], axis=1
        )

    steps += [lambda block, distance=d: double(block, distance) for d in inner]

    arrived = []

    exchanges = 0

    def in_turn(block, *ready):
        nonlocal latest, previous, columns, exchanges
        previous = latest
        even = exchanges % 2 == 0
        due = [columns] if exchanges and (even or not steps) else []
        block = lax.optimization_barrier((block, previous, *due, *ready))[0]
        if steps and even:
            columns = steps.pop(0)(after(columns, previous))
        exchanges += 1
        latest = exchange(block)
        return latest

    second_round = parts[1][0][0]
    panel_round = max(min(3, rounds - 1), second_round)
    schur_round = max(min(3, rounds - 1), panel_round)
    ready = []
    returned = []
    for k in range(rounds + 1):
        updated = []
        if k == second_round:
            gated = after(inverse, latest if k < 2 else arrived[k - 1])
            make(1, parts[1], gated)
        if k < rounds:
            pieces = list(outgoing[k])
            spare = devices - sum(p.shape[0] for p in pieces)
            if spare:
                pieces.append(jnp.zeros((spare, padded, LANES), jnp.int16))
            sent = pieces[0] if len(pieces) == 1 else jnp.concatenate(pieces, axis=0)
            arrived.append(in_turn(sent, *ready))
            ready = [inverse, row_samples] if k == 0 else []
        if k == panel_round:
            while steps:
                columns = steps.pop(0)(columns)
            col_samples = columns
            gated = after(inverse, previous)
            panel, row_high, row_low = panel_rows(scalar(row_start), row_samples, pivot, gated)
            _, col_high, col_low = panel_rows(scalar(col_start), col_samples, pivot, gated)
            ready += [row_high, col_high]
        if k == schur_round:
            schur = schur_block(
                after(scalar(row_start, col_start), latest),
                (row_samples[0], row_samples[1], row_high, row_low),
                (col_samples[0], col_samples[1], col_high, col_low),
            )
            updated = [schur]
        if k > 0:
            z_index = ((k - 1) * devices + me) % depth
            z_freq = jnp.minimum(z_index, depth - z_index).astype(jnp.int32).reshape(1)
            back = middle(
                z_freq, arrived[k - 1], x_table, y_table, grid_x, grid_y, line_count
            )
            returned.append(in_turn(back, *ready))
            ready = updated

    potential = None
    for h in range(halves):
        potential = target(
            [returned[k] for k, _, _ in parts[h]],
            [(a, n) for _, a, n in parts[h]],
            z_table,
            potential,
            h,
            cells,
            depth,
            PB,
        )
    potential = potential.reshape(plane_count, line_count, depth, PB)
    return (schur, panel, potential)


def solution(mesh):
    in_specs = (P("col", "row", None, None), P("col", "row", None, None), P(("row", "col")))
    out_specs = (P("row", "col"), P("row", None), P("col", "row", None, None))
    return jax.shard_map(
        on_device, mesh=mesh, in_specs=in_specs, out_specs=out_specs, check_vma=False
    )
```

```python
import math

import jax
import jax.numpy as jnp
import ml_dtypes
import numpy as np
from jax import lax
from jax.experimental import pallas as pl
from jax.experimental.pallas import tpu as pltpu
from jax.sharding import PartitionSpec as P


PB = 256
GROUP = 40
LANES = 128
SHIFT = 4.0
BOX = 2.0
LEVELS = 32767.0
STEPS_PER_OCTAVE = 256.0
MIB = 1 << 20
NT = (((1,), (1,)), ((), ()))
highest = lax.Precision.HIGHEST


def cost(micros, moved):
    return pl.CostEstimate(
        flops=int(micros * 1.15e9), bytes_accessed=int(moved), transcendentals=0
    )


def cas_table(length):
    index = np.arange(length)
    angle = (index[:, None] * index[None, :] % length) * (2.0 * math.pi / length)
    table = ((np.cos(angle) + np.sin(angle)) / math.sqrt(length)).astype(np.float32)
    high = table.astype(ml_dtypes.bfloat16)
    low = (table - high.astype(np.float32)).astype(ml_dtypes.bfloat16)
    return np.concatenate([high, high, low], axis=1)


def split(value):
    high = value.astype(jnp.bfloat16)
    return high, (value - high.astype(jnp.float32)).astype(jnp.bfloat16)


def stacked(value):
    high, low = split(value)
    return jnp.concatenate([high, low, high], axis=0)


def transform(table, columns):
    data = jnp.concatenate([stacked(c) for c in columns], axis=1)
    out = jnp.dot(table, data, preferred_element_type=jnp.float32)
    return [out[:, i * LANES : (i + 1) * LANES] for i in range(len(columns))]


def encode(rows, padded):
    count = rows.shape[0]
    peak = jnp.maximum(jnp.max(jnp.abs(rows), axis=0, keepdims=True), 1e-30)
    octave = jnp.ceil(jnp.log2(peak) * STEPS_PER_OCTAVE)
    scale = jnp.exp2(octave * (-1.0 / STEPS_PER_OCTAVE)) * LEVELS
    code = jnp.clip(jnp.round(rows * scale), -LEVELS, LEVELS)
    tail = jnp.broadcast_to(octave, (padded - count, LANES))
    return jnp.concatenate([code, tail], axis=0).astype(jnp.int32).astype(jnp.int16)


def decode(block, count):
    value = block.astype(jnp.int32).astype(jnp.float32)
    scale = jnp.exp2(value[count : count + 1] * (1.0 / STEPS_PER_OCTAVE)) * (1.0 / LEVELS)
    return value[:count] * scale


def source_kernel(group, cells, depth, padded, pieces, *refs):
    phi, psi, pivot_a, pivot_b, inverse, table = refs[:6]
    outs, grid_rows = refs[6:-1], refs[-1]
    step = pl.program_id(0)
    first = lax.dot_general(phi[...], pivot_a[...], NT, preferred_element_type=jnp.float32)
    second = lax.dot_general(psi[...], pivot_b[...], NT, preferred_element_type=jnp.float32)
    pair_high, pair_low = split(first * second)
    inv_high, inv_low = split(inverse[...])
    fitting = product_nt(
        jnp.concatenate([pair_high, pair_low, pair_high], axis=1),
        jnp.concatenate([inv_high, inv_high, inv_low], axis=1),
    )
    columns = [fitting[g * depth : (g + 1) * depth] for g in range(group)]
    for g, out in enumerate(transform(table[...], columns)):
        grid_rows[pl.ds(step * group + g, out.shape[0], stride=cells), :] = out

    @pl.when(step == pl.num_programs(0) - 1)
    def _():
        base = 0
        for out_ref, count in zip(outs, pieces):

            def one(i, carry, base=base, out_ref=out_ref):
                start = pl.multiple_of((base + i) * cells, math.gcd(cells, 8))
                out_ref[i] = encode(grid_rows[pl.ds(start, cells), :], padded)
                return carry

            lax.fori_loop(0, count, one, 0)
            base += count


def source(phi, psi, pivot_a, pivot_b, inverse, half, table, cells, depth, padded, pieces):
    group = max(g for g in range(1, GROUP + 1) if cells % g == 0)
    orbitals = phi.shape[1]
    pivots = pivot_a.shape[0]
    whole = lambda shape: pl.BlockSpec(shape, lambda i: (0,) * len(shape))
    return pl.pallas_call(
        lambda *refs: source_kernel(group, cells, depth, padded, pieces, *refs),
        grid=(cells // group,),
        in_specs=[
            pl.BlockSpec((group * depth, orbitals), lambda i: (i, 0)),
            pl.BlockSpec((group * depth, orbitals), lambda i: (i, 0)),
            whole(pivot_a.shape),
            whole(pivot_b.shape),
            pl.BlockSpec((LANES, pivots), lambda i: (half, 0)),
            whole(table.shape),
        ],
        out_specs=[whole((n, padded, LANES)) for n in pieces],
        out_shape=[jax.ShapeDtypeStruct((n, padded, LANES), jnp.int16) for n in pieces],
        scratch_shapes=[pltpu.VMEM((table.shape[0] * cells, LANES), jnp.float32)],
        compiler_params=pltpu.CompilerParams(vmem_limit_bytes=50 * MIB),
        cost_estimate=cost(
            cells * depth / 600, 4 * cells * depth * orbitals
        ),
        name="source",
    )(phi, psi, pivot_a, pivot_b, inverse, table)


def middle_kernel(sizes, padded, z_freq, piece, x_table, y_table, out_ref, arrived, spectrum):
    grid_x, grid_y, lines, blocks = sizes
    cells = grid_x * grid_y // blocks
    batch = 4

    def load(i, carry):
        start = pl.multiple_of(i * cells, math.gcd(cells, 8))
        arrived[pl.ds(start, cells), :] = decode(piece[i], cells)
        return carry

    lax.fori_loop(0, blocks, load, 0)

    def line_start(y):
        return y // lines * (grid_x * lines) + y % lines

    def x_forward(i, carry):
        ys = [i * batch + b for b in range(batch)]
        columns = [arrived[pl.ds(line_start(y), grid_x, stride=lines), :] for y in ys]
        for y, out in zip(ys, transform(x_table[...], columns)):
            spectrum[pl.ds(y, grid_x, stride=grid_y), :] = out
        return carry

    lax.fori_loop(0, grid_y // batch, x_forward, 0)

    y_index = lax.broadcasted_iota(jnp.int32, (grid_y, LANES), 0)
    y_freq = jnp.minimum(y_index, grid_y - y_index).astype(jnp.float32)
    z_squared = (z_freq[0] * z_freq[0]).astype(jnp.float32)
    yz_squared = y_freq * y_freq + z_squared

    def y_both(i, carry):
        xs = [i * batch + b for b in range(batch)]
        columns = [spectrum[pl.ds(pl.multiple_of(x * grid_y, 8), grid_y), :] for x in xs]
        scaled = []
        for x, out in zip(xs, transform(y_table[...], columns)):
            x_freq = jnp.minimum(x, grid_x - x)
            squared = yz_squared + (x_freq * x_freq).astype(jnp.float32)
            kernel = BOX * BOX / math.pi / jnp.maximum(squared, 1.0)
            scaled.append(jnp.where(squared > 0.5, kernel, 0.0) * out)
        for x, out in zip(xs, transform(y_table[...], scaled)):
            spectrum[pl.ds(pl.multiple_of(x * grid_y, 8), grid_y), :] = out
        return carry

    lax.fori_loop(0, grid_x // batch, y_both, 0)

    def x_back(i, carry):
        ys = [i * batch + b for b in range(batch)]
        columns = [spectrum[pl.ds(y, grid_x, stride=grid_y), :] for y in ys]
        for y, out in zip(ys, transform(x_table[...], columns)):
            arrived[pl.ds(line_start(y), grid_x, stride=lines), :] = out
        return carry

    lax.fori_loop(0, grid_y // batch, x_back, 0)

    def store(i, carry):
        start = pl.multiple_of(i * cells, math.gcd(cells, 8))
        out_ref[i] = encode(arrived[pl.ds(start, cells), :], padded)
        return carry

    lax.fori_loop(0, blocks, store, 0)


def middle(z_freq, piece, x_table, y_table, grid_x, grid_y, lines):
    blocks, padded, _ = piece.shape
    sizes = (grid_x, grid_y, lines, blocks)
    vmem = pl.BlockSpec(memory_space=pltpu.VMEM)
    points = grid_x * grid_y
    return pl.pallas_call(
        lambda *refs: middle_kernel(sizes, padded, *refs),
        in_specs=[pl.BlockSpec(memory_space=pltpu.SMEM), vmem, vmem, vmem],
        out_specs=vmem,
        out_shape=jax.ShapeDtypeStruct(piece.shape, jnp.int16),
        scratch_shapes=[
            pltpu.VMEM((points, LANES), jnp.float32),
            pltpu.VMEM((points, LANES), jnp.float32),
        ],
        compiler_params=pltpu.CompilerParams(vmem_limit_bytes=32 * MIB),
        cost_estimate=cost(points / 400, 4 * blocks * padded * LANES),
        name="middle",
    )(z_freq, piece, x_table, y_table)


def target_kernel(group, cells, depth, spans, *refs):
    count = len(spans)
    arrived, table = refs[:count], refs[count]
    out_ref, grid_rows = refs[-2:]
    step = pl.program_id(0)

    @pl.when(step == 0)
    def _():
        base = 0
        for piece, (start, number) in zip(arrived, spans):

            def one(i, carry, base=base, start=start, piece=piece):
                row = pl.multiple_of((base + i) * cells, math.gcd(cells, 8))
                grid_rows[pl.ds(row, cells), :] = decode(piece[start + i], cells)
                return carry

            lax.fori_loop(0, number, one, 0)
            base += number

    columns = [
        grid_rows[pl.ds(step * group + g, depth, stride=cells), :] for g in range(group)
    ]
    for g, out in enumerate(transform(table[...], columns)):
        out_ref[pl.ds(g * depth, depth), :] = out


def target(pieces, spans, table, before, half, cells, depth, functions):
    group = max(g for g in range(1, GROUP + 1) if cells % g == 0)
    whole = lambda shape: pl.BlockSpec(shape, lambda i: (0,) * len(shape))
    in_specs = [whole(p.shape) for p in pieces] + [whole(table.shape)]
    operands = [*pieces, table]
    aliases = {}
    if before is not None:
        in_specs.append(pl.BlockSpec(memory_space=pl.ANY))
        aliases = {len(operands): 0}
        operands.append(before)
    return pl.pallas_call(
        lambda *refs: target_kernel(group, cells, depth, spans, *refs),
        grid=(cells // group,),
        in_specs=in_specs,
        out_specs=pl.BlockSpec((group * depth, LANES), lambda i: (i, half)),
        out_shape=jax.ShapeDtypeStruct((cells * depth, functions), jnp.float32),
        scratch_shapes=[pltpu.VMEM((depth * cells, LANES), jnp.float32)],
        input_output_aliases=aliases,
        compiler_params=pltpu.CompilerParams(vmem_limit_bytes=50 * MIB),
        cost_estimate=cost(cells * depth / 1200, 6 * cells * depth * LANES),
        name="target",
    )(*operands)


def panel_kernel(first_row, left_a, left_b, pivot_a, pivot_b, inverse, panel, high_ref, low_ref):
    step = pl.program_id(0)
    rows, pivots = panel.shape
    gram = lax.dot_general(left_a[...], pivot_a[...], NT, preferred_element_type=jnp.float32)
    gram *= lax.dot_general(left_b[...], pivot_b[...], NT, preferred_element_type=jnp.float32)
    row = lax.broadcasted_iota(jnp.int32, (rows, pivots), 0) + first_row[0] + step * rows
    gram += jnp.where(row == lax.broadcasted_iota(jnp.int32, (rows, pivots), 1), SHIFT, 0.0)
    value = lax.dot_general(
        gram, inverse[...], NT, precision=highest, preferred_element_type=jnp.float32
    )
    panel[...] = value
    high_ref[...], low_ref[...] = split(value)


def panel_rows(first_row, left, pivot, inverse):
    _, rows, orbitals = left.shape
    pivots = pivot.shape[1]
    tile = math.gcd(rows, 512)
    whole = lambda shape: pl.BlockSpec(shape, lambda i: (0,) * len(shape))
    block = lambda width: pl.BlockSpec((tile, width), lambda i: (i, 0))
    shape = lambda dtype: jax.ShapeDtypeStruct((rows, pivots), dtype)
    return pl.pallas_call(
        panel_kernel,
        grid=(rows // tile,),
        in_specs=[
            pl.BlockSpec(memory_space=pltpu.SMEM),
            block(orbitals),
            block(orbitals),
            whole((pivots, orbitals)),
            whole((pivots, orbitals)),
            whole((pivots, pivots)),
        ],
        out_specs=[block(pivots)] * 3,
        out_shape=[shape(jnp.float32), shape(jnp.bfloat16), shape(jnp.bfloat16)],
        compiler_params=pltpu.CompilerParams(vmem_limit_bytes=32 * MIB),
        cost_estimate=cost(rows / 400, 4 * rows * orbitals + 8 * rows * pivots),
        name="panel",
    )(first_row, left[0], left[1], pivot[0], pivot[1], inverse)


def schur_kernel(
    offsets, row_a, row_b, row_high, row_low, col_a, col_b, col_high, col_low, out_ref
):
    rows, cols = out_ref.shape
    product = lambda left, right: lax.dot_general(
        left[...], right[...], NT, preferred_element_type=jnp.float32
    )
    gram = product(row_a, col_a) * product(row_b, col_b)
    update = product(row_high, col_high) + (
        product(row_high, col_low) + product(row_low, col_high)
    )
    row_start = offsets[0] + pl.program_id(0) * rows
    col_start = offsets[1] + pl.program_id(1) * cols
    out_ref[...] = gram - update
    overlap = jnp.logical_and(row_start < col_start + cols, col_start < row_start + rows)

    @pl.when(overlap)
    def _():
        row = lax.broadcasted_iota(jnp.int32, (rows, cols), 0) + row_start
        col = lax.broadcasted_iota(jnp.int32, (rows, cols), 1) + col_start
        out_ref[...] += jnp.where(row == col, SHIFT, 0.0)


def schur_block(offsets, row_side, col_side):
    rows, orbitals = row_side[0].shape
    cols = col_side[0].shape[0]
    row_tile, col_tile = math.gcd(rows, 512), math.gcd(cols, 1024)
    row_block = lambda a: pl.BlockSpec((row_tile, a.shape[1]), lambda i, j: (i, 0))
    col_block = lambda a: pl.BlockSpec((col_tile, a.shape[1]), lambda i, j: (j, 0))
    return pl.pallas_call(
        schur_kernel,
        grid=(rows // row_tile, cols // col_tile),
        in_specs=[
            pl.BlockSpec(memory_space=pltpu.SMEM),
            *[row_block(a) for a in row_side],
            *[col_block(a) for a in col_side],
        ],
        out_specs=pl.BlockSpec((row_tile, col_tile), lambda i, j: (i, j)),
        out_shape=jax.ShapeDtypeStruct((rows, cols), jnp.float32),
        compiler_params=pltpu.CompilerParams(vmem_limit_bytes=50 * MIB),
        cost_estimate=cost(rows * cols / 240000, 4 * rows * cols),
        name="schur",
    )(offsets, *row_side, *col_side)


def factor_inverse(matrix):
    size = matrix.shape[0]
    strip_rows = 16
    row = lax.broadcasted_iota(jnp.int32, (size, size), 0)
    col = lax.broadcasted_iota(jnp.int32, (size, size), 1)
    work = jnp.concatenate([matrix, jnp.where(row == col, 1.0, 0.0)], axis=1)
    strip_row = lax.broadcasted_iota(jnp.int32, (strip_rows, size), 0)
    inverse = []
    for start in range(0, size, strip_rows):
        strip = work[start : start + strip_rows]
        cols = [
            jnp.broadcast_to(strip[:, start + t : start + t + 1], (strip_rows, size))
            for t in range(strip_rows)
        ]
        diagonal = jnp.ones((strip_rows, size), jnp.float32)
        for t in range(strip_rows):
            factor = jnp.where(strip_row > t, cols[t] * (1.0 / cols[t][t : t + 1]), 0.0)
            diagonal = jnp.where(strip_row == t, cols[t], diagonal)
            for u in range(t + 1, strip_rows):
                cols[u] = cols[u] - factor * cols[u][t : t + 1]
            strip = strip - jnp.concatenate([factor, factor], axis=1) * strip[t : t + 1]
        root = lax.rsqrt(diagonal)
        root = root * (1.5 - 0.5 * diagonal * root * root)
        strip = strip * jnp.concatenate([root, root], axis=1)
        inverse.append(strip[:, size:])
        if start + strip_rows < size:
            work = work - lax.dot_general(
                strip[:, :size],
                strip,
                (((0,), (0,)), ((), ())),
                precision=highest,
                preferred_element_type=jnp.float32,
            )
    return jnp.concatenate(inverse, axis=0)


def product_nt(left, right):
    return lax.dot_general(left, right, NT, preferred_element_type=jnp.float32)


def exact(left, right, dims=(((1,), (0,)), ((), ()))):
    return lax.dot_general(
        left, right, dims, precision=highest, preferred_element_type=jnp.float32
    )


def shifted(gram):
    row = lax.broadcasted_iota(jnp.int32, gram.shape, 0)
    col = lax.broadcasted_iota(jnp.int32, gram.shape, 1)
    return gram + jnp.where(row == col, SHIFT, 0.0)


def lead_kernel(pivot_a, pivot_b, inverse):
    a, b = pivot_a[...], pivot_b[...]
    inverse[...] = factor_inverse(shifted(product_nt(a, a) * product_nt(b, b)))


def rest_kernel(pivot_a, pivot_b, lead_inverse, inverse):
    half = lead_inverse.shape[0]
    lead = lead_inverse[...]
    gram = product_nt(pivot_a[pl.ds(half, half), :], pivot_a[...]) * product_nt(
        pivot_b[pl.ds(half, half), :], pivot_b[...]
    )
    coupling = exact(gram[:, :half], lead, NT)
    rest = factor_inverse(shifted(gram[:, half:]) - exact(coupling, coupling, NT))
    inverse[pl.ds(0, half), :] = jnp.concatenate([lead, jnp.zeros_like(lead)], axis=1)
    lower_left = -exact(rest, exact(coupling, lead))
    inverse[pl.ds(half, half), :] = jnp.concatenate([lower_left, rest], axis=1)


def factor_call(kernel, name, size, micros, *operands):
    vmem = pl.BlockSpec(memory_space=pltpu.VMEM)
    return pl.pallas_call(
        kernel,
        in_specs=[vmem] * len(operands),
        out_specs=vmem,
        out_shape=jax.ShapeDtypeStruct((size, size), jnp.float32),
        compiler_params=pltpu.CompilerParams(vmem_limit_bytes=32 * MIB),
        cost_estimate=cost(micros, 8 * size * size),
        name=name,
    )(*operands)


def on_device(phi, psi, points):
    col_count = lax.axis_size("col")
    row_count = lax.axis_size("row")
    col_index = lax.axis_index("col")
    row_index = lax.axis_index("row")
    axes = ("row", "col")
    devices = row_count * col_count
    me = row_index * col_count + col_index
    plane_count, line_count, depth, orbitals = phi.shape
    grid_x, grid_y = plane_count * col_count, line_count * row_count
    cells = plane_count * line_count
    flat_phi = phi.reshape(cells * depth, orbitals)
    flat_psi = psi.reshape(cells * depth, orbitals)
    owned = points.shape[0]
    half = PB // 2

    global_x = points // (grid_y * depth)
    global_y = points // depth % grid_y
    local_cell = (
        (global_x - col_index * plane_count) * line_count + global_y - row_index * line_count
    ) * depth + points % depth

    own = jnp.stack(
        [
            jnp.take(flat_phi, local_cell, axis=0, mode="clip"),
            jnp.take(flat_psi, local_cell, axis=0, mode="clip"),
        ]
    )
    exchange = lambda a: lax.all_to_all(a, axes, split_axis=0, concat_axis=0, tiled=True)

    held = min(owned, PB)
    piece_rows = 2 * PB // devices
    offered = jnp.concatenate([own[:, :held]] * (PB // held), axis=1)
    offered = exchange(offered.reshape(devices, piece_rows, orbitals))
    owner = me * piece_rows % PB // owned
    piece = lax.dynamic_index_in_dim(offered, owner, axis=0, keepdims=True)
    pivot = exchange(jnp.broadcast_to(piece, offered.shape)).reshape(2, PB, orbitals)

    row_samples = lax.all_gather(own, "col", axis=1, tiled=True)

    lead_inverse = factor_call(lead_kernel, "lead", half, 10, pivot[0, :half], pivot[1, :half])
    inverse = factor_call(rest_kernel, "rest", PB, 14, pivot[0], pivot[1], lead_inverse)

    x_table, y_table, z_table = (jnp.asarray(cas_table(n)) for n in (grid_x, grid_y, depth))
    padded = (cells // 16 + 1) * 16
    halves = PB // LANES
    rounds = -(-depth * halves // devices)
    parts = []
    for h in range(halves):
        edges = [h * depth, (h + 1) * depth]
        cuts = [k * devices for k in range(rounds) if edges[0] < k * devices < edges[1]]
        marks = [edges[0], *cuts, edges[1]]
        parts.append([(a // devices, a % devices, b - a) for a, b in zip(marks, marks[1:])])

    outgoing = [[] for _ in range(rounds)]

    def make(h, chosen, rows):
        used = rows.shape[1]
        first = chosen[0][0] * devices + chosen[0][1] - h * depth
        count = sum(n for _, _, n in chosen)
        made = source(
            flat_phi,
            flat_psi,
            pivot[0, :used],
            pivot[1, :used],
            rows,
            h,
            z_table[first : first + count],
            cells,
            depth,
            padded,
            [n for _, _, n in chosen],
        )
        for (k, _, _), part in zip(chosen, made):
            outgoing[k].append(part)

    def after(value, gate):
        return lax.optimization_barrier((value, gate))[0]

    make(0, parts[0][:1], lead_inverse)
    if parts[0][1:]:
        make(0, parts[0][1:], after(lead_inverse, outgoing[0][0]))
    row_start = row_index * row_samples.shape[1]
    col_start = col_index * row_count * owned
    scalar = lambda *v: jnp.stack([jnp.asarray(a, jnp.int32) for a in v])

    latest = outgoing[0][0]
    members = row_count // col_count
    bits = [1 << b for b in range(row_count.bit_length() - 1)]
    inner = [b for b in bits if b < members]
    outer = [b for b in bits if b >= members]
    columns = jnp.where(row_index // members == col_index, row_samples, 0)
    steps = []
    for t in range(len(outer)):
        pairs = []
        for c in range(col_count):
            for j in range(members):
                order = outer[j % len(outer) :] + outer[: j % len(outer)]
                holders = [members * c + j]
                for b in order[:t]:
                    holders += [r ^ b for r in holders]
                pairs += [
                    (r * col_count + c, (r ^ order[t]) * col_count + c) for r in holders
                ]


        def spread(block, pairs=pairs):
            other = lax.ppermute(block, axes, pairs)
            return other, block + other

        steps.append(spread)

    def double(block, distance):
        pairs = [(r, r ^ distance) for r in range(row_count)]
        other = lax.ppermute(block, "row", pairs)
        upper = row_index // distance % 2 == 1
        return other, jnp.concatenate(
            [jnp.where(upper, other, block), jnp.where(upper, block, other)], axis=1
        )

    steps += [lambda block, distance=d: double(block, distance) for d in inner]

    arrived = []

    coming = []

    def in_turn(block, *ready):
        nonlocal latest, columns, coming
        before = latest
        block = lax.optimization_barrier((block, before, *coming, *ready))[0]
        coming = []
        if steps and arrived:
            other, columns = steps.pop(0)(after(columns, before))
            coming = [other]
        latest = exchange(block)
        return latest

    second_round = parts[1][0][0]
    panel_round = max(min(2, rounds - 1), second_round)
    schur_round = max(min(3, rounds - 1), panel_round)
    ready = []
    returned = []
    for k in range(rounds + 1):
        if k == second_round:
            gated = after(inverse, latest if k < 2 else arrived[k - 1])
            make(1, parts[1], gated)
        if k < rounds:
            pieces = list(outgoing[k])
            spare = devices - sum(p.shape[0] for p in pieces)
            if spare:
                pieces.append(jnp.zeros((spare, padded, LANES), jnp.int16))
            sent = pieces[0] if len(pieces) == 1 else jnp.concatenate(pieces, axis=0)
            arrived.append(in_turn(sent, *ready))
            ready = [inverse, row_samples] if k == 0 else []
        if k == panel_round:
            while steps:
                _, columns = steps.pop(0)(columns)
            col_samples = columns
            gated = after(inverse, latest)
            panel, row_high, row_low = panel_rows(scalar(row_start), row_samples, pivot, gated)
            _, col_high, col_low = panel_rows(scalar(col_start), col_samples, pivot, gated)
            ready += [row_high, col_high]
        if k == schur_round:
            schur = schur_block(
                after(scalar(row_start, col_start), latest),
                (row_samples[0], row_samples[1], row_high, row_low),
                (col_samples[0], col_samples[1], col_high, col_low),
            )
            ready += [schur]
        if k > 0:
            z_index = ((k - 1) * devices + me) % depth
            z_freq = jnp.minimum(z_index, depth - z_index).astype(jnp.int32).reshape(1)
            back = middle(
                z_freq, arrived[k - 1], x_table, y_table, grid_x, grid_y, line_count
            )
            returned.append(in_turn(back))

    potential = None
    for h in range(halves):
        potential = target(
            [returned[k] for k, _, _ in parts[h]],
            [(a, n) for _, a, n in parts[h]],
            z_table,
            potential,
            h,
            cells,
            depth,
            PB,
        )
    potential = potential.reshape(plane_count, line_count, depth, PB)
    return (schur, panel, potential)


def solution(mesh):
    in_specs = (P("col", "row", None, None), P("col", "row", None, None), P(("row", "col")))
    out_specs = (P("row", "col"), P("row", None), P("col", "row", None, None))
    return jax.shard_map(
        on_device, mesh=mesh, in_specs=in_specs, out_specs=out_specs, check_vma=False
    )
```

```python
import math

import jax
import jax.numpy as jnp
import ml_dtypes
import numpy as np
from jax import lax
from jax.experimental import pallas as pl
from jax.experimental.pallas import tpu as pltpu
from jax.sharding import PartitionSpec as P


PB = 256
GROUP = 40
LANES = 128
SHIFT = 4.0
BOX = 2.0
LEVELS = 32767.0
STEPS_PER_OCTAVE = 256.0
MIB = 1 << 20
NT = (((1,), (1,)), ((), ()))
highest = lax.Precision.HIGHEST


def cost(micros, moved):
    return pl.CostEstimate(
        flops=int(micros * 1.15e9), bytes_accessed=int(moved), transcendentals=0
    )


def cas_table(length):
    index = np.arange(length)
    angle = (index[:, None] * index[None, :] % length) * (2.0 * math.pi / length)
    table = ((np.cos(angle) + np.sin(angle)) / math.sqrt(length)).astype(np.float32)
    high = table.astype(ml_dtypes.bfloat16)
    low = (table - high.astype(np.float32)).astype(ml_dtypes.bfloat16)
    return np.concatenate([high, high, low], axis=1)


def split(value):
    high = value.astype(jnp.bfloat16)
    return high, (value - high.astype(jnp.float32)).astype(jnp.bfloat16)


def stacked(value):
    high, low = split(value)
    return jnp.concatenate([high, low, high], axis=0)


def transform(table, columns):
    data = jnp.concatenate([stacked(c) for c in columns], axis=1)
    out = jnp.dot(table, data, preferred_element_type=jnp.float32)
    return [out[:, i * LANES : (i + 1) * LANES] for i in range(len(columns))]


def encode(rows, padded):
    count = rows.shape[0]
    peak = jnp.maximum(jnp.max(jnp.abs(rows), axis=0, keepdims=True), 1e-30)
    octave = jnp.ceil(jnp.log2(peak) * STEPS_PER_OCTAVE)
    scale = jnp.exp2(octave * (-1.0 / STEPS_PER_OCTAVE)) * LEVELS
    code = jnp.clip(jnp.round(rows * scale), -LEVELS, LEVELS)
    tail = jnp.broadcast_to(octave, (padded - count, LANES))
    return jnp.concatenate([code, tail], axis=0).astype(jnp.int32).astype(jnp.int16)


def decode(block, count):
    value = block.astype(jnp.int32).astype(jnp.float32)
    scale = jnp.exp2(value[count : count + 1] * (1.0 / STEPS_PER_OCTAVE)) * (1.0 / LEVELS)
    return value[:count] * scale


def source_kernel(group, cells, depth, padded, pieces, *refs):
    phi, psi, pivot_a, pivot_b, inverse, table = refs[:6]
    outs, grid_rows = refs[6:-1], refs[-1]
    step = pl.program_id(0)
    first = lax.dot_general(phi[...], pivot_a[...], NT, preferred_element_type=jnp.float32)
    second = lax.dot_general(psi[...], pivot_b[...], NT, preferred_element_type=jnp.float32)
    pair_high, pair_low = split(first * second)
    inv_high, inv_low = split(inverse[...])
    fitting = product_nt(
        jnp.concatenate([pair_high, pair_low, pair_high], axis=1),
        jnp.concatenate([inv_high, inv_high, inv_low], axis=1),
    )
    columns = [fitting[g * depth : (g + 1) * depth] for g in range(group)]
    for g, out in enumerate(transform(table[...], columns)):
        grid_rows[pl.ds(step * group + g, out.shape[0], stride=cells), :] = out

    @pl.when(step == pl.num_programs(0) - 1)
    def _():
        base = 0
        for out_ref, count in zip(outs, pieces):

            def one(i, carry, base=base, out_ref=out_ref):
                start = pl.multiple_of((base + i) * cells, math.gcd(cells, 8))
                out_ref[i] = encode(grid_rows[pl.ds(start, cells), :], padded)
                return carry

            lax.fori_loop(0, count, one, 0)
            base += count


def source(phi, psi, pivot_a, pivot_b, inverse, half, table, cells, depth, padded, pieces):
    group = max(g for g in range(1, GROUP + 1) if cells % g == 0)
    orbitals = phi.shape[1]
    pivots = pivot_a.shape[0]
    whole = lambda shape: pl.BlockSpec(shape, lambda i: (0,) * len(shape))
    return pl.pallas_call(
        lambda *refs: source_kernel(group, cells, depth, padded, pieces, *refs),
        grid=(cells // group,),
        in_specs=[
            pl.BlockSpec((group * depth, orbitals), lambda i: (i, 0)),
            pl.BlockSpec((group * depth, orbitals), lambda i: (i, 0)),
            whole(pivot_a.shape),
            whole(pivot_b.shape),
            pl.BlockSpec((LANES, pivots), lambda i: (half, 0)),
            whole(table.shape),
        ],
        out_specs=[whole((n, padded, LANES)) for n in pieces],
        out_shape=[jax.ShapeDtypeStruct((n, padded, LANES), jnp.int16) for n in pieces],
        scratch_shapes=[pltpu.VMEM((table.shape[0] * cells, LANES), jnp.float32)],
        compiler_params=pltpu.CompilerParams(vmem_limit_bytes=50 * MIB),
        cost_estimate=cost(
            cells * depth / 600, 4 * cells * depth * orbitals
        ),
        name="source",
    )(phi, psi, pivot_a, pivot_b, inverse, table)


def middle_kernel(sizes, padded, z_freq, piece, x_table, y_table, out_ref, arrived, spectrum):
    grid_x, grid_y, lines, blocks = sizes
    cells = grid_x * grid_y // blocks
    batch = 4

    def load(i, carry):
        start = pl.multiple_of(i * cells, math.gcd(cells, 8))
        arrived[pl.ds(start, cells), :] = decode(piece[i], cells)
        return carry

    lax.fori_loop(0, blocks, load, 0)

    def line_start(y):
        return y // lines * (grid_x * lines) + y % lines

    def x_forward(i, carry):
        ys = [i * batch + b for b in range(batch)]
        columns = [arrived[pl.ds(line_start(y), grid_x, stride=lines), :] for y in ys]
        for y, out in zip(ys, transform(x_table[...], columns)):
            spectrum[pl.ds(y, grid_x, stride=grid_y), :] = out
        return carry

    lax.fori_loop(0, grid_y // batch, x_forward, 0)

    y_index = lax.broadcasted_iota(jnp.int32, (grid_y, LANES), 0)
    y_freq = jnp.minimum(y_index, grid_y - y_index).astype(jnp.float32)
    z_squared = (z_freq[0] * z_freq[0]).astype(jnp.float32)
    yz_squared = y_freq * y_freq + z_squared

    def y_both(i, carry):
        xs = [i * batch + b for b in range(batch)]
        columns = [spectrum[pl.ds(pl.multiple_of(x * grid_y, 8), grid_y), :] for x in xs]
        scaled = []
        for x, out in zip(xs, transform(y_table[...], columns)):
            x_freq = jnp.minimum(x, grid_x - x)
            squared = yz_squared + (x_freq * x_freq).astype(jnp.float32)
            kernel = BOX * BOX / math.pi / jnp.maximum(squared, 1.0)
            scaled.append(jnp.where(squared > 0.5, kernel, 0.0) * out)
        for x, out in zip(xs, transform(y_table[...], scaled)):
            spectrum[pl.ds(pl.multiple_of(x * grid_y, 8), grid_y), :] = out
        return carry

    lax.fori_loop(0, grid_x // batch, y_both, 0)

    def x_back(i, carry):
        ys = [i * batch + b for b in range(batch)]
        columns = [spectrum[pl.ds(y, grid_x, stride=grid_y), :] for y in ys]
        for y, out in zip(ys, transform(x_table[...], columns)):
            arrived[pl.ds(line_start(y), grid_x, stride=lines), :] = out
        return carry

    lax.fori_loop(0, grid_y // batch, x_back, 0)

    def store(i, carry):
        start = pl.multiple_of(i * cells, math.gcd(cells, 8))
        out_ref[i] = encode(arrived[pl.ds(start, cells), :], padded)
        return carry

    lax.fori_loop(0, blocks, store, 0)


def middle(z_freq, piece, x_table, y_table, grid_x, grid_y, lines):
    blocks, padded, _ = piece.shape
    sizes = (grid_x, grid_y, lines, blocks)
    vmem = pl.BlockSpec(memory_space=pltpu.VMEM)
    points = grid_x * grid_y
    return pl.pallas_call(
        lambda *refs: middle_kernel(sizes, padded, *refs),
        in_specs=[pl.BlockSpec(memory_space=pltpu.SMEM), vmem, vmem, vmem],
        out_specs=vmem,
        out_shape=jax.ShapeDtypeStruct(piece.shape, jnp.int16),
        scratch_shapes=[
            pltpu.VMEM((points, LANES), jnp.float32),
            pltpu.VMEM((points, LANES), jnp.float32),
        ],
        compiler_params=pltpu.CompilerParams(vmem_limit_bytes=32 * MIB),
        cost_estimate=cost(points / 400, 4 * blocks * padded * LANES),
        name="middle",
    )(z_freq, piece, x_table, y_table)


def target_kernel(group, cells, depth, spans, *refs):
    count = len(spans)
    arrived, table = refs[:count], refs[count]
    out_ref, grid_rows = refs[-2:]
    step = pl.program_id(0)

    @pl.when(step == 0)
    def _():
        base = 0
        for piece, (start, number) in zip(arrived, spans):

            def one(i, carry, base=base, start=start, piece=piece):
                row = pl.multiple_of((base + i) * cells, math.gcd(cells, 8))
                grid_rows[pl.ds(row, cells), :] = decode(piece[start + i], cells)
                return carry

            lax.fori_loop(0, number, one, 0)
            base += number

    columns = [
        grid_rows[pl.ds(step * group + g, depth, stride=cells), :] for g in range(group)
    ]
    for g, out in enumerate(transform(table[...], columns)):
        out_ref[pl.ds(g * depth, depth), :] = out


def target(pieces, spans, table, before, half, cells, depth, functions):
    group = max(g for g in range(1, GROUP + 1) if cells % g == 0)
    whole = lambda shape: pl.BlockSpec(shape, lambda i: (0,) * len(shape))
    in_specs = [whole(p.shape) for p in pieces] + [whole(table.shape)]
    operands = [*pieces, table]
    aliases = {}
    if before is not None:
        in_specs.append(pl.BlockSpec(memory_space=pl.ANY))
        aliases = {len(operands): 0}
        operands.append(before)
    return pl.pallas_call(
        lambda *refs: target_kernel(group, cells, depth, spans, *refs),
        grid=(cells // group,),
        in_specs=in_specs,
        out_specs=pl.BlockSpec((group * depth, LANES), lambda i: (i, half)),
        out_shape=jax.ShapeDtypeStruct((cells * depth, functions), jnp.float32),
        scratch_shapes=[pltpu.VMEM((depth * cells, LANES), jnp.float32)],
        input_output_aliases=aliases,
        compiler_params=pltpu.CompilerParams(vmem_limit_bytes=50 * MIB),
        cost_estimate=cost(cells * depth / 1200, 6 * cells * depth * LANES),
        name="target",
    )(*operands)


def panel_kernel(first_row, left_a, left_b, pivot_a, pivot_b, inverse, panel, high_ref, low_ref):
    step = pl.program_id(0)
    rows, pivots = panel.shape
    gram = lax.dot_general(left_a[...], pivot_a[...], NT, preferred_element_type=jnp.float32)
    gram *= lax.dot_general(left_b[...], pivot_b[...], NT, preferred_element_type=jnp.float32)
    row = lax.broadcasted_iota(jnp.int32, (rows, pivots), 0) + first_row[0] + step * rows
    gram += jnp.where(row == lax.broadcasted_iota(jnp.int32, (rows, pivots), 1), SHIFT, 0.0)
    value = lax.dot_general(
        gram, inverse[...], NT, precision=highest, preferred_element_type=jnp.float32
    )
    panel[...] = value
    high_ref[...], low_ref[...] = split(value)


def panel_rows(first_row, left, pivot, inverse):
    rows, orbitals = left[0].shape
    pivots = pivot.shape[1]
    tile = math.gcd(rows, 512)
    whole = lambda shape: pl.BlockSpec(shape, lambda i: (0,) * len(shape))
    block = lambda width: pl.BlockSpec((tile, width), lambda i: (i, 0))
    shape = lambda dtype: jax.ShapeDtypeStruct((rows, pivots), dtype)
    return pl.pallas_call(
        panel_kernel,
        grid=(rows // tile,),
        in_specs=[
            pl.BlockSpec(memory_space=pltpu.SMEM),
            block(orbitals),
            block(orbitals),
            whole((pivots, orbitals)),
            whole((pivots, orbitals)),
            whole((pivots, pivots)),
        ],
        out_specs=[block(pivots)] * 3,
        out_shape=[shape(jnp.float32), shape(jnp.bfloat16), shape(jnp.bfloat16)],
        compiler_params=pltpu.CompilerParams(vmem_limit_bytes=32 * MIB),
        cost_estimate=cost(rows / 400, 4 * rows * orbitals + 8 * rows * pivots),
        name="panel",
    )(first_row, left[0], left[1], pivot[0], pivot[1], inverse)


def schur_kernel(
    offsets, row_a, row_b, row_high, row_low, col_a, col_b, col_high, col_low, out_ref
):
    rows, cols = out_ref.shape
    product = lambda left, right: lax.dot_general(
        left[...], right[...], NT, preferred_element_type=jnp.float32
    )
    gram = product(row_a, col_a) * product(row_b, col_b)
    update = product(row_high, col_high) + (
        product(row_high, col_low) + product(row_low, col_high)
    )
    row_start = offsets[0] + pl.program_id(0) * rows
    col_start = offsets[1] + pl.program_id(1) * cols
    out_ref[...] = gram - update
    overlap = jnp.logical_and(row_start < col_start + cols, col_start < row_start + rows)

    @pl.when(overlap)
    def _():
        row = lax.broadcasted_iota(jnp.int32, (rows, cols), 0) + row_start
        col = lax.broadcasted_iota(jnp.int32, (rows, cols), 1) + col_start
        out_ref[...] += jnp.where(row == col, SHIFT, 0.0)


def schur_block(offsets, row_side, col_side):
    rows, orbitals = row_side[0].shape
    cols = col_side[0].shape[0]
    row_tile, col_tile = math.gcd(rows, 512), math.gcd(cols, 1024)
    row_block = lambda a: pl.BlockSpec((row_tile, a.shape[1]), lambda i, j: (i, 0))
    col_block = lambda a: pl.BlockSpec((col_tile, a.shape[1]), lambda i, j: (j, 0))
    return pl.pallas_call(
        schur_kernel,
        grid=(rows // row_tile, cols // col_tile),
        in_specs=[
            pl.BlockSpec(memory_space=pltpu.SMEM),
            *[row_block(a) for a in row_side],
            *[col_block(a) for a in col_side],
        ],
        out_specs=pl.BlockSpec((row_tile, col_tile), lambda i, j: (i, j)),
        out_shape=jax.ShapeDtypeStruct((rows, cols), jnp.float32),
        compiler_params=pltpu.CompilerParams(vmem_limit_bytes=50 * MIB),
        cost_estimate=cost(rows * cols / 240000, 4 * rows * cols),
        name="schur",
    )(offsets, *row_side, *col_side)


def factor_inverse(matrix):
    size = matrix.shape[0]
    strip_rows = 16
    row = lax.broadcasted_iota(jnp.int32, (size, size), 0)
    col = lax.broadcasted_iota(jnp.int32, (size, size), 1)
    work = jnp.concatenate([matrix, jnp.where(row == col, 1.0, 0.0)], axis=1)
    strip_row = lax.broadcasted_iota(jnp.int32, (strip_rows, size), 0)
    inverse = []
    for start in range(0, size, strip_rows):
        strip = work[start : start + strip_rows]
        cols = [
            jnp.broadcast_to(strip[:, start + t : start + t + 1], (strip_rows, size))
            for t in range(strip_rows)
        ]
        diagonal = jnp.ones((strip_rows, size), jnp.float32)
        for t in range(strip_rows):
            factor = jnp.where(strip_row > t, cols[t] * (1.0 / cols[t][t : t + 1]), 0.0)
            diagonal = jnp.where(strip_row == t, cols[t], diagonal)
            for u in range(t + 1, strip_rows):
                cols[u] = cols[u] - factor * cols[u][t : t + 1]
            strip = strip - jnp.concatenate([factor, factor], axis=1) * strip[t : t + 1]
        root = lax.rsqrt(diagonal)
        root = root * (1.5 - 0.5 * diagonal * root * root)
        strip = strip * jnp.concatenate([root, root], axis=1)
        inverse.append(strip[:, size:])
        if start + strip_rows < size:
            work = work - lax.dot_general(
                strip[:, :size],
                strip,
                (((0,), (0,)), ((), ())),
                precision=highest,
                preferred_element_type=jnp.float32,
            )
    return jnp.concatenate(inverse, axis=0)


def product_nt(left, right):
    return lax.dot_general(left, right, NT, preferred_element_type=jnp.float32)


def exact(left, right, dims=(((1,), (0,)), ((), ()))):
    return lax.dot_general(
        left, right, dims, precision=highest, preferred_element_type=jnp.float32
    )


def shifted(gram):
    row = lax.broadcasted_iota(jnp.int32, gram.shape, 0)
    col = lax.broadcasted_iota(jnp.int32, gram.shape, 1)
    return gram + jnp.where(row == col, SHIFT, 0.0)


def lead_kernel(pivot_a, pivot_b, inverse):
    a, b = pivot_a[...], pivot_b[...]
    inverse[...] = factor_inverse(shifted(product_nt(a, a) * product_nt(b, b)))


def rest_kernel(pivot_a, pivot_b, lead_inverse, inverse):
    half = lead_inverse.shape[0]
    lead = lead_inverse[...]
    gram = product_nt(pivot_a[pl.ds(half, half), :], pivot_a[...]) * product_nt(
        pivot_b[pl.ds(half, half), :], pivot_b[...]
    )
    coupling = exact(gram[:, :half], lead, NT)
    rest = factor_inverse(shifted(gram[:, half:]) - exact(coupling, coupling, NT))
    inverse[pl.ds(0, half), :] = jnp.concatenate([lead, jnp.zeros_like(lead)], axis=1)
    lower_left = -exact(rest, exact(coupling, lead))
    inverse[pl.ds(half, half), :] = jnp.concatenate([lower_left, rest], axis=1)


def factor_call(kernel, name, size, micros, *operands):
    vmem = pl.BlockSpec(memory_space=pltpu.VMEM)
    return pl.pallas_call(
        kernel,
        in_specs=[vmem] * len(operands),
        out_specs=vmem,
        out_shape=jax.ShapeDtypeStruct((size, size), jnp.float32),
        compiler_params=pltpu.CompilerParams(vmem_limit_bytes=32 * MIB),
        cost_estimate=cost(micros, 8 * size * size),
        name=name,
    )(*operands)


def on_device(phi, psi, points):
    col_count = lax.axis_size("col")
    row_count = lax.axis_size("row")
    col_index = lax.axis_index("col")
    row_index = lax.axis_index("row")
    axes = ("row", "col")
    devices = row_count * col_count
    me = row_index * col_count + col_index
    plane_count, line_count, depth, orbitals = phi.shape
    grid_x, grid_y = plane_count * col_count, line_count * row_count
    cells = plane_count * line_count
    flat_phi = phi.reshape(cells * depth, orbitals)
    flat_psi = psi.reshape(cells * depth, orbitals)
    owned = points.shape[0]
    half = PB // 2

    global_x = points // (grid_y * depth)
    global_y = points // depth % grid_y
    local_cell = (
        (global_x - col_index * plane_count) * line_count + global_y - row_index * line_count
    ) * depth + points % depth

    own = jnp.stack(
        [
            jnp.take(flat_phi, local_cell, axis=0, mode="clip"),
            jnp.take(flat_psi, local_cell, axis=0, mode="clip"),
        ]
    )
    exchange = lambda a: lax.all_to_all(a, axes, split_axis=0, concat_axis=0, tiled=True)

    held = min(owned, PB)
    piece_rows = 2 * PB // devices
    offered = jnp.concatenate([own[:, :held]] * (PB // held), axis=1)
    own, offered = lax.optimization_barrier((own, offered))
    offered = exchange(offered.reshape(devices, piece_rows, orbitals))
    owner = me * piece_rows % PB // owned
    piece = lax.dynamic_index_in_dim(offered, owner, axis=0, keepdims=True)
    pivot = exchange(jnp.broadcast_to(piece, offered.shape)).reshape(2, PB, orbitals)

    row_samples = lax.all_gather(own, "col", axis=1, tiled=True)

    lead_inverse = factor_call(lead_kernel, "lead", half, 10, pivot[0, :half], pivot[1, :half])
    inverse = factor_call(rest_kernel, "rest", PB, 14, pivot[0], pivot[1], lead_inverse)

    x_table, y_table, z_table = (jnp.asarray(cas_table(n)) for n in (grid_x, grid_y, depth))
    padded = (cells // 16 + 1) * 16
    halves = PB // LANES
    rounds = -(-depth * halves // devices)
    parts = []
    for h in range(halves):
        edges = [h * depth, (h + 1) * depth]
        cuts = [k * devices for k in range(rounds) if edges[0] < k * devices < edges[1]]
        marks = [edges[0], *cuts, edges[1]]
        parts.append([(a // devices, a % devices, b - a) for a, b in zip(marks, marks[1:])])

    outgoing = [[] for _ in range(rounds)]

    def make(h, chosen, rows):
        used = rows.shape[1]
        first = chosen[0][0] * devices + chosen[0][1] - h * depth
        count = sum(n for _, _, n in chosen)
        made = source(
            flat_phi,
            flat_psi,
            pivot[0, :used],
            pivot[1, :used],
            rows,
            h,
            z_table[first : first + count],
            cells,
            depth,
            padded,
            [n for _, _, n in chosen],
        )
        for (k, _, _), part in zip(chosen, made):
            outgoing[k].append(part)

    def after(value, gate):
        return lax.optimization_barrier((value, gate))[0]

    make(0, parts[0][:1], lead_inverse)
    if parts[0][1:]:
        make(0, parts[0][1:], after(lead_inverse, outgoing[0][0]))
    row_start = row_index * row_samples.shape[1]
    col_start = col_index * row_count * owned
    scalar = lambda *v: jnp.stack([jnp.asarray(a, jnp.int32) for a in v])

    latest = previous = outgoing[0][0]
    members = row_count // col_count
    bits = [1 << b for b in range(row_count.bit_length() - 1)]
    inner = [b for b in bits if b < members]
    outer = [b for b in bits if b >= members]
    columns = [
        jnp.where(row_index // members == col_index, row_samples[i], 0) for i in range(2)
    ]
    steps = []
    for t in range(len(outer)):
        pairs = []
        for c in range(col_count):
            for j in range(members):
                order = outer[j % len(outer) :] + outer[: j % len(outer)]
                holders = [members * c + j]
                for b in order[:t]:
                    holders += [r ^ b for r in holders]
                pairs += [
                    (r * col_count + c, (r ^ order[t]) * col_count + c) for r in holders
                ]


        def spread(block, pairs=pairs):
            other = lax.ppermute(block, axes, pairs)
            return other, block + other

        steps += [((0, 1), spread)] if t == 0 else [((0,), spread), ((1,), spread)]

    def double(block, distance):
        pairs = [(r, r ^ distance) for r in range(row_count)]
        other = lax.ppermute(block, "row", pairs)
        upper = row_index // distance % 2 == 1
        return other, jnp.concatenate(
            [jnp.where(upper, other, block), jnp.where(upper, block, other)], axis=0
        )

    steps += [((0, 1), lambda block, distance=d: double(block, distance)) for d in inner]

    arrived = []

    coming = []

    def step_on(*gate):
        which, move = steps.pop(0)
        for i in which:
            block = after(columns[i], gate) if gate else columns[i]
            other, columns[i] = move(block)
            coming.append(other)

    def in_turn(block, *ready):
        nonlocal latest, previous
        previous = latest
        block = lax.optimization_barrier((block, previous, *coming, *ready))[0]
        coming.clear()
        if steps and arrived:
            step_on(previous)
        latest = exchange(block)
        return latest

    second_round = parts[1][0][0]
    panel_round = max(min(3, rounds - 1), second_round, 1)
    ready = []
    returned = []
    for k in range(rounds + 1):
        updated = []
        if k == second_round:
            gated = after(inverse, latest if k < 2 else arrived[k - 1])
            make(1, parts[1], gated)
        if k < rounds:
            pieces = list(outgoing[k])
            spare = devices - sum(p.shape[0] for p in pieces)
            if spare:
                pieces.append(jnp.zeros((spare, padded, LANES), jnp.int16))
            sent = pieces[0] if len(pieces) == 1 else jnp.concatenate(pieces, axis=0)
            arrived.append(in_turn(sent, *ready))
            ready = []
        if k == 0:
            updated += [inverse, row_samples]
        if k == panel_round - 1:
            panel, row_high, row_low = panel_rows(
                scalar(row_start), row_samples, pivot, after(inverse, latest)
            )
            updated += [row_high]
        if k == panel_round:
            while steps:
                step_on()
            _, col_high, col_low = panel_rows(
                scalar(col_start), columns, pivot, after(inverse, previous)
            )
            ready += [col_high]
            schur = schur_block(
                after(scalar(row_start, col_start), latest),
                (row_samples[0], row_samples[1], row_high, row_low),
                (columns[0], columns[1], col_high, col_low),
            )
            updated += [schur]
        if k > 0:
            z_index = ((k - 1) * devices + me) % depth
            z_freq = jnp.minimum(z_index, depth - z_index).astype(jnp.int32).reshape(1)
            back = middle(
                z_freq, arrived[k - 1], x_table, y_table, grid_x, grid_y, line_count
            )
            returned.append(in_turn(back, *ready))
        ready = updated

    potential = None
    for h in range(halves):
        potential = target(
            [returned[k] for k, _, _ in parts[h]],
            [(a, n) for _, a, n in parts[h]],
            z_table,
            potential,
            h,
            cells,
            depth,
            PB,
        )
    potential = potential.reshape(plane_count, line_count, depth, PB)
    return (schur, panel, potential)


def solution(mesh):
    in_specs = (P("col", "row", None, None), P("col", "row", None, None), P(("row", "col")))
    out_specs = (P("row", "col"), P("row", None), P("col", "row", None, None))
    return jax.shard_map(
        on_device, mesh=mesh, in_specs=in_specs, out_specs=out_specs, check_vma=False
    )
```

```python
import math

import jax
import jax.numpy as jnp
import ml_dtypes
import numpy as np
from jax import lax
from jax.experimental import pallas as pl
from jax.experimental.pallas import tpu as pltpu
from jax.sharding import PartitionSpec as P


PB = 256
GROUP = 40
LANES = 128
SHIFT = 4.0
BOX = 2.0
LEVELS = 32767.0
STEPS_PER_OCTAVE = 256.0
MIB = 1 << 20
NT = (((1,), (1,)), ((), ()))
highest = lax.Precision.HIGHEST


def cost(micros, moved):
    return pl.CostEstimate(
        flops=int(micros * 1.15e9), bytes_accessed=int(moved), transcendentals=0
    )


def cas_table(length):
    index = np.arange(length)
    angle = (index[:, None] * index[None, :] % length) * (2.0 * math.pi / length)
    table = ((np.cos(angle) + np.sin(angle)) / math.sqrt(length)).astype(np.float32)
    high = table.astype(ml_dtypes.bfloat16)
    low = (table - high.astype(np.float32)).astype(ml_dtypes.bfloat16)
    return np.concatenate([high, high, low], axis=1)


def split(value):
    high = value.astype(jnp.bfloat16)
    return high, (value - high.astype(jnp.float32)).astype(jnp.bfloat16)


def stacked(value):
    high, low = split(value)
    return jnp.concatenate([high, low, high], axis=0)


def transform(table, columns):
    data = jnp.concatenate([stacked(c) for c in columns], axis=1)
    out = jnp.dot(table, data, preferred_element_type=jnp.float32)
    return [out[:, i * LANES : (i + 1) * LANES] for i in range(len(columns))]


def encode(rows, padded):
    count = rows.shape[0]
    peak = jnp.maximum(jnp.max(jnp.abs(rows), axis=0, keepdims=True), 1e-30)
    octave = jnp.ceil(jnp.log2(peak) * STEPS_PER_OCTAVE)
    scale = jnp.exp2(octave * (-1.0 / STEPS_PER_OCTAVE)) * LEVELS
    code = jnp.clip(jnp.round(rows * scale), -LEVELS, LEVELS)
    tail = jnp.broadcast_to(octave, (padded - count, LANES))
    return jnp.concatenate([code, tail], axis=0).astype(jnp.int32).astype(jnp.int16)


def decode(block, count):
    value = block.astype(jnp.int32).astype(jnp.float32)
    scale = jnp.exp2(value[count : count + 1] * (1.0 / STEPS_PER_OCTAVE)) * (1.0 / LEVELS)
    return value[:count] * scale


def source_kernel(group, cells, depth, padded, pieces, *refs):
    phi, psi, pivot_a, pivot_b, inverse, table = refs[:6]
    outs, grid_rows = refs[6:-1], refs[-1]
    step = pl.program_id(0)
    first = lax.dot_general(phi[...], pivot_a[...], NT, preferred_element_type=jnp.float32)
    second = lax.dot_general(psi[...], pivot_b[...], NT, preferred_element_type=jnp.float32)
    pair_high, pair_low = split(first * second)
    inv_high, inv_low = split(inverse[...])
    fitting = product_nt(
        jnp.concatenate([pair_high, pair_low, pair_high], axis=1),
        jnp.concatenate([inv_high, inv_high, inv_low], axis=1),
    )
    columns = [fitting[g * depth : (g + 1) * depth] for g in range(group)]
    for g, out in enumerate(transform(table[...], columns)):
        grid_rows[pl.ds(step * group + g, out.shape[0], stride=cells), :] = out

    @pl.when(step == pl.num_programs(0) - 1)
    def _():
        base = 0
        for out_ref, count in zip(outs, pieces):

            def one(i, carry, base=base, out_ref=out_ref):
                start = pl.multiple_of((base + i) * cells, math.gcd(cells, 8))
                out_ref[i] = encode(grid_rows[pl.ds(start, cells), :], padded)
                return carry

            lax.fori_loop(0, count, one, 0)
            base += count


def source(phi, psi, pivot_a, pivot_b, inverse, half, table, cells, depth, padded, pieces):
    group = max(g for g in range(1, GROUP + 1) if cells % g == 0)
    orbitals = phi.shape[1]
    pivots = pivot_a.shape[0]
    whole = lambda shape: pl.BlockSpec(shape, lambda i: (0,) * len(shape))
    return pl.pallas_call(
        lambda *refs: source_kernel(group, cells, depth, padded, pieces, *refs),
        grid=(cells // group,),
        in_specs=[
            pl.BlockSpec((group * depth, orbitals), lambda i: (i, 0)),
            pl.BlockSpec((group * depth, orbitals), lambda i: (i, 0)),
            whole(pivot_a.shape),
            whole(pivot_b.shape),
            pl.BlockSpec((LANES, pivots), lambda i: (half, 0)),
            whole(table.shape),
        ],
        out_specs=[whole((n, padded, LANES)) for n in pieces],
        out_shape=[jax.ShapeDtypeStruct((n, padded, LANES), jnp.int16) for n in pieces],
        scratch_shapes=[pltpu.VMEM((table.shape[0] * cells, LANES), jnp.float32)],
        compiler_params=pltpu.CompilerParams(vmem_limit_bytes=50 * MIB),
        cost_estimate=cost(
            cells * depth / 600, 4 * cells * depth * orbitals
        ),
        name="source",
    )(phi, psi, pivot_a, pivot_b, inverse, table)


def middle_kernel(sizes, padded, z_freq, piece, x_table, y_table, out_ref, arrived, spectrum):
    grid_x, grid_y, lines, blocks = sizes
    cells = grid_x * grid_y // blocks
    batch = 4

    def load(i, carry):
        start = pl.multiple_of(i * cells, math.gcd(cells, 8))
        arrived[pl.ds(start, cells), :] = decode(piece[i], cells)
        return carry

    lax.fori_loop(0, blocks, load, 0)

    def line_start(y):
        return y // lines * (grid_x * lines) + y % lines

    def x_forward(i, carry):
        ys = [i * batch + b for b in range(batch)]
        columns = [arrived[pl.ds(line_start(y), grid_x, stride=lines), :] for y in ys]
        for y, out in zip(ys, transform(x_table[...], columns)):
            spectrum[pl.ds(y, grid_x, stride=grid_y), :] = out
        return carry

    lax.fori_loop(0, grid_y // batch, x_forward, 0)

    y_index = lax.broadcasted_iota(jnp.int32, (grid_y, LANES), 0)
    y_freq = jnp.minimum(y_index, grid_y - y_index).astype(jnp.float32)
    z_squared = (z_freq[0] * z_freq[0]).astype(jnp.float32)
    yz_squared = y_freq * y_freq + z_squared

    def y_both(i, carry):
        xs = [i * batch + b for b in range(batch)]
        columns = [spectrum[pl.ds(pl.multiple_of(x * grid_y, 8), grid_y), :] for x in xs]
        scaled = []
        for x, out in zip(xs, transform(y_table[...], columns)):
            x_freq = jnp.minimum(x, grid_x - x)
            squared = yz_squared + (x_freq * x_freq).astype(jnp.float32)
            kernel = BOX * BOX / math.pi / jnp.maximum(squared, 1.0)
            scaled.append(jnp.where(squared > 0.5, kernel, 0.0) * out)
        for x, out in zip(xs, transform(y_table[...], scaled)):
            spectrum[pl.ds(pl.multiple_of(x * grid_y, 8), grid_y), :] = out
        return carry

    lax.fori_loop(0, grid_x // batch, y_both, 0)

    def x_back(i, carry):
        ys = [i * batch + b for b in range(batch)]
        columns = [spectrum[pl.ds(y, grid_x, stride=grid_y), :] for y in ys]
        for y, out in zip(ys, transform(x_table[...], columns)):
            arrived[pl.ds(line_start(y), grid_x, stride=lines), :] = out
        return carry

    lax.fori_loop(0, grid_y // batch, x_back, 0)

    def store(i, carry):
        start = pl.multiple_of(i * cells, math.gcd(cells, 8))
        out_ref[i] = encode(arrived[pl.ds(start, cells), :], padded)
        return carry

    lax.fori_loop(0, blocks, store, 0)


def middle(z_freq, piece, x_table, y_table, grid_x, grid_y, lines):
    blocks, padded, _ = piece.shape
    sizes = (grid_x, grid_y, lines, blocks)
    vmem = pl.BlockSpec(memory_space=pltpu.VMEM)
    points = grid_x * grid_y
    return pl.pallas_call(
        lambda *refs: middle_kernel(sizes, padded, *refs),
        in_specs=[pl.BlockSpec(memory_space=pltpu.SMEM), vmem, vmem, vmem],
        out_specs=vmem,
        out_shape=jax.ShapeDtypeStruct(piece.shape, jnp.int16),
        scratch_shapes=[
            pltpu.VMEM((points, LANES), jnp.float32),
            pltpu.VMEM((points, LANES), jnp.float32),
        ],
        compiler_params=pltpu.CompilerParams(vmem_limit_bytes=32 * MIB),
        cost_estimate=cost(points / 400, 4 * blocks * padded * LANES),
        name="middle",
    )(z_freq, piece, x_table, y_table)


def target_kernel(group, cells, depth, spans, *refs):
    count = len(spans)
    arrived, table = refs[:count], refs[count]
    out_ref, grid_rows = refs[-2:]
    step = pl.program_id(0)

    @pl.when(step == 0)
    def _():
        base = 0
        for piece, (start, number) in zip(arrived, spans):

            def one(i, carry, base=base, start=start, piece=piece):
                row = pl.multiple_of((base + i) * cells, math.gcd(cells, 8))
                grid_rows[pl.ds(row, cells), :] = decode(piece[start + i], cells)
                return carry

            lax.fori_loop(0, number, one, 0)
            base += number

    columns = [
        grid_rows[pl.ds(step * group + g, depth, stride=cells), :] for g in range(group)
    ]
    for g, out in enumerate(transform(table[...], columns)):
        out_ref[pl.ds(g * depth, depth), :] = out


def target(pieces, spans, table, before, half, cells, depth, functions):
    group = max(g for g in range(1, GROUP + 1) if cells % g == 0)
    whole = lambda shape: pl.BlockSpec(shape, lambda i: (0,) * len(shape))
    in_specs = [whole(p.shape) for p in pieces] + [whole(table.shape)]
    operands = [*pieces, table]
    aliases = {}
    if before is not None:
        in_specs.append(pl.BlockSpec(memory_space=pl.ANY))
        aliases = {len(operands): 0}
        operands.append(before)
    return pl.pallas_call(
        lambda *refs: target_kernel(group, cells, depth, spans, *refs),
        grid=(cells // group,),
        in_specs=in_specs,
        out_specs=pl.BlockSpec((group * depth, LANES), lambda i: (i, half)),
        out_shape=jax.ShapeDtypeStruct((cells * depth, functions), jnp.float32),
        scratch_shapes=[pltpu.VMEM((depth * cells, LANES), jnp.float32)],
        input_output_aliases=aliases,
        compiler_params=pltpu.CompilerParams(vmem_limit_bytes=50 * MIB),
        cost_estimate=cost(cells * depth / 1200, 6 * cells * depth * LANES),
        name="target",
    )(*operands)


def panel_kernel(first_row, left_a, left_b, pivot_a, pivot_b, inverse, panel, high_ref, low_ref):
    step = pl.program_id(0)
    rows, pivots = panel.shape
    gram = lax.dot_general(left_a[...], pivot_a[...], NT, preferred_element_type=jnp.float32)
    gram *= lax.dot_general(left_b[...], pivot_b[...], NT, preferred_element_type=jnp.float32)
    row = lax.broadcasted_iota(jnp.int32, (rows, pivots), 0) + first_row[0] + step * rows
    gram += jnp.where(row == lax.broadcasted_iota(jnp.int32, (rows, pivots), 1), SHIFT, 0.0)
    value = lax.dot_general(
        gram, inverse[...], NT, precision=highest, preferred_element_type=jnp.float32
    )
    panel[...] = value
    high_ref[...], low_ref[...] = split(value)


def panel_rows(first_row, left, pivot, inverse):
    rows, orbitals = left[0].shape
    pivots = pivot.shape[1]
    tile = math.gcd(rows, 512)
    whole = lambda shape: pl.BlockSpec(shape, lambda i: (0,) * len(shape))
    block = lambda width: pl.BlockSpec((tile, width), lambda i: (i, 0))
    shape = lambda dtype: jax.ShapeDtypeStruct((rows, pivots), dtype)
    return pl.pallas_call(
        panel_kernel,
        grid=(rows // tile,),
        in_specs=[
            pl.BlockSpec(memory_space=pltpu.SMEM),
            block(orbitals),
            block(orbitals),
            whole((pivots, orbitals)),
            whole((pivots, orbitals)),
            whole((pivots, pivots)),
        ],
        out_specs=[block(pivots)] * 3,
        out_shape=[shape(jnp.float32), shape(jnp.bfloat16), shape(jnp.bfloat16)],
        compiler_params=pltpu.CompilerParams(vmem_limit_bytes=32 * MIB),
        cost_estimate=cost(rows / 400, 4 * rows * orbitals + 8 * rows * pivots),
        name="panel",
    )(first_row, left[0], left[1], pivot[0], pivot[1], inverse)


def schur_kernel(
    offsets, row_a, row_b, row_high, row_low, col_a, col_b, col_high, col_low, out_ref
):
    rows, cols = out_ref.shape
    product = lambda left, right: lax.dot_general(
        left[...], right[...], NT, preferred_element_type=jnp.float32
    )
    gram = product(row_a, col_a) * product(row_b, col_b)
    update = product(row_high, col_high) + (
        product(row_high, col_low) + product(row_low, col_high)
    )
    row_start = offsets[0] + pl.program_id(0) * rows
    col_start = offsets[1] + pl.program_id(1) * cols
    out_ref[...] = gram - update
    overlap = jnp.logical_and(row_start < col_start + cols, col_start < row_start + rows)

    @pl.when(overlap)
    def _():
        row = lax.broadcasted_iota(jnp.int32, (rows, cols), 0) + row_start
        col = lax.broadcasted_iota(jnp.int32, (rows, cols), 1) + col_start
        out_ref[...] += jnp.where(row == col, SHIFT, 0.0)


def schur_block(offsets, row_side, col_side):
    rows, orbitals = row_side[0].shape
    cols = col_side[0].shape[0]
    row_tile, col_tile = math.gcd(rows, 512), math.gcd(cols, 1024)
    row_block = lambda a: pl.BlockSpec((row_tile, a.shape[1]), lambda i, j: (i, 0))
    col_block = lambda a: pl.BlockSpec((col_tile, a.shape[1]), lambda i, j: (j, 0))
    return pl.pallas_call(
        schur_kernel,
        grid=(rows // row_tile, cols // col_tile),
        in_specs=[
            pl.BlockSpec(memory_space=pltpu.SMEM),
            *[row_block(a) for a in row_side],
            *[col_block(a) for a in col_side],
        ],
        out_specs=pl.BlockSpec((row_tile, col_tile), lambda i, j: (i, j)),
        out_shape=jax.ShapeDtypeStruct((rows, cols), jnp.float32),
        compiler_params=pltpu.CompilerParams(vmem_limit_bytes=50 * MIB),
        cost_estimate=cost(rows * cols / 240000, 4 * rows * cols),
        name="schur",
    )(offsets, *row_side, *col_side)


def factor_inverse(matrix):
    size = matrix.shape[0]
    strip_rows = 16
    row = lax.broadcasted_iota(jnp.int32, (size, size), 0)
    col = lax.broadcasted_iota(jnp.int32, (size, size), 1)
    work = jnp.concatenate([matrix, jnp.where(row == col, 1.0, 0.0)], axis=1)
    strip_row = lax.broadcasted_iota(jnp.int32, (strip_rows, size), 0)
    inverse = []
    for start in range(0, size, strip_rows):
        strip = work[start : start + strip_rows]
        cols = [
            jnp.broadcast_to(strip[:, start + t : start + t + 1], (strip_rows, size))
            for t in range(strip_rows)
        ]
        diagonal = jnp.ones((strip_rows, size), jnp.float32)
        for t in range(strip_rows):
            factor = jnp.where(strip_row > t, cols[t] * (1.0 / cols[t][t : t + 1]), 0.0)
            diagonal = jnp.where(strip_row == t, cols[t], diagonal)
            for u in range(t + 1, strip_rows):
                cols[u] = cols[u] - factor * cols[u][t : t + 1]
            strip = strip - jnp.concatenate([factor, factor], axis=1) * strip[t : t + 1]
        root = lax.rsqrt(diagonal)
        root = root * (1.5 - 0.5 * diagonal * root * root)
        strip = strip * jnp.concatenate([root, root], axis=1)
        inverse.append(strip[:, size:])
        if start + strip_rows < size:
            work = work - lax.dot_general(
                strip[:, :size],
                strip,
                (((0,), (0,)), ((), ())),
                precision=highest,
                preferred_element_type=jnp.float32,
            )
    return jnp.concatenate(inverse, axis=0)


def product_nt(left, right):
    return lax.dot_general(left, right, NT, preferred_element_type=jnp.float32)


def exact(left, right, dims=(((1,), (0,)), ((), ()))):
    return lax.dot_general(
        left, right, dims, precision=highest, preferred_element_type=jnp.float32
    )


def shifted(gram):
    row = lax.broadcasted_iota(jnp.int32, gram.shape, 0)
    col = lax.broadcasted_iota(jnp.int32, gram.shape, 1)
    return gram + jnp.where(row == col, SHIFT, 0.0)


def lead_kernel(pivot_a, pivot_b, inverse):
    a, b = pivot_a[...], pivot_b[...]
    inverse[...] = factor_inverse(shifted(product_nt(a, a) * product_nt(b, b)))


def rest_kernel(pivot_a, pivot_b, lead_inverse, inverse):
    half = lead_inverse.shape[0]
    lead = lead_inverse[...]
    gram = product_nt(pivot_a[pl.ds(half, half), :], pivot_a[...]) * product_nt(
        pivot_b[pl.ds(half, half), :], pivot_b[...]
    )
    coupling = exact(gram[:, :half], lead, NT)
    rest = factor_inverse(shifted(gram[:, half:]) - exact(coupling, coupling, NT))
    inverse[pl.ds(0, half), :] = jnp.concatenate([lead, jnp.zeros_like(lead)], axis=1)
    lower_left = -exact(rest, exact(coupling, lead))
    inverse[pl.ds(half, half), :] = jnp.concatenate([lower_left, rest], axis=1)


def factor_call(kernel, name, size, micros, *operands):
    vmem = pl.BlockSpec(memory_space=pltpu.VMEM)
    return pl.pallas_call(
        kernel,
        in_specs=[vmem] * len(operands),
        out_specs=vmem,
        out_shape=jax.ShapeDtypeStruct((size, size), jnp.float32),
        compiler_params=pltpu.CompilerParams(vmem_limit_bytes=32 * MIB),
        cost_estimate=cost(micros, 8 * size * size),
        name=name,
    )(*operands)


def on_device(phi, psi, points):
    col_count = lax.axis_size("col")
    row_count = lax.axis_size("row")
    col_index = lax.axis_index("col")
    row_index = lax.axis_index("row")
    axes = ("row", "col")
    devices = row_count * col_count
    me = row_index * col_count + col_index
    plane_count, line_count, depth, orbitals = phi.shape
    grid_x, grid_y = plane_count * col_count, line_count * row_count
    cells = plane_count * line_count
    flat_phi = phi.reshape(cells * depth, orbitals)
    flat_psi = psi.reshape(cells * depth, orbitals)
    owned = points.shape[0]
    half = PB // 2

    global_x = points // (grid_y * depth)
    global_y = points // depth % grid_y
    local_cell = (
        (global_x - col_index * plane_count) * line_count + global_y - row_index * line_count
    ) * depth + points % depth

    own = jnp.stack(
        [
            jnp.take(flat_phi, local_cell, axis=0, mode="clip"),
            jnp.take(flat_psi, local_cell, axis=0, mode="clip"),
        ]
    )
    exchange = lambda a: lax.all_to_all(a, axes, split_axis=0, concat_axis=0, tiled=True)

    held = min(owned, PB)
    piece_rows = 2 * PB // devices
    offered = jnp.concatenate([own[:, :held]] * (PB // held), axis=1)
    own, offered = lax.optimization_barrier((own, offered))
    offered = exchange(offered.reshape(devices, piece_rows, orbitals))
    rising, falling = [own], [own]

    def pass_on(t):
        up = [(c, c + 1) for c in range(t, col_count - 1)]
        down = [(c, c - 1) for c in range(1, col_count - t)]
        rising.append(lax.ppermute(rising[-1], "col", up))
        falling.append(lax.ppermute(falling[-1], "col", down))
        return rising[-1], falling[-1]

    def ordered(value, gate):
        return lax.optimization_barrier((value, gate))[0]

    passed = pass_on(0)
    owner = me * piece_rows % PB // owned
    piece = lax.dynamic_index_in_dim(offered, owner, axis=0, keepdims=True)
    pieces = ordered(jnp.broadcast_to(piece, offered.shape), passed)
    pivot = exchange(pieces).reshape(2, PB, orbitals)
    for t in range(1, col_count - 1):
        if t == 2:
            pivot = ordered(pivot, passed)
        passed = pass_on(t)
    blocks = []
    for b in range(col_count):
        block = own
        for t in range(1, col_count):
            if b + t < col_count:
                block = jnp.where(col_index == b + t, rising[t], block)
            if b - t >= 0:
                block = jnp.where(col_index == b - t, falling[t], block)
        blocks.append(block)
    row_samples = jnp.concatenate(blocks, axis=1)

    lead_inverse = factor_call(lead_kernel, "lead", half, 10, pivot[0, :half], pivot[1, :half])
    inverse = factor_call(rest_kernel, "rest", PB, 14, pivot[0], pivot[1], lead_inverse)

    x_table, y_table, z_table = (jnp.asarray(cas_table(n)) for n in (grid_x, grid_y, depth))
    padded = (cells // 16 + 1) * 16
    halves = PB // LANES
    rounds = -(-depth * halves // devices)
    parts = []
    for h in range(halves):
        edges = [h * depth, (h + 1) * depth]
        cuts = [k * devices for k in range(rounds) if edges[0] < k * devices < edges[1]]
        marks = [edges[0], *cuts, edges[1]]
        parts.append([(a // devices, a % devices, b - a) for a, b in zip(marks, marks[1:])])

    outgoing = [[] for _ in range(rounds)]

    def make(h, chosen, rows):
        used = rows.shape[1]
        first = chosen[0][0] * devices + chosen[0][1] - h * depth
        count = sum(n for _, _, n in chosen)
        made = source(
            flat_phi,
            flat_psi,
            pivot[0, :used],
            pivot[1, :used],
            rows,
            h,
            z_table[first : first + count],
            cells,
            depth,
            padded,
            [n for _, _, n in chosen],
        )
        for (k, _, _), part in zip(chosen, made):
            outgoing[k].append(part)

    def after(value, gate):
        return lax.optimization_barrier((value, gate))[0]

    make(0, parts[0][:1], lead_inverse)
    if parts[0][1:]:
        make(0, parts[0][1:], after(lead_inverse, (outgoing[0][0], passed)))
    row_start = row_index * row_samples.shape[1]
    col_start = col_index * row_count * owned
    scalar = lambda *v: jnp.stack([jnp.asarray(a, jnp.int32) for a in v])

    latest = previous = outgoing[0][0]
    members = row_count // col_count
    bits = [1 << b for b in range(row_count.bit_length() - 1)]
    inner = [b for b in bits if b < members]
    outer = [b for b in bits if b >= members]
    columns = [
        jnp.where(row_index // members == col_index, row_samples[i], 0) for i in range(2)
    ]
    steps = []
    for t in range(len(outer)):
        pairs = []
        for c in range(col_count):
            for j in range(members):
                order = outer[j % len(outer) :] + outer[: j % len(outer)]
                holders = [members * c + j]
                for b in order[:t]:
                    holders += [r ^ b for r in holders]
                pairs += [
                    (r * col_count + c, (r ^ order[t]) * col_count + c) for r in holders
                ]


        def spread(block, pairs=pairs):
            other = lax.ppermute(block, axes, pairs)
            return other, block + other

        steps += [((0, 1), spread)] if t == 0 else [((0,), spread), ((1,), spread)]

    def double(block, distance):
        pairs = [(r, r ^ distance) for r in range(row_count)]
        other = lax.ppermute(block, "row", pairs)
        upper = row_index // distance % 2 == 1
        return other, jnp.concatenate(
            [jnp.where(upper, other, block), jnp.where(upper, block, other)], axis=0
        )

    steps += [((0, 1), lambda block, distance=d: double(block, distance)) for d in inner]

    arrived = []

    coming = []

    def step_on(*gate):
        which, move = steps.pop(0)
        for i in which:
            block = after(columns[i], gate) if gate else columns[i]
            other, columns[i] = move(block)
            coming.append(other)

    def in_turn(block, *ready):
        nonlocal latest, previous
        previous = latest
        block = lax.optimization_barrier((block, previous, *coming, *ready))[0]
        coming.clear()
        if steps and arrived:
            step_on(previous)
        latest = exchange(block)
        return latest

    second_round = parts[1][0][0]
    panel_round = max(min(3, rounds - 1), second_round, 1)
    ready = []
    returned = []
    for k in range(rounds + 1):
        updated = []
        if k == second_round:
            gated = after(inverse, latest if k < 2 else arrived[k - 1])
            make(1, parts[1], gated)
        if k < rounds:
            pieces = list(outgoing[k])
            spare = devices - sum(p.shape[0] for p in pieces)
            if spare:
                pieces.append(jnp.zeros((spare, padded, LANES), jnp.int16))
            sent = pieces[0] if len(pieces) == 1 else jnp.concatenate(pieces, axis=0)
            arrived.append(in_turn(sent, *ready))
            ready = []
        if k == 0:
            updated += [inverse, row_samples]
        if k == panel_round - 1:
            panel, row_high, row_low = panel_rows(
                scalar(row_start), row_samples, pivot, after(inverse, latest)
            )
            updated += [row_high]
        if k == panel_round:
            while steps:
                step_on()
            _, col_high, col_low = panel_rows(
                scalar(col_start), columns, pivot, after(inverse, previous)
            )
            ready += [col_high]
            schur = schur_block(
                after(scalar(row_start, col_start), latest),
                (row_samples[0], row_samples[1], row_high, row_low),
                (columns[0], columns[1], col_high, col_low),
            )
            updated += [schur]
        if k > 0:
            z_index = ((k - 1) * devices + me) % depth
            z_freq = jnp.minimum(z_index, depth - z_index).astype(jnp.int32).reshape(1)
            back = middle(
                z_freq, arrived[k - 1], x_table, y_table, grid_x, grid_y, line_count
            )
            returned.append(in_turn(back, *ready))
        ready = updated

    potential = None
    for h in range(halves):
        potential = target(
            [returned[k] for k, _, _ in parts[h]],
            [(a, n) for _, a, n in parts[h]],
            z_table,
            potential,
            h,
            cells,
            depth,
            PB,
        )
    potential = potential.reshape(plane_count, line_count, depth, PB)
    return (schur, panel, potential)


def solution(mesh):
    in_specs = (P("col", "row", None, None), P("col", "row", None, None), P(("row", "col")))
    out_specs = (P("row", "col"), P("row", None), P("col", "row", None, None))
    return jax.shard_map(
        on_device, mesh=mesh, in_specs=in_specs, out_specs=out_specs, check_vma=False
    )
```
